256 devices in a mesh: hst: 64 (over y, z, core), head: 4 (over x).
Axes of the slice: x: 4, y: 4, z: 8, core: 2. Of those that a mesh axis runs over, the one named last changes fastest.
Arguments:
- queries: bfloat16 [32768, 4096], P('hst', 'head'), may hold values from -8 to 8
- keys: bfloat16 [32768, 1024], P('hst', 'head'), may hold values from -8 to 8
- values: bfloat16 [32768, 1024], P('hst', 'head'), may hold values from -6 to 6
- pass_rows: int32 [64, 64], P('hst'), may hold values from 0 to 511, as said below
- out_weight: bfloat16 [4096, 4096], P('head'), may hold values from -0.09375 to 0.09375
Outputs:
- layer_out: bfloat16 [32768, 4096], P(('hst', 'head'))
The draws below stay inside these ranges and needn't reach their ends.
Inputs may be any that keep to these rules, and one draw needn't show every extreme that they name: `pass_rows`: each block's 64 row numbers are distinct and ascending, and always include 0 and 511.
All inputs are finite; a program needn't handle non-finite values.
Results may differ from the reference program's by a relative error of at most 0.017.
Values may be sent and summed in bfloat16 or wider, within the bound.
No kernel may reach another device: no remote copies, remote signals or barrier semaphores. Data moves between devices by JAX's collectives and lax.ppermute only.
A program may use at most 128 MiB of HBM per device.

```python
import jax
import jax.numpy as jnp
from jax import lax

QUERY_HEADS = 32
KEY_VALUE_HEADS = 8
HEAD_SIZE = 128
D = 4096
BLOCK_TOKENS = 512
PASSING_ROWS = 64
ANCHOR_ROWS = 128
DOCUMENT_TOKENS = 32768
N_HEAD = 4


def draw_queries(key, part):
    key = jax.random.fold_in(key, 11)
    return jnp.clip(jax.random.normal(key, (DOCUMENT_TOKENS, QUERY_HEADS * HEAD_SIZE), jnp.float32), -6.0, 6.0).astype(jnp.bfloat16)


def draw_keys(key, part):
    key = jax.random.fold_in(key, 23)
    return jnp.clip(jax.random.normal(key, (DOCUMENT_TOKENS, KEY_VALUE_HEADS * HEAD_SIZE), jnp.float32), -6.0, 6.0).astype(jnp.bfloat16)


def draw_pass_rows(key, part):
    key = jax.random.fold_in(key, 5)
    owner_blocks = DOCUMENT_TOKENS // BLOCK_TOKENS
    host_keys = jax.random.split(key, owner_blocks)

    def pick_rows(host_key):
        shuffled = jax.random.permutation(host_key, BLOCK_TOKENS - 2)[:PASSING_ROWS - 2].astype(jnp.int32) + 1
        ends = jnp.array([0, BLOCK_TOKENS - 1], jnp.int32)
        return jnp.sort(jnp.concatenate([ends, shuffled]))
    return jax.vmap(pick_rows)(host_keys).astype(jnp.int32)


def steps_of(stream_key, dims, cuts, smallest, high):
    level = 1.0
    for dim, blocks in cuts:
        steps = jax.random.uniform(jax.random.fold_in(jax.random.fold_in(stream_key, 6), dim), (blocks,), jnp.float32, smallest / len(cuts), high / len(cuts))
        level = level * jnp.repeat(jnp.exp(steps), dims[dim] // blocks).reshape((-1,) + (1,) * (len(dims) - 1 - dim))
    return level


def noise(stream_key, shape, spread, bound, cuts=(), held_as=jnp.bfloat16):
    values = spread * jax.random.normal(stream_key, shape, jnp.float32)
    if cuts:
        values = values * steps_of(stream_key, shape, cuts, -0.22, 0.18)
    return jnp.clip(values, -bound, bound).astype(held_as)


def setup_inputs(seed: int = 0) -> dict:
    key_of = jax.random.split(jax.random.key(seed), 6)
    queries = draw_queries(jax.random.fold_in(key_of[5], 71), 0)
    keys = draw_keys(jax.random.fold_in(key_of[5], 71), 0)
    values = noise(key_of[2], (DOCUMENT_TOKENS, KEY_VALUE_HEADS * HEAD_SIZE), 1.0, 6.0, ((0, 64), (1, 4)))
    pass_rows = draw_pass_rows(jax.random.fold_in(key_of[5], 71), 0)
    out_weight = noise(key_of[4], (QUERY_HEADS * HEAD_SIZE, D), (QUERY_HEADS * HEAD_SIZE) ** -0.5, 0.09375, ((0, 4),))
    return dict(queries=queries, keys=keys, values=values, pass_rows=pass_rows, out_weight=out_weight)


def reference(queries, keys, values, pass_rows, out_weight):
    owner_blocks = DOCUMENT_TOKENS // BLOCK_TOKENS
    group_width = QUERY_HEADS // KEY_VALUE_HEADS
    scale = HEAD_SIZE ** -0.5
    block_offsets = (jnp.arange(owner_blocks, dtype=jnp.int32)[:, None] * BLOCK_TOKENS + pass_rows).reshape(-1).astype(jnp.int32)
    passing_keys = keys[block_offsets].reshape(owner_blocks * PASSING_ROWS, KEY_VALUE_HEADS, HEAD_SIZE).astype(jnp.float32)
    passing_values = values[block_offsets].reshape(owner_blocks * PASSING_ROWS, KEY_VALUE_HEADS, HEAD_SIZE).astype(jnp.float32)
    leading_keys = keys[:ANCHOR_ROWS].reshape(ANCHOR_ROWS, KEY_VALUE_HEADS, HEAD_SIZE).astype(jnp.float32)
    leading_values = values[:ANCHOR_ROWS].reshape(ANCHOR_ROWS, KEY_VALUE_HEADS, HEAD_SIZE).astype(jnp.float32)
    source = jnp.repeat(jnp.arange(owner_blocks, dtype=jnp.int32), PASSING_ROWS)
    line = jnp.arange(BLOCK_TOKENS, dtype=jnp.int32)

    def attend_block(host):
        initial_block = (host * BLOCK_TOKENS).astype(jnp.int32)
        query_head_rows = lax.dynamic_slice_in_dim(queries, initial_block, BLOCK_TOKENS, 0).reshape(BLOCK_TOKENS, KEY_VALUE_HEADS, group_width, HEAD_SIZE).astype(jnp.float32)
        local_keys = lax.dynamic_slice_in_dim(keys, initial_block, BLOCK_TOKENS, 0).reshape(BLOCK_TOKENS, KEY_VALUE_HEADS, HEAD_SIZE).astype(jnp.float32)
        local_values = lax.dynamic_slice_in_dim(values, initial_block, BLOCK_TOKENS, 0).reshape(BLOCK_TOKENS, KEY_VALUE_HEADS, HEAD_SIZE).astype(jnp.float32)
        all_keys = jnp.concatenate([leading_keys, passing_keys, local_keys], axis=0)
        all_values = jnp.concatenate([leading_values, passing_values, local_values], axis=0)
        visible = jnp.concatenate([
            jnp.broadcast_to(host > 0, (BLOCK_TOKENS, ANCHOR_ROWS)),
            jnp.broadcast_to(source[None, :] < host, (BLOCK_TOKENS, owner_blocks * PASSING_ROWS)),
            line[None, :] <= line[:, None]], axis=1)
        scores = jnp.einsum('rhgd,khd->hgrk', query_head_rows, all_keys) * scale
        scores = jnp.where(visible[None, None], scores, -1e30)
        highest = jnp.max(scores, axis=-1, keepdims=True)
        weights = jnp.where(visible[None, None], jnp.exp(scores - highest), 0.0)
        mass = jnp.sum(weights, axis=-1, keepdims=True)
        rounded = lax.optimization_barrier(weights.astype(jnp.bfloat16))
        weighted = jnp.einsum('hgrk,khd->hgrd', rounded.astype(jnp.float32), all_values)
        result = (weighted / mass).transpose(2, 0, 1, 3).reshape(BLOCK_TOKENS, QUERY_HEADS * HEAD_SIZE)
        return result.astype(jnp.bfloat16)

    attended = lax.map(attend_block, jnp.arange(owner_blocks, dtype=jnp.int32)).reshape(DOCUMENT_TOKENS, QUERY_HEADS * HEAD_SIZE)
    width = QUERY_HEADS * HEAD_SIZE // N_HEAD
    summed = jnp.zeros((DOCUMENT_TOKENS, D), jnp.float32)
    for part_index in range(N_HEAD):
        partial_out = jnp.dot(attended[:, part_index * width:(part_index + 1) * width],
                              out_weight[part_index * width:(part_index + 1) * width],
                              preferred_element_type=jnp.float32)
        rounded_part = lax.optimization_barrier(partial_out.astype(jnp.bfloat16))
        summed = summed + rounded_part.astype(jnp.float32)
    return summed.astype(jnp.bfloat16)
```

```python
import functools

import jax
import jax.numpy as jnp
import numpy as np
from jax import lax
from jax.experimental import pallas as pl
from jax.experimental.pallas import tpu as pltpu
from jax.sharding import PartitionSpec as P

HEAD_SIZE = 128
GROUP = 4
HEADS = 2
ANCHOR_ROWS = 128
BLOCK = 512
QUARTER = 128
ROWS = GROUP * QUARTER
SIDE = 2048
FACTOR = float(HEAD_SIZE**-0.5 * np.log2(np.e))
NEG = -1e30
LIMIT = float(2.0**110)
N_Y, N_Z, N_CORE, N_HEAD = 4, 8, 2, 4


def scores_of(q, k):
    return lax.dot_general(q, k, (((1,), (1,)), ((), ())), preferred_element_type=jnp.float32) * FACTOR


def with_ones(v, seen):
    return jnp.concatenate([jnp.where(seen, v, 0), jnp.where(seen, jnp.ones_like(v), 0)], 1)


def attend_kernel(info, q_ref, k_ref, v_ref, anchor_ref, side0, side1, out_ref, m_ref, acc_ref, buf0, buf1, sems):
    first_row = info[0] * QUARTER
    count0, count1, later = info[1], info[2], info[3]
    copy0 = pltpu.make_async_copy(side0, buf0, sems.at[0])
    copy1 = pltpu.make_async_copy(side1, buf1, sems.at[1])
    copy0.start()
    copy1.start()
    queries = [
        jnp.concatenate(
            [q_ref[:, (h * GROUP + g) * HEAD_SIZE : (h * GROUP + g + 1) * HEAD_SIZE] for g in range(GROUP)], 0
        )
        for h in range(HEADS)
    ]

    def near(h):
        k = jnp.concatenate(
            [k_ref[:, h * HEAD_SIZE : (h + 1) * HEAD_SIZE], anchor_ref[:, h * HEAD_SIZE : (h + 1) * HEAD_SIZE]], 0
        )
        columns = slice((HEADS + h) * HEAD_SIZE, (HEADS + h + 1) * HEAD_SIZE)
        v = jnp.concatenate([v_ref[:, h * HEAD_SIZE : (h + 1) * HEAD_SIZE], anchor_ref[:, columns]], 0)
        row = lax.broadcasted_iota(jnp.int32, (ROWS, BLOCK + ANCHOR_ROWS), 0) % QUARTER + first_row
        col = lax.broadcasted_iota(jnp.int32, (ROWS, BLOCK + ANCHOR_ROWS), 1)
        seen = (col <= row) | ((col >= BLOCK) & (later > 0))
        s = jnp.where(seen, scores_of(queries[h], k), NEG)
        return s, jnp.concatenate([v, jnp.ones_like(v)], 1)

    def far(h, buf, start, size, count):
        k = buf[pl.ds(start, size), h * HEAD_SIZE : (h + 1) * HEAD_SIZE]
        v = buf[pl.ds(start, size), (HEADS + h) * HEAD_SIZE : (HEADS + h + 1) * HEAD_SIZE]
        seen = lax.broadcasted_iota(jnp.int32, (size, HEAD_SIZE), 0) + start < count
        return scores_of(queries[h], k), with_ones(v, seen)

    for h in range(HEADS):
        s, v = near(h)
        m = jnp.max(s, axis=1, keepdims=True)
        acc_ref[h] = jnp.dot(jnp.exp2(s - m).astype(jnp.bfloat16), v, preferred_element_type=jnp.float32)
        m_ref[h] = jnp.broadcast_to(m, (ROWS, HEAD_SIZE))
    copy0.wait()
    copy1.wait()
    for buf, count in ((buf0, count0), (buf1, count1)):

        @pl.when(count > 0)
        def _(buf=buf, count=count):
            for h in range(HEADS):
                s, v = far(h, buf, 0, SIDE, count)
                p = jnp.exp2(s - m_ref[h][:, :1]).astype(jnp.bfloat16)
                acc_ref[h] += jnp.dot(p, v, preferred_element_type=jnp.float32)

    worst = jnp.float32(0)
    for h in range(HEADS):
        worst = jnp.maximum(worst, jnp.max(jnp.where(acc_ref[h][:, HEAD_SIZE:] < LIMIT, 0.0, 1.0)))

    @pl.when(worst > 0)
    def _():
        for h in range(HEADS):
            s, v = near(h)
            m = jnp.max(s, axis=1, keepdims=True)
            acc_ref[h] = jnp.dot(jnp.exp2(s - m).astype(jnp.bfloat16), v, preferred_element_type=jnp.float32)
            m_ref[h] = jnp.broadcast_to(m, (ROWS, HEAD_SIZE))
        size = 512
        for buf, count in ((buf0, count0), (buf1, count1)):

            def fold(i, carry, buf=buf, count=count):
                start = pl.multiple_of(i * size, size)
                for h in range(HEADS):
                    s, v = far(h, buf, start, size, count)
                    col = lax.broadcasted_iota(jnp.int32, (ROWS, size), 1) + start
                    s = jnp.where(col < count, s, NEG)
                    old = m_ref[h][:, :1]
                    m = jnp.maximum(old, jnp.max(s, axis=1, keepdims=True))
                    p = jnp.exp2(s - m).astype(jnp.bfloat16)
                    acc_ref[h] = acc_ref[h] * jnp.exp2(old - m) + jnp.dot(p, v, preferred_element_type=jnp.float32)
                    m_ref[h] = jnp.broadcast_to(m, (ROWS, HEAD_SIZE))
                return carry

            lax.fori_loop(0, (count + size - 1) // size, fold, 0)

    for h in range(HEADS):
        o = acc_ref[h][:, :HEAD_SIZE] / acc_ref[h][:, HEAD_SIZE:]
        for g in range(GROUP):
            columns = slice((h * GROUP + g) * HEAD_SIZE, (h * GROUP + g + 1) * HEAD_SIZE)
            out_ref[:, columns] = o[g * QUARTER : (g + 1) * QUARTER].astype(jnp.bfloat16)


def attend(info, queries, keys, values, anchor, side0, side1):
    width = HEADS * GROUP * HEAD_SIZE
    whole = lambda i, info: (0, 0)
    return pl.pallas_call(
        attend_kernel,
        out_shape=jax.ShapeDtypeStruct((QUARTER, width), jnp.bfloat16),
        grid_spec=pltpu.PrefetchScalarGridSpec(
            num_scalar_prefetch=1,
            grid=(1,),
            in_specs=[
                pl.BlockSpec((QUARTER, width), lambda i, info: (info[0], 0)),
                pl.BlockSpec((BLOCK, HEADS * HEAD_SIZE), whole),
                pl.BlockSpec((BLOCK, HEADS * HEAD_SIZE), whole),
                pl.BlockSpec((ANCHOR_ROWS, 2 * HEADS * HEAD_SIZE), whole),
                pl.BlockSpec(memory_space=pl.ANY),
                pl.BlockSpec(memory_space=pl.ANY),
            ],
            out_specs=pl.BlockSpec((QUARTER, width), whole),
            scratch_shapes=[
                pltpu.VMEM((HEADS, ROWS, HEAD_SIZE), jnp.float32),
                pltpu.VMEM((HEADS, ROWS, 2 * HEAD_SIZE), jnp.float32),
                pltpu.VMEM((SIDE, 2 * HEADS * HEAD_SIZE), jnp.bfloat16),
                pltpu.VMEM((SIDE, 2 * HEADS * HEAD_SIZE), jnp.bfloat16),
                pltpu.SemaphoreType.DMA((2,)),
            ],
        ),
        compiler_params=pltpu.CompilerParams(vmem_limit_bytes=50 << 20),
        name="attend",
    )(info, queries, keys, values, anchor, side0, side1)


def place(y, z, core):
    return ((y % N_Y) * N_Z + z % N_Z) * N_CORE + core


def send(x, pairs):
    return lax.ppermute(x, "hst", pairs)


def spread_anchor(own, host):
    a = jnp.where(host == 0, own, jnp.zeros_like(own))
    a = a + send(a, [(place(0, 0, 0), place(0, 3, 0))]) + send(a, [(place(0, 0, 0), place(0, 5, 0))])
    up = send(a, [(place(0, z, 0), place(0, z + 1, 0)) for z in (0, 3, 5)])
    down = send(a, [(place(0, z, 0), place(0, z - 1, 0)) for z in (0, 3)])
    a = a + up + down
    a = a + sum(send(a, [(place(0, z, 0), place(d, z, 0)) for z in range(N_Z)]) for d in (1, 2, 3))
    return a + send(a, [(place(y, z, 0), place(y, z, 1)) for y in range(N_Y) for z in range(N_Z)])


def on_device(queries, keys, values, pass_rows, out_weight):
    host = lax.axis_index("hst")
    me = lax.axis_index("head")
    pair = jnp.concatenate([keys, values], 1)
    one_hot = (pass_rows[0][:, None] == jnp.arange(BLOCK, dtype=jnp.int32)[None, :]).astype(jnp.bfloat16)
    picked = jnp.dot(one_hot, pair, preferred_element_type=jnp.float32).astype(jnp.bfloat16)
    anchor = spread_anchor(pair[:ANCHOR_ROWS], host)
    along_z = [[place(y, z, c) for z in range(N_Z)] for y in range(N_Y) for c in range(N_CORE)]
    along_y = [[place(y, z, c) for y in range(N_Y)] for z in range(N_Z) for c in range(N_CORE)]
    a2a = functools.partial(lax.all_to_all, axis_name="hst", split_axis=0, concat_axis=0, tiled=True)
    line = a2a(jnp.concatenate([picked] * N_Z, 0), axis_index_groups=along_z)
    side0 = a2a(jnp.concatenate([line] * N_Y, 0), axis_index_groups=along_y)
    side1 = send(side0, [(h, h ^ 1) for h in range(N_Y * N_Z * N_CORE)])
    share = pass_rows.shape[1]
    chip, core = host // N_CORE, host % N_CORE
    count0, count1 = chip * share, (chip + core) * share

    def part(d):
        info = jnp.stack([d, count0, count1, host]).astype(jnp.int32)
        att = attend(info, queries, keys, values, anchor, side0, side1)
        return jnp.dot(att, out_weight, preferred_element_type=jnp.float32)

    def shift(x, step):
        return lax.ppermute(x, "head", [(i, (i + step) % N_HEAD) for i in range(N_HEAD)])

    half = out_weight.shape[1] // 2
    far = part((me + 2) % N_HEAD).astype(jnp.bfloat16)
    low = shift(far[:, :half], 1)
    high = shift(far[:, half:], -1)
    right = part((me + 1) % N_HEAD)
    left = part((me + 3) % N_HEAD)
    right = jnp.concatenate([right[:, :half] + low, right[:, half:]], 1).astype(jnp.bfloat16)
    left = jnp.concatenate([left[:, :half], left[:, half:] + high], 1).astype(jnp.bfloat16)
    from_left = shift(right, 1)
    from_right = shift(left, -1)
    own = part(me)
    return (own + from_left + from_right).astype(jnp.bfloat16)


def solution(mesh):
    placed = (P("hst", "head"), P("hst", "head"), P("hst", "head"), P("hst", None), P("head", None))
    return jax.shard_map(
        on_device, mesh=mesh, in_specs=placed, out_specs=P(("hst", "head"), None), check_vma=False
    )
```

```python
import functools

import jax
import jax.numpy as jnp
import numpy as np
from jax import lax
from jax.experimental import pallas as pl
from jax.experimental.pallas import tpu as pltpu
from jax.sharding import PartitionSpec as P

HEAD_SIZE = 128
GROUP = 4
HEADS = 2
ANCHOR_ROWS = 128
BLOCK = 512
QUARTER = 128
STRIP = 64
ROWS = GROUP * QUARTER
N_Y, N_Z, N_CORE, N_HEAD = 4, 8, 2, 4
PASSING = 64
WIDTH = HEADS * HEAD_SIZE
SLICE = ANCHOR_ROWS // N_Z
LINE = N_Z * PASSING
SIDE = N_Y * LINE
PLANE = LINE + SLICE
D = 4096
FACTOR = float(HEAD_SIZE**-0.5 * np.log2(np.e))
NEG = -1e30
LIMIT = float(2.0**110)


def scores_of(q, k):
    return lax.dot_general(q, k, (((1,), (1,)), ((), ())), preferred_element_type=jnp.float32) * FACTOR


def with_ones(v, seen):
    return jnp.concatenate([jnp.where(seen, v, 0), jnp.where(seen, jnp.ones_like(v), 0)], 1)


def attend_kernel(
    info, qa_ref, qb_ref, k_ref, v_ref, anchor_ref, side0, side1, weight, out_ref,
    m_ref, acc_ref
):
    count0, count1, later = info[2], info[3], info[4]
    queries = [
        jnp.concatenate(
            [
                q[:, (h * GROUP + g) * HEAD_SIZE : (h * GROUP + g + 1) * HEAD_SIZE]
                for g in range(GROUP)
                for q in (qa_ref, qb_ref)
            ],
            0,
        )
        for h in range(HEADS)
    ]

    def near(h):
        k = jnp.concatenate(
            [k_ref[:, h * HEAD_SIZE : (h + 1) * HEAD_SIZE], anchor_ref[:, h * HEAD_SIZE : (h + 1) * HEAD_SIZE]], 0
        )
        columns = slice((HEADS + h) * HEAD_SIZE, (HEADS + h + 1) * HEAD_SIZE)
        v = jnp.concatenate([v_ref[:, h * HEAD_SIZE : (h + 1) * HEAD_SIZE], anchor_ref[:, columns]], 0)
        row = lax.broadcasted_iota(jnp.int32, (ROWS, BLOCK + ANCHOR_ROWS), 0) % QUARTER
        row = row + jnp.where(row < STRIP, info[0] * STRIP, info[1] * STRIP - STRIP)
        col = lax.broadcasted_iota(jnp.int32, (ROWS, BLOCK + ANCHOR_ROWS), 1)
        seen = (col <= row) | ((col >= BLOCK) & (later > 0))
        s = jnp.where(seen, scores_of(queries[h], k), NEG)
        return s, jnp.concatenate([v, jnp.ones_like(v)], 1)

    def far(h, side, line, lines, count):
        size, start = lines * LINE, line * LINE
        k, v = [
            jnp.concatenate(
                [side[line + i, :LINE, j * HEAD_SIZE : (j + 1) * HEAD_SIZE] for i in range(lines)], 0
            )
            for j in (h, HEADS + h)
        ]
        seen = lax.broadcasted_iota(jnp.int32, (size, HEAD_SIZE), 0) + start < count
        return scores_of(queries[h], k), with_ones(v, seen)

    for h in range(HEADS):
        s, v = near(h)
        m = jnp.max(s, axis=1, keepdims=True)
        acc_ref[h] = jnp.dot(jnp.exp2(s - m).astype(jnp.bfloat16), v, preferred_element_type=jnp.float32)
        m_ref[h] = jnp.broadcast_to(m, (ROWS, HEAD_SIZE))
    for side, count in ((side0, count0), (side1, count1)):

        @pl.when(count > 0)
        def _(side=side, count=count):
            for h in range(HEADS):
                s, v = far(h, side, 0, N_Y, count)
                p = jnp.exp2(s - m_ref[h][:, :1]).astype(jnp.bfloat16)
                acc_ref[h] += jnp.dot(p, v, preferred_element_type=jnp.float32)

    worst = jnp.float32(0)
    for h in range(HEADS):
        worst = jnp.maximum(worst, jnp.max(jnp.where(acc_ref[h][:, HEAD_SIZE:] < LIMIT, 0.0, 1.0)))

    @pl.when(worst > 0)
    def _():
        for h in range(HEADS):
            s, v = near(h)
            m = jnp.max(s, axis=1, keepdims=True)
            acc_ref[h] = jnp.dot(jnp.exp2(s - m).astype(jnp.bfloat16), v, preferred_element_type=jnp.float32)
            m_ref[h] = jnp.broadcast_to(m, (ROWS, HEAD_SIZE))
        size = LINE
        for side, count in ((side0, count0), (side1, count1)):

            def fold(i, carry, side=side, count=count):
                for h in range(HEADS):
                    s, v = far(h, side, i, 1, count)
                    col = lax.broadcasted_iota(jnp.int32, (ROWS, size), 1) + i * size
                    s = jnp.where(col < count, s, NEG)
                    old = m_ref[h][:, :1]
                    m = jnp.maximum(old, jnp.max(s, axis=1, keepdims=True))
                    p = jnp.exp2(s - m).astype(jnp.bfloat16)
                    acc_ref[h] = acc_ref[h] * jnp.exp2(old - m) + jnp.dot(p, v, preferred_element_type=jnp.float32)
                    m_ref[h] = jnp.broadcast_to(m, (ROWS, HEAD_SIZE))
                return carry

            lax.fori_loop(0, (count + size - 1) // size, fold, 0)

    outs = [acc_ref[h][:, :HEAD_SIZE] / acc_ref[h][:, HEAD_SIZE:] for h in range(HEADS)]
    attended = jnp.concatenate(
        [o[g * QUARTER : (g + 1) * QUARTER].astype(jnp.bfloat16) for o in outs for g in range(GROUP)], 1
    )
    piece = 1024
    for i in range(0, D, piece):
        out_ref[:, i : i + piece] = jnp.dot(
            attended, weight[:, i : i + piece], preferred_element_type=jnp.float32
        ).astype(jnp.bfloat16)


def attend(info, queries, keys, values, anchor, side0, side1, weight):
    width = HEADS * GROUP * HEAD_SIZE
    whole = lambda i, info: (0, 0)
    resident = pl.BlockSpec(memory_space=pltpu.VMEM)
    return pl.pallas_call(
        attend_kernel,
        out_shape=jax.ShapeDtypeStruct((QUARTER, D), jnp.bfloat16),
        grid_spec=pltpu.PrefetchScalarGridSpec(
            num_scalar_prefetch=1,
            grid=(1,),
            in_specs=[
                pl.BlockSpec((STRIP, width), lambda i, info: (info[0], 0)),
                pl.BlockSpec((STRIP, width), lambda i, info: (info[1], 0)),
                pl.BlockSpec((BLOCK, HEADS * HEAD_SIZE), whole),
                pl.BlockSpec((BLOCK, HEADS * HEAD_SIZE), whole),
                pl.BlockSpec((ANCHOR_ROWS, 2 * HEADS * HEAD_SIZE), whole),
                resident,
                resident,
                resident,
            ],
            out_specs=pl.BlockSpec((QUARTER, D), whole),
            scratch_shapes=[
                pltpu.VMEM((HEADS, ROWS, HEAD_SIZE), jnp.float32),
                pltpu.VMEM((HEADS, ROWS, 2 * HEAD_SIZE), jnp.float32),
            ],
        ),
        compiler_params=pltpu.CompilerParams(vmem_limit_bytes=36 << 20),
        name="attend",
    )(info, queries, queries, keys, values, anchor, side0, side1, weight)


def pick_kernel(rows_ref, k_ref, v_ref, out_ref):
    one_hot = lax.broadcasted_iota(jnp.int32, (PASSING, BLOCK), 1) == rows_ref[...]
    one_hot = jnp.where(one_hot, 1.0, 0.0).astype(jnp.bfloat16)
    for i, ref in enumerate((k_ref, v_ref)):
        out_ref[:, i * WIDTH : (i + 1) * WIDTH] = jnp.dot(
            one_hot, ref[...], preferred_element_type=jnp.float32
        ).astype(jnp.bfloat16)


def units_kernel(picked_ref, slices_ref, out_ref):
    for z in range(N_Z):
        out_ref[z, :PASSING] = picked_ref[...]
        out_ref[z, PASSING:] = slices_ref[z * SLICE : (z + 1) * SLICE]


def planes_kernel(line_ref, out_ref):
    for y in range(N_Y):
        for z in range(N_Z):
            out_ref[y, z * PASSING : (z + 1) * PASSING] = line_ref[z, :PASSING]
        out_ref[y, LINE:] = line_ref[0, PASSING:]


def local(kernel, shape, name):
    return pl.pallas_call(kernel, out_shape=jax.ShapeDtypeStruct(shape, jnp.bfloat16), name=name)


def place(y, z, core):
    return ((y % N_Y) * N_Z + z % N_Z) * N_CORE + core


def send(x, pairs):
    return lax.ppermute(x, "hst", pairs)


def on_device(queries, keys, values, pass_rows, out_weight):
    host = lax.axis_index("hst")
    me = lax.axis_index("head")
    first = jnp.concatenate([keys[:ANCHOR_ROWS], values[:ANCHOR_ROWS]], 1)
    other = send(first, [(0, 1)])
    picked = local(pick_kernel, (PASSING, 2 * WIDTH), "pick")(pass_rows.reshape(PASSING, 1), keys, values)
    along_z = [[place(y, z, c) for z in range(N_Z)] for y in range(N_Y) for c in range(N_CORE)]
    along_y = [[place(y, z, c) for y in range(N_Y)] for z in range(N_Z) for c in range(N_CORE)]
    a2a = functools.partial(lax.all_to_all, axis_name="hst", split_axis=0, concat_axis=0, tiled=True)
    cores = [(h, h ^ 1) for h in range(N_Y * N_Z * N_CORE)]
    units = local(units_kernel, (N_Z, PASSING + SLICE, 2 * WIDTH), "units")(
        picked, jnp.where(host == 0, first, other)
    )
    line = a2a(units, axis_index_groups=along_z)
    side0 = a2a(local(planes_kernel, (N_Y, PLANE, 2 * WIDTH), "planes")(line), axis_index_groups=along_y)
    side1 = send(side0, cores)
    piece = side0[0, LINE:]
    anchor = a2a(jnp.broadcast_to(piece[None], (N_Z, *piece.shape)), axis_index_groups=along_z)
    anchor = anchor.reshape(ANCHOR_ROWS, 2 * WIDTH)
    share = pass_rows.shape[1]
    chip, core = host // N_CORE, host % N_CORE
    count0, count1 = chip * share, (chip + core) * share

    def part(a, b, queries=queries):
        info = jnp.stack([a, b, count0, count1, host]).astype(jnp.int32)
        return attend(info, queries, keys, values, anchor, side0, side1, out_weight)

    def shift(x, step):
        return lax.ppermute(x, "head", [(i, (i + step) % N_HEAD) for i in range(N_HEAD)])

    half = D // 2
    right, left, far = [(me + step) % N_HEAD * 2 for step in (1, 3, 2)]
    opposite = part(far, far + 1)
    low = shift(opposite[:, :half], 1)
    high = shift(opposite[:, half:], -1)
    from_left, from_right = [], []
    held = queries
    for strip in range(2):
        rows = slice(strip * STRIP, (strip + 1) * STRIP)
        both = part(right + strip, left + strip, held)
        r, l = both[:STRIP], both[STRIP:]
        r = jnp.concatenate([r[:, :half] + low[rows], r[:, half:]], 1)
        l = jnp.concatenate([l[:, :half], l[:, half:] + high[rows]], 1)
        held, r, l = lax.optimization_barrier((queries, r, l))
        from_left.append(shift(r, 1))
        from_right.append(shift(l, -1))
    own = part(me * 2, me * 2 + 1, held).astype(jnp.float32)
    return (own + jnp.concatenate(from_left, 0) + jnp.concatenate(from_right, 0)).astype(jnp.bfloat16)


def solution(mesh):
    placed = (P("hst", "head"), P("hst", "head"), P("hst", "head"), P("hst", None), P("head", None))
    return jax.shard_map(
        on_device, mesh=mesh, in_specs=placed, out_specs=P(("hst", "head"), None), check_vma=False
    )
```

```python
import functools

import jax
import jax.numpy as jnp
import numpy as np
from jax import lax
from jax.experimental import pallas as pl
from jax.experimental.pallas import tpu as pltpu
from jax.sharding import PartitionSpec as P

HEAD_SIZE = 128
GROUP = 4
HEADS = 2
ANCHOR_ROWS = 128
BLOCK = 512
QUARTER = 128
STRIP = 64
ROWS = GROUP * QUARTER
N_Y, N_Z, N_CORE, N_HEAD = 4, 8, 2, 4
PASSING = 64
WIDTH = HEADS * HEAD_SIZE
SLICE = ANCHOR_ROWS // N_Y
LINE = N_Z * PASSING
SIDE = N_Y * LINE
PLANE = LINE + SLICE
D = 4096
FACTOR = float(HEAD_SIZE**-0.5 * np.log2(np.e))
NEG = -1e30
LIMIT = float(2.0**110)


def scores_of(q, k):
    return lax.dot_general(q, k, (((1,), (1,)), ((), ())), preferred_element_type=jnp.float32) * FACTOR


def with_ones(v, seen):
    return jnp.concatenate([jnp.where(seen, v, 0), jnp.where(seen, jnp.ones_like(v), 0)], 1)


def attend_kernel(
    info, qa_ref, qb_ref, k_ref, v_ref, side0, side1, weight_hbm, out_ref, m_ref, acc_ref, weight, sem
):
    count0, count1, later = info[2], info[3], info[4]
    load = pltpu.make_async_copy(weight_hbm, weight, sem)
    load.start()
    queries = [
        jnp.concatenate(
            [
                q[:, (h * GROUP + g) * HEAD_SIZE : (h * GROUP + g + 1) * HEAD_SIZE]
                for g in range(GROUP)
                for q in (qa_ref, qb_ref)
            ],
            0,
        )
        for h in range(HEADS)
    ]

    anchor = jnp.concatenate(
        [jnp.where(later % N_CORE == 0, side0[y, LINE:], side1[y, LINE:]) for y in range(N_Y)], 0
    )
    row = lax.broadcasted_iota(jnp.int32, (QUARTER, BLOCK + ANCHOR_ROWS), 0)
    row = row + jnp.where(row < STRIP, info[0] * STRIP, info[1] * STRIP - STRIP)
    col = lax.broadcasted_iota(jnp.int32, (QUARTER, BLOCK + ANCHOR_ROWS), 1)
    seen = (col <= row) | ((col >= BLOCK) & (later > 0))
    unseen = jnp.concatenate([jnp.where(seen, 0.0, NEG)] * GROUP, 0)

    def near(h):
        columns = slice(h * HEAD_SIZE, (h + 1) * HEAD_SIZE)
        k = jnp.concatenate([k_ref[:, columns], anchor[:, columns]], 0)
        v = jnp.concatenate([v_ref[:, columns], anchor[:, (HEADS + h) * HEAD_SIZE : (HEADS + h + 1) * HEAD_SIZE]], 0)
        return scores_of(queries[h], k) + unseen, jnp.concatenate([v, jnp.ones_like(v)], 1)

    def far(h, side, line, lines, count):
        size, start = lines * LINE, line * LINE
        k, v = [
            jnp.concatenate(
                [side[line + i, :LINE, j * HEAD_SIZE : (j + 1) * HEAD_SIZE] for i in range(lines)], 0
            )
            for j in (h, HEADS + h)
        ]
        seen = lax.broadcasted_iota(jnp.int32, (size, HEAD_SIZE), 0) + start < count
        return scores_of(queries[h], k), with_ones(v, seen)

    for h in range(HEADS):
        s, v = near(h)
        m = jnp.max(s, axis=1, keepdims=True)
        acc_ref[h] = jnp.dot(jnp.exp2(s - m).astype(jnp.bfloat16), v, preferred_element_type=jnp.float32)
        m_ref[h] = jnp.broadcast_to(m, (ROWS, HEAD_SIZE))
    for side, count in ((side0, count0), (side1, count1)):

        @pl.when(count > 0)
        def _(side=side, count=count):
            for h in range(HEADS):
                s, v = far(h, side, 0, N_Y, count)
                p = jnp.exp2(s - m_ref[h][:, :1]).astype(jnp.bfloat16)
                acc_ref[h] += jnp.dot(p, v, preferred_element_type=jnp.float32)

    worst = jnp.float32(0)
    for h in range(HEADS):
        worst = jnp.maximum(worst, jnp.max(jnp.where(acc_ref[h][:, HEAD_SIZE:] < LIMIT, 0.0, 1.0)))

    @pl.when(worst > 0)
    def _():
        for h in range(HEADS):
            s, v = near(h)
            m = jnp.max(s, axis=1, keepdims=True)
            acc_ref[h] = jnp.dot(jnp.exp2(s - m).astype(jnp.bfloat16), v, preferred_element_type=jnp.float32)
            m_ref[h] = jnp.broadcast_to(m, (ROWS, HEAD_SIZE))
        size = LINE
        for side, count in ((side0, count0), (side1, count1)):

            def fold(i, carry, side=side, count=count):
                for h in range(HEADS):
                    s, v = far(h, side, i, 1, count)
                    col = lax.broadcasted_iota(jnp.int32, (ROWS, size), 1) + i * size
                    s = jnp.where(col < count, s, NEG)
                    old = m_ref[h][:, :1]
                    m = jnp.maximum(old, jnp.max(s, axis=1, keepdims=True))
                    p = jnp.exp2(s - m).astype(jnp.bfloat16)
                    acc_ref[h] = acc_ref[h] * jnp.exp2(old - m) + jnp.dot(p, v, preferred_element_type=jnp.float32)
                    m_ref[h] = jnp.broadcast_to(m, (ROWS, HEAD_SIZE))
                return carry

            lax.fori_loop(0, (count + size - 1) // size, fold, 0)

    load.wait()
    outs = [acc_ref[h][:, :HEAD_SIZE] / acc_ref[h][:, HEAD_SIZE:] for h in range(HEADS)]
    attended = jnp.concatenate(
        [o[g * QUARTER : (g + 1) * QUARTER].astype(jnp.bfloat16) for o in outs for g in range(GROUP)], 1
    )
    piece = 1024
    for i in range(0, D, piece):
        out_ref[:, i : i + piece] = jnp.dot(
            attended, weight[:, i : i + piece], preferred_element_type=jnp.float32
        ).astype(jnp.bfloat16)


def attend(info, queries, keys, values, side0, side1, weight):
    width = HEADS * GROUP * HEAD_SIZE
    whole = lambda i, info: (0, 0)
    resident = pl.BlockSpec(memory_space=pltpu.VMEM)
    return pl.pallas_call(
        attend_kernel,
        out_shape=jax.ShapeDtypeStruct((QUARTER, D), jnp.bfloat16),
        grid_spec=pltpu.PrefetchScalarGridSpec(
            num_scalar_prefetch=1,
            grid=(1,),
            in_specs=[
                pl.BlockSpec((STRIP, width), lambda i, info: (info[0], 0)),
                pl.BlockSpec((STRIP, width), lambda i, info: (info[1], 0)),
                pl.BlockSpec((BLOCK, HEADS * HEAD_SIZE), whole),
                pl.BlockSpec((BLOCK, HEADS * HEAD_SIZE), whole),
                resident,
                resident,
                pl.BlockSpec(memory_space=pl.ANY),
            ],
            out_specs=pl.BlockSpec((QUARTER, D), whole),
            scratch_shapes=[
                pltpu.VMEM((HEADS, ROWS, HEAD_SIZE), jnp.float32),
                pltpu.VMEM((HEADS, ROWS, 2 * HEAD_SIZE), jnp.float32),
                pltpu.VMEM((width, D), jnp.bfloat16),
                pltpu.SemaphoreType.DMA(()),
            ],
        ),
        compiler_params=pltpu.CompilerParams(vmem_limit_bytes=40 << 20),
        name="attend",
    )(info, queries, queries, keys, values, side0, side1, weight)


def slices_kernel(k_ref, v_ref, *outs):
    for i, out in enumerate(outs):
        rows = pl.ds((i + 1) * SLICE, SLICE)
        out[:, :WIDTH] = k_ref[rows]
        out[:, WIDTH:] = v_ref[rows]


def pick_kernel(rows_ref, k_ref, v_ref, out_ref):
    one_hot = lax.broadcasted_iota(jnp.int32, (BLOCK, PASSING), 0) == rows_ref[...]
    one_hot = jnp.where(one_hot, 1.0, 0.0).astype(jnp.bfloat16)
    for i, ref in enumerate((k_ref, v_ref)):
        out_ref[:, i * WIDTH : (i + 1) * WIDTH] = lax.dot_general(
            one_hot, ref[...], (((0,), (0,)), ((), ())), preferred_element_type=jnp.float32
        ).astype(jnp.bfloat16)


def units_kernel(host, picked_ref, k_ref, v_ref, *refs):
    *slices, out_ref = refs
    own = jnp.concatenate([k_ref[:SLICE], v_ref[:SLICE]], 1)
    piece = jnp.where(host[0] == 0, own, jnp.zeros_like(own))
    for ref in slices:
        piece = piece + ref[...]
    for z in range(N_Z):
        out_ref[z, :PASSING] = picked_ref[...]
        out_ref[z, PASSING:] = piece


def planes_kernel(line_ref, out_ref):
    for y in range(N_Y):
        for z in range(N_Z):
            out_ref[y, z * PASSING : (z + 1) * PASSING] = line_ref[z, :PASSING]
        out_ref[y, LINE:] = line_ref[0, PASSING:]


def local(kernel, shapes, name):
    shapes = [jax.ShapeDtypeStruct(shape, jnp.bfloat16) for shape in shapes]
    return pl.pallas_call(kernel, out_shape=shapes, name=name)


def units_of(host, picked, keys, values, slices):
    vmem = pl.BlockSpec(memory_space=pltpu.VMEM)
    return pl.pallas_call(
        units_kernel,
        out_shape=jax.ShapeDtypeStruct((N_Z, PASSING + SLICE, 2 * WIDTH), jnp.bfloat16),
        in_specs=[pl.BlockSpec(memory_space=pltpu.SMEM)] + [vmem] * (3 + len(slices)),
        out_specs=vmem,
        name="units",
    )(host.reshape(1), picked, keys[:SLICE], values[:SLICE], *slices)


def place(y, z, core):
    return ((y % N_Y) * N_Z + z % N_Z) * N_CORE + core


def send(x, pairs):
    return lax.ppermute(x, "hst", pairs)


def on_device(queries, keys, values, pass_rows, out_weight):
    host = lax.axis_index("hst")
    me = lax.axis_index("head")
    along_z = [[place(y, z, c) for z in range(N_Z)] for y in range(N_Y) for c in range(N_CORE)]
    along_y = [[place(y, z, c) for y in range(N_Y)] for z in range(N_Z) for c in range(N_CORE)]
    a2a = functools.partial(lax.all_to_all, axis_name="hst", split_axis=0, concat_axis=0, tiled=True)
    cores = [(h, h ^ 1) for h in range(N_Y * N_Z * N_CORE)]
    slices = local(slices_kernel, [(SLICE, 2 * WIDTH)] * (N_Y - 1), "slices")(keys[:ANCHOR_ROWS], values[:ANCHOR_ROWS])
    slices = [send(x, [(0, place(y + 1, 0, 0))]) for y, x in enumerate(slices)]
    (picked,) = local(pick_kernel, [(PASSING, 2 * WIDTH)], "pick")(pass_rows, keys, values)
    units = units_of(host, picked, keys, values, slices)
    line = a2a(units, axis_index_groups=along_z)
    (planes,) = local(planes_kernel, [(N_Y, PLANE, 2 * WIDTH)], "planes")(line)
    side0 = a2a(planes, axis_index_groups=along_y)
    side1 = send(side0, cores)
    return back_end(host, me, queries, keys, values, side0, side1, out_weight)


def back_end(host, me, queries, keys, values, side0, side1, out_weight):
    chip, core = host // N_CORE, host % N_CORE
    count0, count1 = chip * PASSING, (chip + core) * PASSING

    def part(a, b, queries=queries):
        info = jnp.stack([a, b, count0, count1, host]).astype(jnp.int32)
        return attend(info, queries, keys, values, side0, side1, out_weight)

    def shift(x, step):
        return lax.ppermute(x, "head", [(i, (i + step) % N_HEAD) for i in range(N_HEAD)])

    half = D // 2
    right, left, far = [(me + step) % N_HEAD * 2 for step in (1, 3, 2)]
    opposite = part(far, far + 1)
    low = shift(opposite[:, :half], 1)
    high = shift(opposite[:, half:], -1)
    from_left, from_right = [], []
    held = queries
    for strip in range(2):
        rows = slice(strip * STRIP, (strip + 1) * STRIP)
        both = part(right + strip, left + strip, held)
        r, l = both[:STRIP], both[STRIP:]
        r = jnp.concatenate([r[:, :half] + low[rows], r[:, half:]], 1)
        l = jnp.concatenate([l[:, :half], l[:, half:] + high[rows]], 1)
        held, r, l = lax.optimization_barrier((queries, r, l))
        from_left.append(shift(r, 1))
        from_right.append(shift(l, -1))
    own = part(me * 2, me * 2 + 1, held).astype(jnp.float32)
    return (own + jnp.concatenate(from_left, 0) + jnp.concatenate(from_right, 0)).astype(jnp.bfloat16)


def solution(mesh):
    placed = (P("hst", "head"), P("hst", "head"), P("hst", "head"), P("hst", None), P("head", None))
    return jax.shard_map(
        on_device, mesh=mesh, in_specs=placed, out_specs=P(("hst", "head"), None), check_vma=False
    )
```

```python
import functools

import jax
import jax.numpy as jnp
import numpy as np
from jax import lax
from jax.experimental import pallas as pl
from jax.experimental.pallas import tpu as pltpu
from jax.sharding import PartitionSpec as P

HEAD_SIZE = 128
GROUP = 4
HEADS = 2
ANCHOR_ROWS = 128
BLOCK = 512
QUARTER = 128
STRIP = 64
ROWS = GROUP * QUARTER
N_Y, N_Z, N_CORE, N_HEAD = 4, 8, 2, 4
PASSING = 64
WIDTH = HEADS * HEAD_SIZE
SLICE = ANCHOR_ROWS // N_Y
LINE = N_Z * PASSING
SIDE = N_Y * LINE
PLANE = LINE + SLICE
D = 4096
FACTOR = float(HEAD_SIZE**-0.5 * np.log2(np.e))
NEG = -1e30
LIMIT = float(2.0**110)


def scores_of(q, k):
    return lax.dot_general(q, k, (((1,), (1,)), ((), ())), preferred_element_type=jnp.float32) * FACTOR


def with_ones(v, seen):
    return jnp.concatenate([jnp.where(seen, v, 0), jnp.where(seen, jnp.ones_like(v), 0)], 1)


def attend_kernel(info, q_ref, k_ref, v_ref, side0, side1, weight_hbm, *refs):
    *added, out_a, out_b, m_ref, acc_ref, weight, sem = refs
    count0, count1, later = info[2], info[3], info[4]
    load = pltpu.make_async_copy(weight_hbm, weight, sem)
    load.start()
    strips = [q_ref[pl.ds(pl.multiple_of(info[i] * STRIP, STRIP), STRIP)] for i in range(2)]
    queries = [
        jnp.concatenate(
            [x[:, (h * GROUP + g) * HEAD_SIZE : (h * GROUP + g + 1) * HEAD_SIZE] for g in range(GROUP) for x in strips],
            0,
        )
        for h in range(HEADS)
    ]

    anchor = jnp.concatenate(
        [jnp.where(later % N_CORE == 0, side0[y, LINE:], side1[y, LINE:]) for y in range(N_Y)], 0
    )
    row = lax.broadcasted_iota(jnp.int32, (QUARTER, BLOCK + ANCHOR_ROWS), 0)
    row = row + jnp.where(row < STRIP, info[0] * STRIP, info[1] * STRIP - STRIP)
    col = lax.broadcasted_iota(jnp.int32, (QUARTER, BLOCK + ANCHOR_ROWS), 1)
    seen = (col <= row) | ((col >= BLOCK) & (later > 0))
    unseen = jnp.concatenate([jnp.where(seen, 0.0, NEG)] * GROUP, 0)

    def near(h):
        columns = slice(h * HEAD_SIZE, (h + 1) * HEAD_SIZE)
        k = jnp.concatenate([k_ref[:, columns], anchor[:, columns]], 0)
        v = jnp.concatenate([v_ref[:, columns], anchor[:, (HEADS + h) * HEAD_SIZE : (HEADS + h + 1) * HEAD_SIZE]], 0)
        return scores_of(queries[h], k) + unseen, jnp.concatenate([v, jnp.ones_like(v)], 1)

    def far(h, side, line, lines, count):
        size, start = lines * LINE, line * LINE
        k, v = [
            jnp.concatenate(
                [side[line + i, :LINE, j * HEAD_SIZE : (j + 1) * HEAD_SIZE] for i in range(lines)], 0
            )
            for j in (h, HEADS + h)
        ]
        seen = lax.broadcasted_iota(jnp.int32, (size, HEAD_SIZE), 0) + start < count
        return scores_of(queries[h], k), with_ones(v, seen)

    for h in range(HEADS):
        s, v = near(h)
        m = jnp.max(s, axis=1, keepdims=True)
        acc_ref[h] = jnp.dot(jnp.exp2(s - m).astype(jnp.bfloat16), v, preferred_element_type=jnp.float32)
        m_ref[h] = jnp.broadcast_to(m, (ROWS, HEAD_SIZE))
    for side, count in ((side0, count0), (side1, count1)):

        @pl.when(count > 0)
        def _(side=side, count=count):
            for h in range(HEADS):
                s, v = far(h, side, 0, N_Y, count)
                p = jnp.exp2(s - m_ref[h][:, :1]).astype(jnp.bfloat16)
                acc_ref[h] += jnp.dot(p, v, preferred_element_type=jnp.float32)

    worst = jnp.float32(0)
    for h in range(HEADS):
        worst = jnp.maximum(worst, jnp.max(jnp.where(acc_ref[h][:, HEAD_SIZE:] < LIMIT, 0.0, 1.0)))

    @pl.when(worst > 0)
    def _():
        for h in range(HEADS):
            s, v = near(h)
            m = jnp.max(s, axis=1, keepdims=True)
            acc_ref[h] = jnp.dot(jnp.exp2(s - m).astype(jnp.bfloat16), v, preferred_element_type=jnp.float32)
            m_ref[h] = jnp.broadcast_to(m, (ROWS, HEAD_SIZE))
        size = LINE
        for side, count in ((side0, count0), (side1, count1)):

            def fold(i, carry, side=side, count=count):
                for h in range(HEADS):
                    s, v = far(h, side, i, 1, count)
                    col = lax.broadcasted_iota(jnp.int32, (ROWS, size), 1) + i * size
                    s = jnp.where(col < count, s, NEG)
                    old = m_ref[h][:, :1]
                    m = jnp.maximum(old, jnp.max(s, axis=1, keepdims=True))
                    p = jnp.exp2(s - m).astype(jnp.bfloat16)
                    acc_ref[h] = acc_ref[h] * jnp.exp2(old - m) + jnp.dot(p, v, preferred_element_type=jnp.float32)
                    m_ref[h] = jnp.broadcast_to(m, (ROWS, HEAD_SIZE))
                return carry

            lax.fori_loop(0, (count + size - 1) // size, fold, 0)

    load.wait()
    outs = [acc_ref[h][:, :HEAD_SIZE] / acc_ref[h][:, HEAD_SIZE:] for h in range(HEADS)]
    attended = jnp.concatenate(
        [o[g * QUARTER : (g + 1) * QUARTER].astype(jnp.bfloat16) for o in outs for g in range(GROUP)], 1
    )
    piece = 1024
    for i in range(0, D, piece):
        columns = slice(i, i + piece)
        x = jnp.dot(attended, weight[:, columns], preferred_element_type=jnp.float32)
        for j, out in enumerate((out_a, out_b)):
            strip = x[j * STRIP : (j + 1) * STRIP]
            for ref in added[j::2]:
                strip = strip + ref[:, columns].astype(jnp.float32)
            out[:, columns] = strip.astype(jnp.bfloat16)


def attend(info, queries, keys, values, side0, side1, weight, added):
    width = HEADS * GROUP * HEAD_SIZE
    resident = pl.BlockSpec(memory_space=pltpu.VMEM)
    return pl.pallas_call(
        attend_kernel,
        out_shape=[jax.ShapeDtypeStruct((STRIP, D), jnp.bfloat16)] * 2,
        in_specs=[pl.BlockSpec(memory_space=pltpu.SMEM)]
        + [resident] * 5
        + [pl.BlockSpec(memory_space=pl.ANY)]
        + [resident] * len(added),
        out_specs=[resident] * 2,
        scratch_shapes=[
            pltpu.VMEM((HEADS, ROWS, HEAD_SIZE), jnp.float32),
            pltpu.VMEM((HEADS, ROWS, 2 * HEAD_SIZE), jnp.float32),
            pltpu.VMEM((width, D), jnp.bfloat16),
            pltpu.SemaphoreType.DMA(()),
        ],
        compiler_params=pltpu.CompilerParams(vmem_limit_bytes=40 << 20),
        name="attend",
    )(info, queries, keys, values, side0, side1, weight, *added)


def slices_kernel(k_hbm, v_hbm, *refs):
    *outs, sem = refs
    copies = [
        pltpu.make_async_copy(x.at[pl.ds(i * SLICE, SLICE)], out.at[:, pl.ds(j * WIDTH, WIDTH)], sem.at[i, j])
        for i, out in enumerate(outs)
        for j, x in enumerate((k_hbm, v_hbm))
    ]
    for copy in copies:
        copy.start()
    for copy in copies:
        copy.wait()


def slices_of(keys, values):
    return pl.pallas_call(
        slices_kernel,
        out_shape=[jax.ShapeDtypeStruct((SLICE, 2 * WIDTH), jnp.bfloat16)] * N_Y,
        in_specs=[pl.BlockSpec(memory_space=pl.ANY)] * 2,
        out_specs=[pl.BlockSpec(memory_space=pltpu.VMEM)] * N_Y,
        scratch_shapes=[pltpu.SemaphoreType.DMA((N_Y, 2))],
        name="slices",
    )(keys, values)


def pick_kernel(rows_ref, k_hbm, v_hbm, out_ref, k_buf, v_buf, sem):
    pairs = ((k_hbm, k_buf), (v_hbm, v_buf))
    copies = [pltpu.make_async_copy(x, buf, sem.at[i]) for i, (x, buf) in enumerate(pairs)]
    for copy in copies:
        copy.start()
    one_hot = lax.broadcasted_iota(jnp.int32, (BLOCK, PASSING), 0) == rows_ref[...]
    one_hot = jnp.where(one_hot, 1.0, 0.0).astype(jnp.bfloat16)
    for i, (copy, (_, buf)) in enumerate(zip(copies, pairs)):
        copy.wait()
        out_ref[:, i * WIDTH : (i + 1) * WIDTH] = lax.dot_general(
            one_hot, buf[...], (((0,), (0,)), ((), ())), preferred_element_type=jnp.float32
        ).astype(jnp.bfloat16)


def pick(rows, keys, values):
    vmem, anywhere = pl.BlockSpec(memory_space=pltpu.VMEM), pl.BlockSpec(memory_space=pl.ANY)
    return pl.pallas_call(
        pick_kernel,
        out_shape=jax.ShapeDtypeStruct((PASSING, 2 * WIDTH), jnp.bfloat16),
        in_specs=[vmem, anywhere, anywhere],
        out_specs=vmem,
        scratch_shapes=[pltpu.VMEM((BLOCK, WIDTH), jnp.bfloat16)] * 2 + [pltpu.SemaphoreType.DMA((2,))],
        name="pick",
    )(rows, keys, values)


def units_kernel(host, picked_ref, own_ref, *refs):
    *slices, out_ref = refs
    piece = jnp.where(host[0] == 0, own_ref[...], jnp.zeros(own_ref.shape, own_ref.dtype))
    for ref in slices:
        piece = piece + ref[...]
    for z in range(N_Z):
        out_ref[z, :PASSING] = picked_ref[...]
        out_ref[z, PASSING:] = piece


def planes_kernel(line_ref, out_ref):
    for y in range(N_Y):
        for z in range(N_Z):
            out_ref[y, z * PASSING : (z + 1) * PASSING] = line_ref[z, :PASSING]
        out_ref[y, LINE:] = line_ref[0, PASSING:]


def local(kernel, shapes, name):
    shapes = [jax.ShapeDtypeStruct(shape, jnp.bfloat16) for shape in shapes]
    return pl.pallas_call(kernel, out_shape=shapes, name=name)


def units_of(host, picked, own, slices):
    vmem = pl.BlockSpec(memory_space=pltpu.VMEM)
    return pl.pallas_call(
        units_kernel,
        out_shape=jax.ShapeDtypeStruct((N_Z, PASSING + SLICE, 2 * WIDTH), jnp.bfloat16),
        in_specs=[pl.BlockSpec(memory_space=pltpu.SMEM)] + [vmem] * (2 + len(slices)),
        out_specs=vmem,
        name="units",
    )(host.reshape(1), picked, own, *slices)


def place(y, z, core):
    return ((y % N_Y) * N_Z + z % N_Z) * N_CORE + core


def send(x, pairs):
    return lax.ppermute(x, "hst", pairs)


def on_device(queries, keys, values, pass_rows, out_weight):
    host = lax.axis_index("hst")
    me = lax.axis_index("head")
    along_z = [[place(y, z, c) for z in range(N_Z)] for y in range(N_Y) for c in range(N_CORE)]
    along_y = [[place(y, z, c) for y in range(N_Y)] for z in range(N_Z) for c in range(N_CORE)]
    a2a = functools.partial(lax.all_to_all, axis_name="hst", split_axis=0, concat_axis=0, tiled=True)
    cores = [(h, h ^ 1) for h in range(N_Y * N_Z * N_CORE)]
    first, *slices = slices_of(keys, values)
    slices = [send(x, [(0, place(y + 1, 0, 0))]) for y, x in enumerate(slices)]
    units = units_of(host, pick(pass_rows, keys, values), first, slices)
    line = a2a(units, axis_index_groups=along_z)
    (planes,) = local(planes_kernel, [(N_Y, PLANE, 2 * WIDTH)], "planes")(line)
    side0 = a2a(planes, axis_index_groups=along_y)
    side1 = send(side0, cores)
    return back_end(host, me, queries, keys, values, side0, side1, out_weight)


def back_end(host, me, queries, keys, values, side0, side1, out_weight):
    chip, core = host // N_CORE, host % N_CORE
    count0, count1 = chip * PASSING, (chip + core) * PASSING

    def part(a, b, *added, queries=queries):
        info = jnp.stack([a, b, count0, count1, host]).astype(jnp.int32)
        return attend(info, queries, keys, values, side0, side1, out_weight, added)

    def shift(x, step):
        return lax.ppermute(x, "head", [(i, (i + step) % N_HEAD) for i in range(N_HEAD)])

    right, left, far, own = [(me + step) % N_HEAD * 2 for step in (1, 3, 2, 0)]
    a, b = part(far, far + 1)
    via_right, via_left = shift(a, 1), shift(b, -1)
    a, b = part(right + 1, left)
    held, a, b = lax.optimization_barrier((queries, a, b))
    left1, right0 = shift(a, 1), shift(b, -1)
    a, b = part(right, left + 1, via_right, via_left, queries=held)
    held, a, b = lax.optimization_barrier((queries, a, b))
    left0, right1 = shift(a, 1), shift(b, -1)
    a, b = part(own, own + 1, right0, left1, queries=held)
    return join(a, b, left0, right1)


def join_kernel(a, b, left0, right1, out):
    out[:STRIP] = a[...] + left0[...]
    out[STRIP:] = b[...] + right1[...]


def join(*strips):
    return local(join_kernel, [(2 * STRIP, D)], "join")(*strips)[0]


def solution(mesh):
    placed = (P("hst", "head"), P("hst", "head"), P("hst", "head"), P("hst", None), P("head", None))
    return jax.shard_map(
        on_device, mesh=mesh, in_specs=placed, out_specs=P(("hst", "head"), None), check_vma=False
    )
```

```python
import functools

import jax
import jax.numpy as jnp
import numpy as np
from jax import lax
from jax.experimental import pallas as pl
from jax.experimental.pallas import tpu as pltpu
from jax.sharding import PartitionSpec as P

HEAD_SIZE = 128
GROUP = 4
HEADS = 2
ANCHOR_ROWS = 128
BLOCK = 512
QUARTER = 128
STRIP = 64
ROWS = GROUP * QUARTER
N_Y, N_Z, N_CORE, N_HEAD = 4, 8, 2, 4
PASSING = 64
WIDTH = HEADS * HEAD_SIZE
SLICE = ANCHOR_ROWS // N_Y
LINE = N_Z * PASSING
SIDE = N_Y * LINE
PLANE = LINE + SLICE
D = 4096
FACTOR = float(HEAD_SIZE**-0.5 * np.log2(np.e))
NEG = -1e30
LIMIT = float(2.0**110)


def scores_of(q, k):
    return lax.dot_general(q, k, (((1,), (1,)), ((), ())), preferred_element_type=jnp.float32) * FACTOR


def with_ones(v, seen):
    return jnp.concatenate([jnp.where(seen, v, 0), jnp.where(seen, jnp.ones_like(v), 0)], 1)


def attend_kernel(steps, info, q_hbm, k_hbm, v_hbm, side0, side1, weight_hbm, *refs):
    *added, out_a, out_b, acc_ref, q_ref, k_ref, v_ref, anchor_ref, unseen_ref, attended_ref, weight, sems = refs
    host, me = info[0], info[1]
    first = [(me + step) % N_HEAD * QUARTER + strip * STRIP for step, strip in steps]
    count0, count1 = host // N_CORE * PASSING, (host + 1) // N_CORE * PASSING
    count1 = jnp.where(host % N_CORE == 0, count0, count1)
    loads = [
        pltpu.make_async_copy(q_hbm.at[pl.ds(pl.multiple_of(x, STRIP), STRIP)], q_ref.at[i], sems.at[i])
        for i, x in enumerate(first)
    ] + [
        pltpu.make_async_copy(source, ref, sems.at[2 + i])
        for i, (source, ref) in enumerate(((k_hbm, k_ref), (v_hbm, v_ref), (weight_hbm, weight)))
    ]
    for load in loads:
        load.start()
    *loads, last = loads
    for y in range(N_Y):
        anchor_ref[y * SLICE : (y + 1) * SLICE] = jnp.where(host % N_CORE == 0, side0[y, LINE:], side1[y, LINE:])
    row = lax.broadcasted_iota(jnp.int32, (QUARTER, BLOCK + ANCHOR_ROWS), 0)
    row = row + jnp.where(row < STRIP, first[0], first[1] - STRIP)
    col = lax.broadcasted_iota(jnp.int32, (QUARTER, BLOCK + ANCHOR_ROWS), 1)
    seen = (col <= row) | ((col >= BLOCK) & (host > 0))
    unseen_ref[...] = jnp.where(seen, 0.0, NEG)
    for load in loads:
        load.wait()
    def columns(i):
        return pl.ds(i * HEAD_SIZE if isinstance(i, int) else pl.multiple_of(i * HEAD_SIZE, HEAD_SIZE), HEAD_SIZE)

    def queries(h, g):
        return [q_ref[i, :, columns(h * GROUP + g)] for i in range(2)]

    def near(h):
        k = jnp.concatenate([k_ref[:, columns(h)], anchor_ref[:, columns(h)]], 0)
        v = jnp.concatenate([v_ref[:, columns(h)], anchor_ref[:, columns(HEADS + h)]], 0)
        return k, jnp.concatenate([v, jnp.ones_like(v)], 1)

    def far(h, side, line, lines, count):
        k, v = [
            jnp.concatenate([side[line + i, :LINE, columns(j)] for i in range(lines)], 0) for j in (h, HEADS + h)
        ]
        seen = lax.broadcasted_iota(jnp.int32, (lines * LINE, HEAD_SIZE), 0) + line * LINE < count
        return k, with_ones(v, seen)

    def weigh(s, m, v):
        return jnp.dot(jnp.exp2(s - m).astype(jnp.bfloat16), v, preferred_element_type=jnp.float32)

    heads = []
    for h in range(HEADS):
        q = jnp.concatenate([x for g in range(GROUP) for x in queries(h, g)], 0)
        k, v = near(h)
        s = scores_of(q, k) + jnp.concatenate([unseen_ref[...]] * GROUP, 0)
        m = jnp.max(s, axis=1, keepdims=True)
        acc_ref[h] = weigh(s, m, v)
        heads.append((q, m))

    @pl.when(host > 0)
    def _():
        for side, count in ((side0, count0), (side1, count1)):
            for h, (q, m) in enumerate(heads):
                k, v = far(h, side, 0, N_Y, count)
                acc_ref[h] += weigh(scores_of(q, k), m, v)

    worst = jnp.max(jnp.where(acc_ref[:, :, HEAD_SIZE:] < LIMIT, 0.0, 1.0))

    @pl.when(worst > 0)
    def _():
        def again(i, carry):
            h, g = i // GROUP, i % GROUP
            q = jnp.concatenate(queries(h, g), 0)
            k, v = near(h)
            s = scores_of(q, k) + unseen_ref[...]
            m = jnp.max(s, axis=1, keepdims=True)
            state = m, weigh(s, m, v)
            for side, count in ((side0, count0), (side1, count1)):

                def fold(line, state, side=side, count=count):
                    old, acc = state
                    k, v = far(h, side, line, 1, count)
                    col = lax.broadcasted_iota(jnp.int32, (QUARTER, LINE), 1) + line * LINE
                    s = jnp.where(col < count, scores_of(q, k), NEG)
                    m = jnp.maximum(old, jnp.max(s, axis=1, keepdims=True))
                    return m, acc * jnp.exp2(old - m) + weigh(s, m, v)

                state = lax.fori_loop(0, (count + LINE - 1) // LINE, fold, state)
            acc_ref[h, pl.ds(pl.multiple_of(g * QUARTER, QUARTER), QUARTER)] = state[1]
            return carry

        lax.fori_loop(0, HEADS * GROUP, again, 0)

    outs = [acc_ref[h, :, :HEAD_SIZE] / acc_ref[h, :, HEAD_SIZE:] for h in range(HEADS)]
    attended_ref[...] = jnp.concatenate(
        [o[g * QUARTER : (g + 1) * QUARTER].astype(jnp.bfloat16) for o in outs for g in range(GROUP)], 1
    )
    last.wait()
    piece = 1024

    def project(i, carry):
        cut = pl.ds(pl.multiple_of(i * piece, piece), piece)
        x = jnp.dot(attended_ref[...], weight[:, cut], preferred_element_type=jnp.float32)
        for j, out in enumerate((out_a, out_b)):
            strip = x[j * STRIP : (j + 1) * STRIP]
            for ref in added[j::2]:
                strip = strip + ref[:, cut].astype(jnp.float32)
            out[:, cut] = strip.astype(jnp.bfloat16)
        return carry

    lax.fori_loop(0, D // piece, project, 0)


def attend(steps, info, queries, keys, values, side0, side1, weight, added):
    width = HEADS * GROUP * HEAD_SIZE
    resident, anywhere = pl.BlockSpec(memory_space=pltpu.VMEM), pl.BlockSpec(memory_space=pl.ANY)
    return pl.pallas_call(
        functools.partial(attend_kernel, steps),
        out_shape=[jax.ShapeDtypeStruct((STRIP, D), jnp.bfloat16)] * 2,
        in_specs=[pl.BlockSpec(memory_space=pltpu.SMEM)]
        + [anywhere] * 3
        + [resident] * 2
        + [anywhere]
        + [resident] * len(added),
        out_specs=[resident] * 2,
        scratch_shapes=[
            pltpu.VMEM((HEADS, ROWS, 2 * HEAD_SIZE), jnp.float32),
            pltpu.VMEM((2, STRIP, width), jnp.bfloat16),
            pltpu.VMEM((BLOCK, WIDTH), jnp.bfloat16),
            pltpu.VMEM((BLOCK, WIDTH), jnp.bfloat16),
            pltpu.VMEM((ANCHOR_ROWS, 2 * WIDTH), jnp.bfloat16),
            pltpu.VMEM((QUARTER, BLOCK + ANCHOR_ROWS), jnp.float32),
            pltpu.VMEM((QUARTER, width), jnp.bfloat16),
            pltpu.VMEM((width, D), jnp.bfloat16),
            pltpu.SemaphoreType.DMA((5,)),
        ],
        compiler_params=pltpu.CompilerParams(vmem_limit_bytes=40 << 20),
        name="attend",
    )(info, queries, keys, values, side0, side1, weight, *added)


def slices_kernel(k_hbm, v_hbm, *refs):
    *outs, sem = refs
    copies = [
        pltpu.make_async_copy(x.at[pl.ds(i * SLICE, SLICE)], out.at[:, pl.ds(j * WIDTH, WIDTH)], sem.at[i, j])
        for i, out in enumerate(outs)
        for j, x in enumerate((k_hbm, v_hbm))
    ]
    for copy in copies:
        copy.start()
    for copy in copies:
        copy.wait()


def slices_of(keys, values):
    return pl.pallas_call(
        slices_kernel,
        out_shape=[jax.ShapeDtypeStruct((SLICE, 2 * WIDTH), jnp.bfloat16)] * N_Y,
        in_specs=[pl.BlockSpec(memory_space=pl.ANY)] * 2,
        out_specs=[pl.BlockSpec(memory_space=pltpu.VMEM)] * N_Y,
        scratch_shapes=[pltpu.SemaphoreType.DMA((N_Y, 2))],
        name="slices",
    )(keys, values)


def pick_kernel(rows_ref, k_hbm, v_hbm, out_ref, k_buf, v_buf, sem):
    pairs = ((k_hbm, k_buf), (v_hbm, v_buf))
    copies = [pltpu.make_async_copy(x, buf, sem.at[i]) for i, (x, buf) in enumerate(pairs)]
    for copy in copies:
        copy.start()
    one_hot = lax.broadcasted_iota(jnp.int32, (BLOCK, PASSING), 0) == rows_ref[...]
    one_hot = jnp.where(one_hot, 1.0, 0.0).astype(jnp.bfloat16)
    for i, (copy, (_, buf)) in enumerate(zip(copies, pairs)):
        copy.wait()
        out_ref[:, i * WIDTH : (i + 1) * WIDTH] = lax.dot_general(
            one_hot, buf[...], (((0,), (0,)), ((), ())), preferred_element_type=jnp.float32
        ).astype(jnp.bfloat16)


def pick(rows, keys, values):
    vmem, anywhere = pl.BlockSpec(memory_space=pltpu.VMEM), pl.BlockSpec(memory_space=pl.ANY)
    return pl.pallas_call(
        pick_kernel,
        out_shape=jax.ShapeDtypeStruct((PASSING, 2 * WIDTH), jnp.bfloat16),
        in_specs=[vmem, anywhere, anywhere],
        out_specs=vmem,
        scratch_shapes=[pltpu.VMEM((BLOCK, WIDTH), jnp.bfloat16)] * 2 + [pltpu.SemaphoreType.DMA((2,))],
        name="pick",
    )(rows, keys, values)


def units_kernel(host, picked_ref, own_ref, *refs):
    *slices, out_ref = refs
    piece = jnp.where(host[0] == 0, own_ref[...], jnp.zeros(own_ref.shape, own_ref.dtype))
    for ref in slices:
        piece = piece + ref[...]
    for z in range(N_Z):
        out_ref[z, :PASSING] = picked_ref[...]
        out_ref[z, PASSING:] = piece


def planes_kernel(line_ref, out_ref):
    for y in range(N_Y):
        for z in range(N_Z):
            out_ref[y, z * PASSING : (z + 1) * PASSING] = line_ref[z, :PASSING]
        out_ref[y, LINE:] = line_ref[0, PASSING:]


def local(kernel, shapes, name):
    shapes = [jax.ShapeDtypeStruct(shape, jnp.bfloat16) for shape in shapes]
    return pl.pallas_call(kernel, out_shape=shapes, name=name)


def units_of(host, picked, own, slices):
    vmem = pl.BlockSpec(memory_space=pltpu.VMEM)
    return pl.pallas_call(
        units_kernel,
        out_shape=jax.ShapeDtypeStruct((N_Z, PASSING + SLICE, 2 * WIDTH), jnp.bfloat16),
        in_specs=[pl.BlockSpec(memory_space=pltpu.SMEM)] + [vmem] * (2 + len(slices)),
        out_specs=vmem,
        name="units",
    )(host.reshape(1), picked, own, *slices)


def place(y, z, core):
    return ((y % N_Y) * N_Z + z % N_Z) * N_CORE + core


def send(x, pairs):
    return lax.ppermute(x, "hst", pairs)


def on_device(queries, keys, values, pass_rows, out_weight):
    host = lax.axis_index("hst")
    me = lax.axis_index("head")
    along_z = [[place(y, z, c) for z in range(N_Z)] for y in range(N_Y) for c in range(N_CORE)]
    along_y = [[place(y, z, c) for y in range(N_Y)] for z in range(N_Z) for c in range(N_CORE)]
    a2a = functools.partial(lax.all_to_all, axis_name="hst", split_axis=0, concat_axis=0, tiled=True)
    cores = [(h, h ^ 1) for h in range(N_Y * N_Z * N_CORE)]
    first, *slices = slices_of(keys, values)
    slices = [send(x, [(0, place(y + 1, 0, 0))]) for y, x in enumerate(slices)]
    units = units_of(host, pick(pass_rows, keys, values), first, slices)
    line = a2a(units, axis_index_groups=along_z)
    (planes,) = local(planes_kernel, [(N_Y, PLANE, 2 * WIDTH)], "planes")(line)
    side0 = a2a(planes, axis_index_groups=along_y)
    side1 = send(side0, cores)
    return back_end(host, me, queries, keys, values, side0, side1, out_weight)


def back_end(host, me, queries, keys, values, side0, side1, out_weight):
    info = jnp.stack([host, me]).astype(jnp.int32)

    def part(steps, *added, queries=queries):
        return attend(steps, info, queries, keys, values, side0, side1, out_weight, added)

    def shift(x, step):
        return lax.ppermute(x, "head", [(i, (i + step) % N_HEAD) for i in range(N_HEAD)])

    own, right, far, left = range(N_HEAD)
    a, b = part(((far, 0), (far, 1)))
    via_right, via_left = shift(a, 1), shift(b, -1)
    a, b = part(((right, 1), (left, 0)))
    held, a, b = lax.optimization_barrier((queries, a, b))
    left1, right0 = shift(a, 1), shift(b, -1)
    a, b = part(((right, 0), (left, 1)), via_right, via_left, queries=held)
    held, a, b = lax.optimization_barrier((queries, a, b))
    left0, right1 = shift(a, 1), shift(b, -1)
    a, b = part(((own, 0), (own, 1)), right0, left1, queries=held)
    own, received = [jnp.concatenate(x, 0).astype(jnp.float32) for x in ((a, b), (left0, right1))]
    return (own + received).astype(jnp.bfloat16)


def solution(mesh):
    placed = (P("hst", "head"), P("hst", "head"), P("hst", "head"), P("hst", None), P("head", None))
    return jax.shard_map(
        on_device, mesh=mesh, in_specs=placed, out_specs=P(("hst", "head"), None), check_vma=False
    )
```

```python
import functools

import jax
import jax.numpy as jnp
import numpy as np
from jax import lax
from jax.experimental import pallas as pl
from jax.experimental.pallas import tpu as pltpu
from jax.sharding import PartitionSpec as P

HEAD_SIZE = 128
GROUP = 4
HEADS = 2
ANCHOR_ROWS = 128
BLOCK = 512
QUARTER = 128
STRIP = 64
ROWS = GROUP * QUARTER
N_Y, N_Z, N_CORE, N_HEAD = 4, 8, 2, 4
PASSING = 64
WIDTH = HEADS * HEAD_SIZE
SLICE = ANCHOR_ROWS // N_Y
LINE = N_Z * PASSING
PLANE = LINE + SLICE
CUT = PLANE // 2
D = 4096
FACTOR = float(HEAD_SIZE**-0.5 * np.log2(np.e))
NEG = -1e30
LIMIT = float(2.0**110)


def scores_of(q, k):
    return lax.dot_general(q, k, (((1,), (1,)), ((), ())), preferred_element_type=jnp.float32) * FACTOR


def with_ones(v, seen):
    return jnp.concatenate([jnp.where(seen, v, 0), jnp.where(seen, jnp.ones_like(v), 0)], 1)


def weigh(s, m, v):
    return jnp.dot(jnp.exp2(s - m).astype(jnp.bfloat16), v, preferred_element_type=jnp.float32)


def columns(i):
    return pl.ds(i * HEAD_SIZE if isinstance(i, int) else pl.multiple_of(i * HEAD_SIZE, HEAD_SIZE), HEAD_SIZE)


def near_kernel(q_ref, k_ref, v_ref, out_ref):
    def fold(i, carry):
        h, quarter = i // N_HEAD, i % N_HEAD
        rows = pl.ds(pl.multiple_of(quarter * QUARTER, QUARTER), QUARTER)
        q = jnp.concatenate([q_ref[rows, columns(h * GROUP + g)] for g in range(GROUP)], 0)
        v = v_ref[:, columns(h)]
        row = lax.broadcasted_iota(jnp.int32, (QUARTER, BLOCK), 0) + quarter * QUARTER
        col = lax.broadcasted_iota(jnp.int32, (QUARTER, BLOCK), 1)
        unseen = jnp.concatenate([jnp.where(col <= row, 0.0, NEG)] * GROUP, 0)
        s = scores_of(q, k_ref[:, columns(h)]) + unseen
        m = jnp.max(s, axis=1, keepdims=True)
        x = weigh(s, m, jnp.concatenate([v, jnp.ones_like(v)], 1))
        lane = lax.broadcasted_iota(jnp.int32, x.shape, 1)
        x = jnp.where(lane < HEAD_SIZE + HEAD_SIZE // 2, x, m)
        for g in range(GROUP):
            out_ref[h * GROUP + g, rows] = x[g * QUARTER : (g + 1) * QUARTER]
        return carry

    lax.fori_loop(0, HEADS * N_HEAD, fold, 0)


def near(queries, keys, values):
    shape = jax.ShapeDtypeStruct((HEADS * GROUP, BLOCK, 2 * HEAD_SIZE), jnp.float32)
    return pl.pallas_call(
        near_kernel,
        out_shape=shape,
        compiler_params=pltpu.CompilerParams(vmem_limit_bytes=24 << 20),
        name="near",
    )(queries, keys, values)


PIECES = ((0, 0, LINE, 0), (1, 3, LINE, 0), (2, 1, LINE, 0), (3, 2, CUT, 0), (4, 2, LINE - CUT, CUT))


def attend_kernel(steps, info, q_hbm, near_hbm, weight_hbm, *refs):
    side0, side1, refs = refs[: len(PIECES)], refs[len(PIECES) : 2 * len(PIECES)], refs[2 * len(PIECES) :]
    *added, out_a, out_b, acc_ref, q_ref, near_ref, anchor_ref, attended_ref, weight, sems = refs
    host, me = info[0], info[1]
    loads = [pltpu.make_async_copy(weight_hbm, weight, sems.at[0])]
    for i, (step, strip) in enumerate(steps):
        rows = pl.ds(pl.multiple_of((me + step) % N_HEAD * QUARTER + strip * STRIP, STRIP), STRIP)
        loads.append(pltpu.make_async_copy(q_hbm.at[rows], q_ref.at[i], sems.at[1 + i]))
        loads.append(pltpu.make_async_copy(near_hbm.at[:, rows], near_ref.at[:, pl.ds(i * STRIP, STRIP)], sems.at[3 + i]))
    for load in loads[1:] + loads[:1]:
        load.start()
    chip, core = host // N_CORE, host % N_CORE
    here = chip // N_Z
    for i, j in enumerate((0, 1, 2, 4)):
        start = LINE - CUT if j == 4 else LINE
        x, y = [side[j][start : start + SLICE] for side in (side0, side1)]
        anchor_ref[i * SLICE : (i + 1) * SLICE] = jnp.where(core == 0, x, y)
    for load in loads[1:]:
        load.wait()

    def queries(h, g):
        return [q_ref[i, :, columns(h * GROUP + g)] for i in range(2)]

    def seen_in(piece, other):
        _, step, size, start = piece
        before = chip + other * core - (here + step) % N_Y * N_Z
        return jnp.clip(before * PASSING - start, 0, size)

    def keys(side, piece, h):
        return side[piece[0]][: piece[2], columns(h)]

    def values(side, piece, h, other):
        size = piece[2]
        seen = lax.broadcasted_iota(jnp.int32, (size, HEAD_SIZE), 0) < seen_in(piece, other)
        return with_ones(side[piece[0]][:size, columns(HEADS + h)], seen)

    def anchor(h):
        v = anchor_ref[:, columns(HEADS + h)]
        return anchor_ref[:, columns(h)], jnp.concatenate([v, jnp.ones_like(v)], 1)

    heads = []
    for h in range(HEADS):
        q = jnp.concatenate([x for g in range(GROUP) for x in queries(h, g)], 0)
        acc_ref[h] = jnp.concatenate([near_ref[h * GROUP + g] for g in range(GROUP)], 0)
        heads.append((q, acc_ref[h, :, 2 * HEAD_SIZE - 1 :]))

    @pl.when(host > 0)
    def _():
        for other, side in enumerate((side0, side1)):
            for h, (q, m) in enumerate(heads):
                k = [keys(side, piece, h) for piece in PIECES]
                v = [values(side, piece, h, other) for piece in PIECES]
                if other == 0:
                    k, v = [x + [y] for x, y in zip((k, v), anchor(h))]
                acc_ref[h] += weigh(scores_of(q, jnp.concatenate(k, 0)), m, jnp.concatenate(v, 0))

    sums = slice(HEAD_SIZE, HEAD_SIZE + HEAD_SIZE // 2)
    worst = jnp.max(jnp.where(acc_ref[:, :, sums] < LIMIT, 0.0, 1.0))

    @pl.when(worst > 0)
    def _():
        def again(i, carry):
            h, g = i // GROUP, i % GROUP
            q = jnp.concatenate(queries(h, g), 0)
            acc = near_ref[i]
            old = acc[:, 2 * HEAD_SIZE - 1 :]
            k, v = anchor(h)
            chunks = [(k, v, ANCHOR_ROWS)] + [
                (keys(side, piece, h), values(side, piece, h, other), seen_in(piece, other))
                for other, side in enumerate((side0, side1))
                for piece in PIECES
            ]
            for k, v, count in chunks:
                s = scores_of(q, k)
                s = jnp.where(lax.broadcasted_iota(jnp.int32, s.shape, 1) < count, s, NEG)
                m = jnp.maximum(old, jnp.max(s, axis=1, keepdims=True))
                acc = acc * jnp.exp2(old - m) + weigh(s, m, v)
                old = m
            acc_ref[h, pl.ds(pl.multiple_of(g * QUARTER, QUARTER), QUARTER)] = acc
            return carry

        lax.fori_loop(0, HEADS * GROUP, again, 0)

    outs = [acc_ref[h, :, :HEAD_SIZE] / acc_ref[h, :, HEAD_SIZE : HEAD_SIZE + 1] for h in range(HEADS)]
    attended_ref[...] = jnp.concatenate(
        [o[g * QUARTER : (g + 1) * QUARTER].astype(jnp.bfloat16) for o in outs for g in range(GROUP)], 1
    )
    loads[0].wait()
    piece = 1024

    def project(i, carry):
        cut = pl.ds(pl.multiple_of(i * piece, piece), piece)
        x = jnp.dot(attended_ref[...], weight[:, cut], preferred_element_type=jnp.float32)
        for j, out in enumerate((out_a, out_b)):
            strip = x[j * STRIP : (j + 1) * STRIP]
            for ref in added[j::2]:
                strip = strip + ref[:, cut].astype(jnp.float32)
            out[:, cut] = strip.astype(jnp.bfloat16)
        return carry

    lax.fori_loop(0, D // piece, project, 0)


def attend(steps, info, queries, near_part, weight, sides, added):
    width = HEADS * GROUP * HEAD_SIZE
    resident, anywhere = pl.BlockSpec(memory_space=pltpu.VMEM), pl.BlockSpec(memory_space=pl.ANY)
    return pl.pallas_call(
        functools.partial(attend_kernel, steps),
        out_shape=[jax.ShapeDtypeStruct((STRIP, D), jnp.bfloat16)] * 2,
        in_specs=[pl.BlockSpec(memory_space=pltpu.SMEM)] + [anywhere] * 3 + [resident] * (len(sides) + len(added)),
        out_specs=[resident] * 2,
        scratch_shapes=[
            pltpu.VMEM((HEADS, ROWS, 2 * HEAD_SIZE), jnp.float32),
            pltpu.VMEM((2, STRIP, width), jnp.bfloat16),
            pltpu.VMEM((HEADS * GROUP, QUARTER, 2 * HEAD_SIZE), jnp.float32),
            pltpu.VMEM((ANCHOR_ROWS, 2 * WIDTH), jnp.bfloat16),
            pltpu.VMEM((QUARTER, width), jnp.bfloat16),
            pltpu.VMEM((width, D), jnp.bfloat16),
            pltpu.SemaphoreType.DMA((5,)),
        ],
        compiler_params=pltpu.CompilerParams(vmem_limit_bytes=40 << 20),
        name="attend",
    )(info, queries, near_part, weight, *sides, *added)


def slices_kernel(k_hbm, v_hbm, *refs):
    *outs, sem = refs
    copies = [
        pltpu.make_async_copy(x.at[pl.ds(i * SLICE, SLICE)], out.at[:, pl.ds(j * WIDTH, WIDTH)], sem.at[i, j])
        for i, out in enumerate(outs)
        for j, x in enumerate((k_hbm, v_hbm))
    ]
    for copy in copies:
        copy.start()
    for copy in copies:
        copy.wait()


def slices_of(keys, values):
    return pl.pallas_call(
        slices_kernel,
        out_shape=[jax.ShapeDtypeStruct((SLICE, 2 * WIDTH), jnp.bfloat16)] * N_Y,
        in_specs=[pl.BlockSpec(memory_space=pl.ANY)] * 2,
        out_specs=[pl.BlockSpec(memory_space=pltpu.VMEM)] * N_Y,
        scratch_shapes=[pltpu.SemaphoreType.DMA((N_Y, 2))],
        name="slices",
    )(keys, values)


def pick_kernel(rows_ref, k_hbm, v_hbm, out_ref, k_buf, v_buf, sem):
    pairs = ((k_hbm, k_buf), (v_hbm, v_buf))
    copies = [pltpu.make_async_copy(x, buf, sem.at[i]) for i, (x, buf) in enumerate(pairs)]
    for copy in copies:
        copy.start()
    one_hot = lax.broadcasted_iota(jnp.int32, (BLOCK, PASSING), 0) == rows_ref[...]
    one_hot = jnp.where(one_hot, 1.0, 0.0).astype(jnp.bfloat16)
    for i, (copy, (_, buf)) in enumerate(zip(copies, pairs)):
        copy.wait()
        out_ref[:, i * WIDTH : (i + 1) * WIDTH] = lax.dot_general(
            one_hot, buf[...], (((0,), (0,)), ((), ())), preferred_element_type=jnp.float32
        ).astype(jnp.bfloat16)


def pick(rows, keys, values):
    vmem, anywhere = pl.BlockSpec(memory_space=pltpu.VMEM), pl.BlockSpec(memory_space=pl.ANY)
    return pl.pallas_call(
        pick_kernel,
        out_shape=jax.ShapeDtypeStruct((PASSING, 2 * WIDTH), jnp.bfloat16),
        in_specs=[vmem, anywhere, anywhere],
        out_specs=vmem,
        scratch_shapes=[pltpu.VMEM((BLOCK, WIDTH), jnp.bfloat16)] * 2 + [pltpu.SemaphoreType.DMA((2,))],
        name="pick",
    )(rows, keys, values)


def units_kernel(host, picked_ref, own_ref, *refs):
    *slices, out_ref = refs
    piece = jnp.where(host[0] == 0, own_ref[...], jnp.zeros(own_ref.shape, own_ref.dtype))
    for ref in slices:
        piece = piece + ref[...]
    for z in range(N_Z):
        out_ref[z, :PASSING] = picked_ref[...]
        out_ref[z, PASSING:] = piece


def plane_kernel(line_ref, out_ref):
    for z in range(N_Z):
        out_ref[z * PASSING : (z + 1) * PASSING] = line_ref[z, :PASSING]
    out_ref[LINE:] = line_ref[0, PASSING:]


def local(kernel, shapes, name):
    shapes = [jax.ShapeDtypeStruct(shape, jnp.bfloat16) for shape in shapes]
    return pl.pallas_call(kernel, out_shape=shapes, name=name)


def units_of(host, picked, own, slices):
    vmem = pl.BlockSpec(memory_space=pltpu.VMEM)
    return pl.pallas_call(
        units_kernel,
        out_shape=jax.ShapeDtypeStruct((N_Z, PASSING + SLICE, 2 * WIDTH), jnp.bfloat16),
        in_specs=[pl.BlockSpec(memory_space=pltpu.SMEM)] + [vmem] * (2 + len(slices)),
        out_specs=vmem,
        name="units",
    )(host.reshape(1), picked, own, *slices)


def place(y, z, core):
    return ((y % N_Y) * N_Z + z % N_Z) * N_CORE + core


def send(x, pairs):
    return lax.ppermute(x, "hst", pairs)


def on_device(queries, keys, values, pass_rows, out_weight):
    host = lax.axis_index("hst")
    me = lax.axis_index("head")
    along_z = [[place(y, z, c) for z in range(N_Z)] for y in range(N_Y) for c in range(N_CORE)]
    a2a = functools.partial(lax.all_to_all, axis_name="hst", split_axis=0, concat_axis=0, tiled=True)
    cores = [(h, h ^ 1) for h in range(N_Y * N_Z * N_CORE)]
    first, *slices = slices_of(keys, values)
    slices = [send(x, [(0, place(y + 1, 0, 0))]) for y, x in enumerate(slices)]
    units = units_of(host, pick(pass_rows, keys, values), first, slices)
    line = a2a(units, axis_index_groups=along_z)
    (plane,) = local(plane_kernel, [(PLANE, 2 * WIDTH)], "plane")(line)

    def along_y(x, step):
        places = [(y, z, c) for y in range(N_Y) for z in range(N_Z) for c in range(N_CORE)]
        return send(x, [(place(y, z, c), place(y + step, z, c)) for y, z, c in places])

    below, above = along_y(plane, 1), along_y(plane, -1)
    early, _ = lax.optimization_barrier((queries, plane))
    below, above, near_part = lax.optimization_barrier((below, above, near(early, keys, values)))
    side0 = [plane, below, above, along_y(below[:CUT], 1), along_y(above[CUT:], -1)]
    side1 = [send(x, cores) for x in side0]
    return back_end(host, me, queries, near_part, side0 + side1, out_weight)


def back_end(host, me, queries, near_part, sides, out_weight):
    info = jnp.stack([host, me]).astype(jnp.int32)

    def part(steps, *added, queries=queries):
        return attend(steps, info, queries, near_part, out_weight, sides, added)

    def shift(x, step):
        return lax.ppermute(x, "head", [(i, (i + step) % N_HEAD) for i in range(N_HEAD)])

    own, right, far, left = range(N_HEAD)
    a, b = part(((far, 0), (far, 1)))
    via_right, via_left = shift(a, 1), shift(b, -1)
    a, b = part(((right, 1), (left, 0)))
    held, a, b = lax.optimization_barrier((queries, a, b))
    left1, right0 = shift(a, 1), shift(b, -1)
    a, b = part(((right, 0), (left, 1)), via_right, via_left, queries=held)
    held, a, b = lax.optimization_barrier((queries, a, b))
    left0, right1 = shift(a, 1), shift(b, -1)
    a, b = part(((own, 0), (own, 1)), right0, left1, queries=held)
    own, received = [jnp.concatenate(x, 0).astype(jnp.float32) for x in ((a, b), (left0, right1))]
    return (own + received).astype(jnp.bfloat16)


def solution(mesh):
    placed = (P("hst", "head"), P("hst", "head"), P("hst", "head"), P("hst", None), P("head", None))
    return jax.shard_map(
        on_device, mesh=mesh, in_specs=placed, out_specs=P(("hst", "head"), None), check_vma=False
    )
```

```python
import functools

import jax
import jax.numpy as jnp
import numpy as np
from jax import lax
from jax.experimental import pallas as pl
from jax.experimental.pallas import tpu as pltpu
from jax.sharding import PartitionSpec as P

HEAD_SIZE = 128
GROUP = 4
HEADS = 2
ANCHOR_ROWS = 128
BLOCK = 512
QUARTER = 128
STRIP = 64
ROWS = GROUP * QUARTER
N_Y, N_Z, N_CORE, N_HEAD = 4, 8, 2, 4
PASSING = 64
WIDTH = HEADS * HEAD_SIZE
SLICE = ANCHOR_ROWS // N_Y
LINE = N_Z * PASSING
PLANE = LINE + SLICE
CUT = PLANE // 2
D = 4096
FACTOR = float(HEAD_SIZE**-0.5 * np.log2(np.e))
NEG = -1e30
LIMIT = float(2.0**110)


def scores_of(q, k):
    return lax.dot_general(q, k, (((1,), (1,)), ((), ())), preferred_element_type=jnp.float32) * FACTOR


def with_ones(v, seen):
    return jnp.concatenate([jnp.where(seen, v, 0), jnp.where(seen, jnp.ones_like(v), 0)], 1)


def weigh(s, m, v):
    return jnp.dot(jnp.exp2(s - m).astype(jnp.bfloat16), v, preferred_element_type=jnp.float32)


def columns(i):
    return pl.ds(i * HEAD_SIZE if isinstance(i, int) else pl.multiple_of(i * HEAD_SIZE, HEAD_SIZE), HEAD_SIZE)


def near_kernel(q_ref, k_ref, v_ref, out_hbm, out_ref, sems):
    def store(i):
        h, quarter = i // N_HEAD, i % N_HEAD
        rows = pl.ds(pl.multiple_of(quarter * QUARTER, QUARTER), QUARTER)
        at = (pl.ds(h * GROUP, GROUP), rows)
        return h, quarter, rows, pltpu.make_async_copy(out_ref.at[at], out_hbm.at[at], sems.at[i])

    def fold(i, carry):
        h, quarter, rows, copy = store(i)
        q = jnp.concatenate([q_ref[rows, columns(h * GROUP + g)] for g in range(GROUP)], 0)
        v = v_ref[:, columns(h)]
        row = lax.broadcasted_iota(jnp.int32, (QUARTER, BLOCK), 0) + quarter * QUARTER
        col = lax.broadcasted_iota(jnp.int32, (QUARTER, BLOCK), 1)
        unseen = jnp.concatenate([jnp.where(col <= row, 0.0, NEG)] * GROUP, 0)
        s = scores_of(q, k_ref[:, columns(h)]) + unseen
        m = jnp.max(s, axis=1, keepdims=True)
        x = weigh(s, m, jnp.concatenate([v, jnp.ones_like(v)], 1))
        lane = lax.broadcasted_iota(jnp.int32, x.shape, 1)
        x = jnp.where(lane < HEAD_SIZE + HEAD_SIZE // 2, x, m)
        for g in range(GROUP):
            out_ref[h * GROUP + g, rows] = x[g * QUARTER : (g + 1) * QUARTER]
        copy.start()
        return carry

    def finish(i, carry):
        store(i)[-1].wait()
        return carry

    lax.fori_loop(0, HEADS * N_HEAD, fold, 0)
    lax.fori_loop(0, HEADS * N_HEAD, finish, 0)


def near(queries, keys, values):
    shape = jax.ShapeDtypeStruct((HEADS * GROUP, BLOCK, 2 * HEAD_SIZE), jnp.float32)
    vmem = pl.BlockSpec(memory_space=pltpu.VMEM)
    return pl.pallas_call(
        near_kernel,
        out_shape=shape,
        in_specs=[vmem] * 3,
        out_specs=pl.BlockSpec(memory_space=pltpu.HBM),
        scratch_shapes=[pltpu.VMEM(shape.shape, shape.dtype), pltpu.SemaphoreType.DMA((HEADS * N_HEAD,))],
        compiler_params=pltpu.CompilerParams(vmem_limit_bytes=16 << 20),
        name="near",
    )(queries, keys, values)


PIECES = ((0, 0, LINE, 0), (1, 3, LINE, 0), (2, 1, LINE, 0), (3, 2, CUT, 0), (4, 2, LINE - CUT, CUT))


EARLY = 3


def queries(q_ref, h, g):
    return [q_ref[i, :, columns(h * GROUP + g)] for i in range(2)]


def seen_in(piece, host, other):
    _, step, size, start = piece
    chip = host // N_CORE
    before = chip + other * (host % N_CORE) - (chip // N_Z + step) % N_Y * N_Z
    return jnp.clip(before * PASSING - start, 0, size)


def passing(side, pieces, h, host, other):
    k = [side[piece[0]][: piece[2], columns(h)] for piece in pieces]
    v = []
    for piece in pieces:
        seen = lax.broadcasted_iota(jnp.int32, (piece[2], HEAD_SIZE), 0) < seen_in(piece, host, other)
        v.append(with_ones(side[piece[0]][: piece[2], columns(HEADS + h)], seen))
    return k, v


def strip_loads(steps, me, q_hbm, near_hbm, q_ref, near_ref, sems):
    q_loads, near_loads = [], []
    for i, (step, strip) in enumerate(steps):
        rows = pl.ds(pl.multiple_of((me + step) % N_HEAD * QUARTER + strip * STRIP, STRIP), STRIP)
        q_loads.append(pltpu.make_async_copy(q_hbm.at[rows], q_ref.at[i], sems.at[i]))
        near_loads.append(
            pltpu.make_async_copy(near_hbm.at[:, rows], near_ref.at[:, pl.ds(i * STRIP, STRIP)], sems.at[2 + i])
        )
    return q_loads, near_loads


def start_heads(q_ref, state, acc_ref):
    heads = []
    for h in range(HEADS):
        q = jnp.concatenate([x for g in range(GROUP) for x in queries(q_ref, h, g)], 0)
        acc_ref[h] = jnp.concatenate([state[h * GROUP + g] for g in range(GROUP)], 0)
        heads.append((q, acc_ref[h, :, 2 * HEAD_SIZE - 1 :]))
    return heads


def early_kernel(steps, info, q_hbm, near_hbm, *refs):
    side0, side1 = refs[:EARLY], refs[EARLY : 2 * EARLY]
    out_ref, acc_ref, q_ref, near_ref, sems = refs[2 * EARLY :]
    host, me = info[0], info[1]
    q_loads, near_loads = strip_loads(steps, me, q_hbm, near_hbm, q_ref, near_ref, sems)
    for copy in q_loads + near_loads:
        copy.start()
    for copy in q_loads + near_loads:
        copy.wait()
    heads = start_heads(q_ref, near_ref, acc_ref)

    @pl.when(host > 0)
    def _():
        for other, side in enumerate((side0, side1)):
            for h, (q, m) in enumerate(heads):
                k, v = passing(side, PIECES[:EARLY], h, host, other)
                acc_ref[h] += weigh(scores_of(q, jnp.concatenate(k, 0)), m, jnp.concatenate(v, 0))

    for h, (q, m) in enumerate(heads):
        lane = lax.broadcasted_iota(jnp.int32, (ROWS, 2 * HEAD_SIZE), 1)
        x = jnp.where(lane < HEAD_SIZE + HEAD_SIZE // 2, acc_ref[h], m)
        for g in range(GROUP):
            out_ref[h * GROUP + g] = x[g * QUARTER : (g + 1) * QUARTER]


def attend_early(steps, info, queries, near_part, side0, side1):
    width = HEADS * GROUP * HEAD_SIZE
    vmem, anywhere, hbm = [pl.BlockSpec(memory_space=x) for x in (pltpu.VMEM, pl.ANY, pltpu.HBM)]
    state = (HEADS * GROUP, QUARTER, 2 * HEAD_SIZE)
    return pl.pallas_call(
        functools.partial(early_kernel, steps),
        out_shape=jax.ShapeDtypeStruct(state, jnp.float32),
        in_specs=[pl.BlockSpec(memory_space=pltpu.SMEM), anywhere, hbm] + [vmem] * (2 * EARLY),
        out_specs=vmem,
        scratch_shapes=[
            pltpu.VMEM((HEADS, ROWS, 2 * HEAD_SIZE), jnp.float32),
            pltpu.VMEM((2, STRIP, width), jnp.bfloat16),
            pltpu.VMEM(state, jnp.float32),
            pltpu.SemaphoreType.DMA((4,)),
        ],
        compiler_params=pltpu.CompilerParams(vmem_limit_bytes=24 << 20),
        name="early",
    )(info, queries, near_part, *side0, *side1)


def attend_kernel(steps, early, info, q_hbm, near_hbm, weight_hbm, *refs):
    side0, side1, refs = refs[: len(PIECES)], refs[len(PIECES) : 2 * len(PIECES)], refs[2 * len(PIECES) :]
    *added, out_a, out_b, acc_ref, q_ref, near_ref, anchor_ref, attended_ref, weight, sems = refs
    state, added = (added[0], added[1:]) if early else (near_ref, added)
    host, me = info[0], info[1]
    load, near_load = strip_loads(steps, me, q_hbm, near_hbm, q_ref, near_ref, sems)
    last = pltpu.make_async_copy(weight_hbm, weight, sems.at[4])
    for copy in load + ([] if early else near_load) + [last]:
        copy.start()
    core = host % N_CORE
    for i, j in enumerate((0, 1, 2, 4)):
        start = LINE - CUT if j == 4 else LINE
        x, y = [side[j][start : start + SLICE] for side in (side0, side1)]
        anchor_ref[i * SLICE : (i + 1) * SLICE] = jnp.where(core == 0, x, y)
    for copy in load + ([] if early else near_load):
        copy.wait()

    def anchor(h):
        v = anchor_ref[:, columns(HEADS + h)]
        return anchor_ref[:, columns(h)], jnp.concatenate([v, jnp.ones_like(v)], 1)

    heads = start_heads(q_ref, state, acc_ref)

    @pl.when(host > 0)
    def _():
        for other, side in enumerate((side0, side1)):
            for h, (q, m) in enumerate(heads):
                k, v = passing(side, PIECES[EARLY:] if early else PIECES, h, host, other)
                if other == 0:
                    k, v = [x + [y] for x, y in zip((k, v), anchor(h))]
                acc_ref[h] += weigh(scores_of(q, jnp.concatenate(k, 0)), m, jnp.concatenate(v, 0))

    sums = slice(HEAD_SIZE, HEAD_SIZE + HEAD_SIZE // 2)
    worst = jnp.max(jnp.where(acc_ref[:, :, sums] < LIMIT, 0.0, 1.0))

    @pl.when(worst > 0)
    def _():
        if early:
            for copy in near_load:
                copy.start()
            for copy in near_load:
                copy.wait()

        def again(i, carry):
            h, g = i // GROUP, i % GROUP
            q = jnp.concatenate(queries(q_ref, h, g), 0)
            acc = near_ref[i]
            old = acc[:, 2 * HEAD_SIZE - 1 :]
            k, v = anchor(h)
            chunks = [(k, v, ANCHOR_ROWS)] + [
                (*(x[0] for x in passing(side, [piece], h, host, other)), seen_in(piece, host, other))
                for other, side in enumerate((side0, side1))
                for piece in PIECES
            ]
            for k, v, count in chunks:
                s = scores_of(q, k)
                s = jnp.where(lax.broadcasted_iota(jnp.int32, s.shape, 1) < count, s, NEG)
                m = jnp.maximum(old, jnp.max(s, axis=1, keepdims=True))
                acc = acc * jnp.exp2(old - m) + weigh(s, m, v)
                old = m
            acc_ref[h, pl.ds(pl.multiple_of(g * QUARTER, QUARTER), QUARTER)] = acc
            return carry

        lax.fori_loop(0, HEADS * GROUP, again, 0)

    outs = [acc_ref[h, :, :HEAD_SIZE] / acc_ref[h, :, HEAD_SIZE : HEAD_SIZE + 1] for h in range(HEADS)]
    attended_ref[...] = jnp.concatenate(
        [o[g * QUARTER : (g + 1) * QUARTER].astype(jnp.bfloat16) for o in outs for g in range(GROUP)], 1
    )
    last.wait()
    piece = 1024

    def project(i, carry):
        cut = pl.ds(pl.multiple_of(i * piece, piece), piece)
        x = jnp.dot(attended_ref[...], weight[:, cut], preferred_element_type=jnp.float32)
        for j, out in enumerate((out_a, out_b)):
            strip = x[j * STRIP : (j + 1) * STRIP]
            for ref in added[j::2]:
                strip = strip + ref[:, cut].astype(jnp.float32)
            out[:, cut] = strip.astype(jnp.bfloat16)
        return carry

    lax.fori_loop(0, D // piece, project, 0)


def attend(steps, info, queries, near_part, weight, sides, added, early):
    width = HEADS * GROUP * HEAD_SIZE
    resident, anywhere, hbm = [pl.BlockSpec(memory_space=x) for x in (pltpu.VMEM, pl.ANY, pltpu.HBM)]
    return pl.pallas_call(
        functools.partial(attend_kernel, steps, early),
        out_shape=[jax.ShapeDtypeStruct((STRIP, D), jnp.bfloat16)] * 2,
        in_specs=[pl.BlockSpec(memory_space=pltpu.SMEM), anywhere, hbm, anywhere]
        + [resident] * (len(sides) + len(added)),
        out_specs=[resident] * 2,
        scratch_shapes=[
            pltpu.VMEM((HEADS, ROWS, 2 * HEAD_SIZE), jnp.float32),
            pltpu.VMEM((2, STRIP, width), jnp.bfloat16),
            pltpu.VMEM((HEADS * GROUP, QUARTER, 2 * HEAD_SIZE), jnp.float32),
            pltpu.VMEM((ANCHOR_ROWS, 2 * WIDTH), jnp.bfloat16),
            pltpu.VMEM((QUARTER, width), jnp.bfloat16),
            pltpu.VMEM((width, D), jnp.bfloat16),
            pltpu.SemaphoreType.DMA((5,)),
        ],
        compiler_params=pltpu.CompilerParams(vmem_limit_bytes=30 << 20),
        name="attend",
    )(info, queries, near_part, weight, *sides, *added)


def slices_kernel(k_hbm, v_hbm, *refs):
    *outs, sem = refs
    copies = [
        pltpu.make_async_copy(x.at[pl.ds(i * SLICE, SLICE)], out.at[:, pl.ds(j * WIDTH, WIDTH)], sem.at[i, j])
        for i, out in enumerate(outs)
        for j, x in enumerate((k_hbm, v_hbm))
    ]
    for copy in copies:
        copy.start()
    for copy in copies:
        copy.wait()


def slices_of(keys, values):
    return pl.pallas_call(
        slices_kernel,
        out_shape=[jax.ShapeDtypeStruct((SLICE, 2 * WIDTH), jnp.bfloat16)] * N_Y,
        in_specs=[pl.BlockSpec(memory_space=pl.ANY)] * 2,
        out_specs=[pl.BlockSpec(memory_space=pltpu.VMEM)] * N_Y,
        scratch_shapes=[pltpu.SemaphoreType.DMA((N_Y, 2))],
        name="slices",
    )(keys, values)


def pick_kernel(rows_ref, k_hbm, v_hbm, out_ref, k_buf, v_buf, sem):
    pairs = ((k_hbm, k_buf), (v_hbm, v_buf))
    copies = [pltpu.make_async_copy(x, buf, sem.at[i]) for i, (x, buf) in enumerate(pairs)]
    for copy in copies:
        copy.start()
    one_hot = lax.broadcasted_iota(jnp.int32, (BLOCK, PASSING), 0) == rows_ref[...]
    one_hot = jnp.where(one_hot, 1.0, 0.0).astype(jnp.bfloat16)
    for i, (copy, (_, buf)) in enumerate(zip(copies, pairs)):
        copy.wait()
        out_ref[:, i * WIDTH : (i + 1) * WIDTH] = lax.dot_general(
            one_hot, buf[...], (((0,), (0,)), ((), ())), preferred_element_type=jnp.float32
        ).astype(jnp.bfloat16)


def pick(rows, keys, values):
    vmem, anywhere = pl.BlockSpec(memory_space=pltpu.VMEM), pl.BlockSpec(memory_space=pl.ANY)
    return pl.pallas_call(
        pick_kernel,
        out_shape=jax.ShapeDtypeStruct((PASSING, 2 * WIDTH), jnp.bfloat16),
        in_specs=[vmem, anywhere, anywhere],
        out_specs=vmem,
        scratch_shapes=[pltpu.VMEM((BLOCK, WIDTH), jnp.bfloat16)] * 2 + [pltpu.SemaphoreType.DMA((2,))],
        name="pick",
    )(rows, keys, values)


def units_kernel(host, picked_ref, own_ref, *refs):
    *slices, out_ref = refs
    piece = jnp.where(host[0] == 0, own_ref[...], jnp.zeros(own_ref.shape, own_ref.dtype))
    for ref in slices:
        piece = piece + ref[...]
    for z in range(N_Z):
        out_ref[z, :PASSING] = picked_ref[...]
        out_ref[z, PASSING:] = piece


def plane_kernel(line_ref, out_ref):
    for z in range(N_Z):
        out_ref[z * PASSING : (z + 1) * PASSING] = line_ref[z, :PASSING]
    out_ref[LINE:] = line_ref[0, PASSING:]


def local(kernel, shapes, name):
    shapes = [jax.ShapeDtypeStruct(shape, jnp.bfloat16) for shape in shapes]
    return pl.pallas_call(kernel, out_shape=shapes, name=name)


def units_of(host, picked, own, slices):
    vmem = pl.BlockSpec(memory_space=pltpu.VMEM)
    return pl.pallas_call(
        units_kernel,
        out_shape=jax.ShapeDtypeStruct((N_Z, PASSING + SLICE, 2 * WIDTH), jnp.bfloat16),
        in_specs=[pl.BlockSpec(memory_space=pltpu.SMEM)] + [vmem] * (2 + len(slices)),
        out_specs=vmem,
        name="units",
    )(host.reshape(1), picked, own, *slices)


def place(y, z, core):
    return ((y % N_Y) * N_Z + z % N_Z) * N_CORE + core


def send(x, pairs):
    return lax.ppermute(x, "hst", pairs)


def on_device(queries, keys, values, pass_rows, out_weight):
    host = lax.axis_index("hst")
    me = lax.axis_index("head")
    along_z = [[place(y, z, c) for z in range(N_Z)] for y in range(N_Y) for c in range(N_CORE)]
    a2a = functools.partial(lax.all_to_all, axis_name="hst", split_axis=0, concat_axis=0, tiled=True)
    cores = [(h, h ^ 1) for h in range(N_Y * N_Z * N_CORE)]
    first, *slices = slices_of(keys, values)
    slices = [send(x, [(0, place(y + 1, 0, 0))]) for y, x in enumerate(slices)]
    units = units_of(host, pick(pass_rows, keys, values), first, slices)
    line = a2a(units, axis_index_groups=along_z)
    (plane,) = local(plane_kernel, [(PLANE, 2 * WIDTH)], "plane")(line)

    def along_y(x, step):
        places = [(y, z, c) for y in range(N_Y) for z in range(N_Z) for c in range(N_CORE)]
        return send(x, [(place(y, z, c), place(y + step, z, c)) for y, z, c in places])

    below, above = along_y(plane, 1), along_y(plane, -1)
    held, _ = lax.optimization_barrier((queries, plane))
    below, above, near_part = lax.optimization_barrier((below, above, near(held, keys, values)))
    side0 = [plane, below, above]
    side1 = [send(x, cores) for x in side0]
    halves = [along_y(below[:CUT], 1), along_y(above[CUT:], -1)]
    info = jnp.stack([host, me]).astype(jnp.int32)
    own, right, far, left = range(N_HEAD)
    first = ((far, 0), (far, 1))
    *halves, state = lax.optimization_barrier(
        (*halves, attend_early(first, info, queries, near_part, side0, side1))
    )
    sides = side0 + halves + side1 + [send(x, cores) for x in halves]

    def part(steps, *added, queries=queries, early=False):
        return attend(steps, info, queries, near_part, out_weight, sides, added, early)

    def shift(x, step):
        return lax.ppermute(x, "head", [(i, (i + step) % N_HEAD) for i in range(N_HEAD)])

    a, b = part(first, state, early=True)
    via_right, via_left = shift(a, 1), shift(b, -1)
    a, b = part(((right, 1), (left, 0)))
    held, a, b = lax.optimization_barrier((queries, a, b))
    left1, right0 = shift(a, 1), shift(b, -1)
    a, b = part(((right, 0), (left, 1)), via_right, via_left, queries=held)
    held, a, b = lax.optimization_barrier((queries, a, b))
    left0, right1 = shift(a, 1), shift(b, -1)
    a, b = part(((own, 0), (own, 1)), right0, left1, queries=held)
    own, received = [jnp.concatenate(x, 0).astype(jnp.float32) for x in ((a, b), (left0, right1))]
    return (own + received).astype(jnp.bfloat16)


def solution(mesh):
    placed = (P("hst", "head"), P("hst", "head"), P("hst", "head"), P("hst", None), P("head", None))
    return jax.shard_map(
        on_device, mesh=mesh, in_specs=placed, out_specs=P(("hst", "head"), None), check_vma=False
    )
```

```python
import functools

import jax
import jax.numpy as jnp
import numpy as np
from jax import lax
from jax.experimental import pallas as pl
from jax.experimental.pallas import tpu as pltpu
from jax.sharding import PartitionSpec as P

HEAD_SIZE = 128
GROUP = 4
HEADS = 2
ANCHOR_ROWS = 128
BLOCK = 512
QUARTER = 128
STRIP = 64
ROWS = GROUP * QUARTER
N_Y, N_Z, N_CORE, N_HEAD = 4, 8, 2, 4
PASSING = 64
WIDTH = HEADS * HEAD_SIZE
SLICE = ANCHOR_ROWS // N_Y
LINE = N_Z * PASSING
PLANE = LINE + SLICE
CUT = PLANE // 2
D = 4096
FACTOR = float(HEAD_SIZE**-0.5 * np.log2(np.e))
NEG = -1e30
LIMIT = float(2.0**110)


def in_hbm(*arrays):
    return [pltpu.with_memory_space_constraint(x, pltpu.HBM) for x in arrays]


def scores_of(q, k):
    return lax.dot_general(q, k, (((1,), (1,)), ((), ())), preferred_element_type=jnp.float32) * FACTOR


def with_ones(v, seen):
    return jnp.concatenate([jnp.where(seen, v, 0), jnp.where(seen, jnp.ones_like(v), 0)], 1)


def weigh(s, m, v):
    return jnp.dot(jnp.exp2(s - m).astype(jnp.bfloat16), v, preferred_element_type=jnp.float32)


def columns(i):
    return pl.ds(i * HEAD_SIZE if isinstance(i, int) else pl.multiple_of(i * HEAD_SIZE, HEAD_SIZE), HEAD_SIZE)


def near_kernel(q_ref, k_ref, v_ref, out_hbm, out_ref, sems):
    def store(i):
        h, quarter = i // N_HEAD, i % N_HEAD
        rows = pl.ds(pl.multiple_of(quarter * QUARTER, QUARTER), QUARTER)
        at = (pl.ds(h * GROUP, GROUP), rows)
        return h, quarter, rows, pltpu.make_async_copy(out_ref.at[at], out_hbm.at[at], sems.at[i])

    def fold(i, carry):
        h, quarter, rows, copy = store(i)
        q = jnp.concatenate([q_ref[rows, columns(h * GROUP + g)] for g in range(GROUP)], 0)
        v = v_ref[:, columns(h)]
        row = lax.broadcasted_iota(jnp.int32, (QUARTER, BLOCK), 0) + quarter * QUARTER
        col = lax.broadcasted_iota(jnp.int32, (QUARTER, BLOCK), 1)
        unseen = jnp.concatenate([jnp.where(col <= row, 0.0, NEG)] * GROUP, 0)
        s = scores_of(q, k_ref[:, columns(h)]) + unseen
        m = jnp.max(s, axis=1, keepdims=True)
        x = weigh(s, m, jnp.concatenate([v, jnp.ones_like(v)], 1))
        lane = lax.broadcasted_iota(jnp.int32, x.shape, 1)
        x = jnp.where(lane < HEAD_SIZE + HEAD_SIZE // 2, x, m)
        for g in range(GROUP):
            out_ref[h * GROUP + g, rows] = x[g * QUARTER : (g + 1) * QUARTER]
        copy.start()
        return carry

    def finish(i, carry):
        store(i)[-1].wait()
        return carry

    lax.fori_loop(0, HEADS * N_HEAD, fold, 0)
    lax.fori_loop(0, HEADS * N_HEAD, finish, 0)


def near(queries, keys, values):
    shape = pltpu.HBM((HEADS * GROUP, BLOCK, 2 * HEAD_SIZE), jnp.float32)
    vmem = pl.BlockSpec(memory_space=pltpu.VMEM)
    return pl.pallas_call(
        near_kernel,
        out_shape=shape,
        in_specs=[vmem] * 3,
        out_specs=pl.BlockSpec(memory_space=pltpu.HBM),
        scratch_shapes=[pltpu.VMEM(shape.shape, shape.dtype), pltpu.SemaphoreType.DMA((HEADS * N_HEAD,))],
        compiler_params=pltpu.CompilerParams(vmem_limit_bytes=16 << 20),
        name="near",
    )(queries, keys, values)


PIECES = ((0, 0, LINE, 0), (1, 3, LINE, 0), (2, 1, LINE, 0), (3, 2, CUT, 0), (4, 2, LINE - CUT, CUT))


EARLY = 3


def queries(q_ref, h, g):
    return [q_ref[i, :, columns(h * GROUP + g)] for i in range(2)]


def seen_in(piece, host, other):
    _, step, size, start = piece
    chip = host // N_CORE
    before = chip + other * (host % N_CORE) - (chip // N_Z + step) % N_Y * N_Z
    return jnp.clip(before * PASSING - start, 0, size)


def passing(side, pieces, h, host, other):
    k = [side[piece[0]][: piece[2], columns(h)] for piece in pieces]
    v = []
    for piece in pieces:
        seen = lax.broadcasted_iota(jnp.int32, (piece[2], HEAD_SIZE), 0) < seen_in(piece, host, other)
        v.append(with_ones(side[piece[0]][: piece[2], columns(HEADS + h)], seen))
    return k, v


def strip_loads(steps, me, q_hbm, near_hbm, q_ref, near_ref, sems):
    q_loads, near_loads = [], []
    for i, (step, strip) in enumerate(steps):
        rows = pl.ds(pl.multiple_of((me + step) % N_HEAD * QUARTER + strip * STRIP, STRIP), STRIP)
        q_loads.append(pltpu.make_async_copy(q_hbm.at[rows], q_ref.at[i], sems.at[i]))
        near_loads.append(
            pltpu.make_async_copy(near_hbm.at[:, rows], near_ref.at[:, pl.ds(i * STRIP, STRIP)], sems.at[2 + i])
        )
    return q_loads, near_loads


def start_heads(q_ref, state, acc_ref):
    heads = []
    for h in range(HEADS):
        q = jnp.concatenate([x for g in range(GROUP) for x in queries(q_ref, h, g)], 0)
        acc_ref[h] = jnp.concatenate([state[h * GROUP + g] for g in range(GROUP)], 0)
        heads.append((q, acc_ref[h, :, 2 * HEAD_SIZE - 1 :]))
    return heads


def early_kernel(steps, info, q_hbm, near_hbm, *refs):
    side0, side1 = refs[:EARLY], refs[EARLY : 2 * EARLY]
    out_ref, acc_ref, q_ref, near_ref, sems = refs[2 * EARLY :]
    host, me = info[0], info[1]
    q_loads, near_loads = strip_loads(steps, me, q_hbm, near_hbm, q_ref, near_ref, sems)
    for copy in q_loads + near_loads:
        copy.start()
    for copy in q_loads + near_loads:
        copy.wait()
    heads = start_heads(q_ref, near_ref, acc_ref)

    @pl.when(host > 0)
    def _():
        for other, side in enumerate((side0, side1)):
            for h, (q, m) in enumerate(heads):
                k, v = passing(side, PIECES[:EARLY], h, host, other)
                acc_ref[h] += weigh(scores_of(q, jnp.concatenate(k, 0)), m, jnp.concatenate(v, 0))

    for h, (q, m) in enumerate(heads):
        lane = lax.broadcasted_iota(jnp.int32, (ROWS, 2 * HEAD_SIZE), 1)
        x = jnp.where(lane < HEAD_SIZE + HEAD_SIZE // 2, acc_ref[h], m)
        for g in range(GROUP):
            out_ref[h * GROUP + g] = x[g * QUARTER : (g + 1) * QUARTER]


def attend_early(steps, info, queries, near_part, side0, side1):
    width = HEADS * GROUP * HEAD_SIZE
    vmem, anywhere, hbm = [pl.BlockSpec(memory_space=x) for x in (pltpu.VMEM, pl.ANY, pltpu.HBM)]
    state = (HEADS * GROUP, QUARTER, 2 * HEAD_SIZE)
    return pl.pallas_call(
        functools.partial(early_kernel, steps),
        out_shape=jax.ShapeDtypeStruct(state, jnp.float32),
        in_specs=[pl.BlockSpec(memory_space=pltpu.SMEM), anywhere, hbm] + [vmem] * (2 * EARLY),
        out_specs=vmem,
        scratch_shapes=[
            pltpu.VMEM((HEADS, ROWS, 2 * HEAD_SIZE), jnp.float32),
            pltpu.VMEM((2, STRIP, width), jnp.bfloat16),
            pltpu.VMEM(state, jnp.float32),
            pltpu.SemaphoreType.DMA((4,)),
        ],
        compiler_params=pltpu.CompilerParams(vmem_limit_bytes=24 << 20),
        name="early",
    )(info, *in_hbm(queries, near_part), *side0, *side1)


def attend_kernel(steps, early, info, q_hbm, near_hbm, weight_hbm, *refs):
    side0, side1, refs = refs[: len(PIECES)], refs[len(PIECES) : 2 * len(PIECES)], refs[2 * len(PIECES) :]
    *added, out_a, out_b, acc_ref, q_ref, near_ref, anchor_ref, attended_ref, weight, sems = refs
    state, added = (added[0], added[1:]) if early else (near_ref, added)
    host, me = info[0], info[1]
    load, near_load = strip_loads(steps, me, q_hbm, near_hbm, q_ref, near_ref, sems)
    last = pltpu.make_async_copy(weight_hbm, weight, sems.at[4])
    for copy in load + ([] if early else near_load) + [last]:
        copy.start()
    core = host % N_CORE
    for i, j in enumerate((0, 1, 2, 4)):
        start = LINE - CUT if j == 4 else LINE
        x, y = [side[j][start : start + SLICE] for side in (side0, side1)]
        anchor_ref[i * SLICE : (i + 1) * SLICE] = jnp.where(core == 0, x, y)
    for copy in load + ([] if early else near_load):
        copy.wait()

    def anchor(h):
        v = anchor_ref[:, columns(HEADS + h)]
        return anchor_ref[:, columns(h)], jnp.concatenate([v, jnp.ones_like(v)], 1)

    heads = start_heads(q_ref, state, acc_ref)

    @pl.when(host > 0)
    def _():
        for other, side in enumerate((side0, side1)):
            for h, (q, m) in enumerate(heads):
                k, v = passing(side, PIECES[EARLY:] if early else PIECES, h, host, other)
                if other == 0:
                    k, v = [x + [y] for x, y in zip((k, v), anchor(h))]
                acc_ref[h] += weigh(scores_of(q, jnp.concatenate(k, 0)), m, jnp.concatenate(v, 0))

    sums = slice(HEAD_SIZE, HEAD_SIZE + HEAD_SIZE // 2)
    worst = jnp.max(jnp.where(acc_ref[:, :, sums] < LIMIT, 0.0, 1.0))

    @pl.when(worst > 0)
    def _():
        if early:
            for copy in near_load:
                copy.start()
            for copy in near_load:
                copy.wait()

        def again(i, carry):
            h, g = i // GROUP, i % GROUP
            q = jnp.concatenate(queries(q_ref, h, g), 0)
            acc = near_ref[i]
            old = acc[:, 2 * HEAD_SIZE - 1 :]
            k, v = anchor(h)
            chunks = [(k, v, ANCHOR_ROWS)] + [
                (*(x[0] for x in passing(side, [piece], h, host, other)), seen_in(piece, host, other))
                for other, side in enumerate((side0, side1))
                for piece in PIECES
            ]
            for k, v, count in chunks:
                s = scores_of(q, k)
                s = jnp.where(lax.broadcasted_iota(jnp.int32, s.shape, 1) < count, s, NEG)
                m = jnp.maximum(old, jnp.max(s, axis=1, keepdims=True))
                acc = acc * jnp.exp2(old - m) + weigh(s, m, v)
                old = m
            acc_ref[h, pl.ds(pl.multiple_of(g * QUARTER, QUARTER), QUARTER)] = acc
            return carry

        lax.fori_loop(0, HEADS * GROUP, again, 0)

    outs = [acc_ref[h, :, :HEAD_SIZE] / acc_ref[h, :, HEAD_SIZE : HEAD_SIZE + 1] for h in range(HEADS)]
    attended_ref[...] = jnp.concatenate(
        [o[g * QUARTER : (g + 1) * QUARTER].astype(jnp.bfloat16) for o in outs for g in range(GROUP)], 1
    )
    last.wait()
    piece = 1024

    def project(i, carry):
        cut = pl.ds(pl.multiple_of(i * piece, piece), piece)
        x = jnp.dot(attended_ref[...], weight[:, cut], preferred_element_type=jnp.float32)
        for j, out in enumerate((out_a, out_b)):
            strip = x[j * STRIP : (j + 1) * STRIP]
            for ref in added[j::2]:
                strip = strip + ref[:, cut].astype(jnp.float32)
            out[:, cut] = strip.astype(jnp.bfloat16)
        return carry

    lax.fori_loop(0, D // piece, project, 0)


def attend(steps, info, queries, near_part, weight, sides, added, early):
    width = HEADS * GROUP * HEAD_SIZE
    resident, anywhere, hbm = [pl.BlockSpec(memory_space=x) for x in (pltpu.VMEM, pl.ANY, pltpu.HBM)]
    return pl.pallas_call(
        functools.partial(attend_kernel, steps, early),
        out_shape=[jax.ShapeDtypeStruct((STRIP, D), jnp.bfloat16)] * 2,
        in_specs=[pl.BlockSpec(memory_space=pltpu.SMEM), anywhere, hbm, anywhere]
        + [resident] * (len(sides) + len(added)),
        out_specs=[resident] * 2,
        scratch_shapes=[
            pltpu.VMEM((HEADS, ROWS, 2 * HEAD_SIZE), jnp.float32),
            pltpu.VMEM((2, STRIP, width), jnp.bfloat16),
            pltpu.VMEM((HEADS * GROUP, QUARTER, 2 * HEAD_SIZE), jnp.float32),
            pltpu.VMEM((ANCHOR_ROWS, 2 * WIDTH), jnp.bfloat16),
            pltpu.VMEM((QUARTER, width), jnp.bfloat16),
            pltpu.VMEM((width, D), jnp.bfloat16),
            pltpu.SemaphoreType.DMA((5,)),
        ],
        compiler_params=pltpu.CompilerParams(vmem_limit_bytes=30 << 20),
        name="attend",
    )(info, *in_hbm(queries, near_part, weight), *sides, *added)


def slices_kernel(k_hbm, v_hbm, *refs):
    *outs, sem = refs
    copies = [
        pltpu.make_async_copy(x.at[pl.ds(i * SLICE, SLICE)], out.at[:, pl.ds(j * WIDTH, WIDTH)], sem.at[i, j])
        for i, out in enumerate(outs)
        for j, x in enumerate((k_hbm, v_hbm))
    ]
    for copy in copies:
        copy.start()
    for copy in copies:
        copy.wait()


def slices_of(keys, values):
    return pl.pallas_call(
        slices_kernel,
        out_shape=[jax.ShapeDtypeStruct((SLICE, 2 * WIDTH), jnp.bfloat16)] * N_Y,
        in_specs=[pl.BlockSpec(memory_space=pl.ANY)] * 2,
        out_specs=[pl.BlockSpec(memory_space=pltpu.VMEM)] * N_Y,
        scratch_shapes=[pltpu.SemaphoreType.DMA((N_Y, 2))],
        name="slices",
    )(*in_hbm(keys, values))


def pick_kernel(rows_ref, k_hbm, v_hbm, out_ref, k_buf, v_buf, sem):
    pairs = ((k_hbm, k_buf), (v_hbm, v_buf))
    copies = [pltpu.make_async_copy(x, buf, sem.at[i]) for i, (x, buf) in enumerate(pairs)]
    for copy in copies:
        copy.start()
    one_hot = lax.broadcasted_iota(jnp.int32, (BLOCK, PASSING), 0) == rows_ref[...]
    one_hot = jnp.where(one_hot, 1.0, 0.0).astype(jnp.bfloat16)
    for i, (copy, (_, buf)) in enumerate(zip(copies, pairs)):
        copy.wait()
        out_ref[:, i * WIDTH : (i + 1) * WIDTH] = lax.dot_general(
            one_hot, buf[...], (((0,), (0,)), ((), ())), preferred_element_type=jnp.float32
        ).astype(jnp.bfloat16)


def pick(rows, keys, values):
    vmem, anywhere = pl.BlockSpec(memory_space=pltpu.VMEM), pl.BlockSpec(memory_space=pl.ANY)
    return pl.pallas_call(
        pick_kernel,
        out_shape=jax.ShapeDtypeStruct((PASSING, 2 * WIDTH), jnp.bfloat16),
        in_specs=[vmem, anywhere, anywhere],
        out_specs=vmem,
        scratch_shapes=[pltpu.VMEM((BLOCK, WIDTH), jnp.bfloat16)] * 2 + [pltpu.SemaphoreType.DMA((2,))],
        name="pick",
    )(rows, *in_hbm(keys, values))


def units_kernel(host, picked_ref, own_ref, *refs):
    *slices, out_ref = refs
    piece = jnp.where(host[0] == 0, own_ref[...], jnp.zeros(own_ref.shape, own_ref.dtype))
    for ref in slices:
        piece = piece + ref[...]
    for z in range(N_Z):
        out_ref[z, :PASSING] = picked_ref[...]
        out_ref[z, PASSING:] = piece


def plane_kernel(line_ref, out_ref):
    for z in range(N_Z):
        out_ref[z * PASSING : (z + 1) * PASSING] = line_ref[z, :PASSING]
    out_ref[LINE:] = line_ref[0, PASSING:]


def local(kernel, shapes, name):
    shapes = [jax.ShapeDtypeStruct(shape, jnp.bfloat16) for shape in shapes]
    return pl.pallas_call(kernel, out_shape=shapes, name=name)


def units_of(host, picked, own, slices):
    vmem = pl.BlockSpec(memory_space=pltpu.VMEM)
    return pl.pallas_call(
        units_kernel,
        out_shape=jax.ShapeDtypeStruct((N_Z, PASSING + SLICE, 2 * WIDTH), jnp.bfloat16),
        in_specs=[pl.BlockSpec(memory_space=pltpu.SMEM)] + [vmem] * (2 + len(slices)),
        out_specs=vmem,
        name="units",
    )(host.reshape(1), picked, own, *slices)


def place(y, z, core):
    return ((y % N_Y) * N_Z + z % N_Z) * N_CORE + core


def send(x, pairs):
    return lax.ppermute(x, "hst", pairs)


def on_device(queries, keys, values, pass_rows, out_weight):
    host = lax.axis_index("hst")
    me = lax.axis_index("head")
    along_z = [[place(y, z, c) for z in range(N_Z)] for y in range(N_Y) for c in range(N_CORE)]
    a2a = functools.partial(lax.all_to_all, axis_name="hst", split_axis=0, concat_axis=0, tiled=True)
    cores = [(h, h ^ 1) for h in range(N_Y * N_Z * N_CORE)]
    first, *slices = slices_of(keys, values)
    slices = [send(x, [(0, place(y + 1, 0, 0))]) for y, x in enumerate(slices)]
    units = units_of(host, pick(pass_rows, keys, values), first, slices)
    line = a2a(units, axis_index_groups=along_z)
    (plane,) = local(plane_kernel, [(PLANE, 2 * WIDTH)], "plane")(line)

    def along_y(x, step):
        places = [(y, z, c) for y in range(N_Y) for z in range(N_Z) for c in range(N_CORE)]
        return send(x, [(place(y, z, c), place(y + step, z, c)) for y, z, c in places])

    below, above = along_y(plane, 1), along_y(plane, -1)
    held, _ = lax.optimization_barrier((queries, plane))
    below, above, near_part = lax.optimization_barrier((below, above, near(held, keys, values)))
    side0 = [plane, below, above]
    side1 = [send(x, cores) for x in side0]
    halves = [along_y(below[:CUT], 1), along_y(above[CUT:], -1)]
    info = jnp.stack([host, me]).astype(jnp.int32)
    own, right, far, left = range(N_HEAD)
    first = ((far, 0), (far, 1))
    *halves, state = lax.optimization_barrier(
        (*halves, attend_early(first, info, queries, near_part, side0, side1))
    )
    sides = side0 + halves + side1 + [send(x, cores) for x in halves]

    def part(steps, *added, queries=queries, early=False):
        return attend(steps, info, queries, near_part, out_weight, sides, added, early)

    def shift(x, step):
        return lax.ppermute(x, "head", [(i, (i + step) % N_HEAD) for i in range(N_HEAD)])

    a, b = part(first, state, early=True)
    via_right, via_left = shift(a, 1), shift(b, -1)
    a, b = part(((right, 1), (left, 0)))
    held, a, b = lax.optimization_barrier((queries, a, b))
    left1, right0 = shift(a, 1), shift(b, -1)
    a, b = part(((right, 0), (left, 1)), via_right, via_left, queries=held)
    held, a, b = lax.optimization_barrier((queries, a, b))
    left0, right1 = shift(a, 1), shift(b, -1)
    a, b = part(((own, 0), (own, 1)), right0, left1, queries=held)
    own, received = [jnp.concatenate(x, 0).astype(jnp.float32) for x in ((a, b), (left0, right1))]
    return (own + received).astype(jnp.bfloat16)


def solution(mesh):
    placed = (P("hst", "head"), P("hst", "head"), P("hst", "head"), P("hst", None), P("head", None))
    return jax.shard_map(
        on_device, mesh=mesh, in_specs=placed, out_specs=P(("hst", "head"), None), check_vma=False
    )
```

```python
import functools

import jax
import jax.numpy as jnp
import numpy as np
from jax import lax
from jax.experimental import pallas as pl
from jax.experimental.pallas import tpu as pltpu
from jax.sharding import PartitionSpec as P

HEAD_SIZE = 128
GROUP = 4
HEADS = 2
ANCHOR_ROWS = 128
BLOCK = 512
QUARTER = 128
STRIP = 64
ROWS = GROUP * QUARTER
N_Y, N_Z, N_CORE, N_HEAD = 4, 8, 2, 4
PASSING = 64
WIDTH = HEADS * HEAD_SIZE
SLICE = ANCHOR_ROWS // N_Y
LINE = N_Z * PASSING
PLANE = LINE + SLICE
CUT = PLANE // 2
D = 4096
FACTOR = float(HEAD_SIZE**-0.5 * np.log2(np.e))
NEG = -1e30
LIMIT = float(2.0**110)


def in_hbm(*arrays):
    return [pltpu.with_memory_space_constraint(x, pltpu.HBM) for x in arrays]


def in_vmem(*arrays):
    return [pltpu.with_memory_space_constraint(x, pltpu.VMEM) for x in arrays]


def scores_of(q, k):
    return lax.dot_general(q, k, (((1,), (1,)), ((), ())), preferred_element_type=jnp.float32) * FACTOR


def with_ones(v, seen):
    return jnp.concatenate([jnp.where(seen, v, 0), jnp.where(seen, jnp.ones_like(v), 0)], 1)


def weigh(s, m, v):
    return jnp.dot(jnp.exp2(s - m).astype(jnp.bfloat16), v, preferred_element_type=jnp.float32)


def columns(i):
    return pl.ds(i * HEAD_SIZE if isinstance(i, int) else pl.multiple_of(i * HEAD_SIZE, HEAD_SIZE), HEAD_SIZE)


def near_kernel(q_ref, k_ref, v_ref, out_ref):
    def fold(i, carry):
        h, quarter = i // N_HEAD, i % N_HEAD
        rows = pl.ds(pl.multiple_of(quarter * QUARTER, QUARTER), QUARTER)
        q = jnp.concatenate([q_ref[rows, columns(h * GROUP + g)] for g in range(GROUP)], 0)
        v = v_ref[:, columns(h)]
        row = lax.broadcasted_iota(jnp.int32, (QUARTER, BLOCK), 0) + quarter * QUARTER
        col = lax.broadcasted_iota(jnp.int32, (QUARTER, BLOCK), 1)
        unseen = jnp.concatenate([jnp.where(col <= row, 0.0, NEG)] * GROUP, 0)
        s = scores_of(q, k_ref[:, columns(h)]) + unseen
        m = jnp.max(s, axis=1, keepdims=True)
        x = weigh(s, m, jnp.concatenate([v, jnp.ones_like(v)], 1))
        lane = lax.broadcasted_iota(jnp.int32, x.shape, 1)
        x = jnp.where(lane < HEAD_SIZE + HEAD_SIZE // 2, x, m)
        for g in range(GROUP):
            out_ref[h * GROUP + g, rows] = x[g * QUARTER : (g + 1) * QUARTER]
        return carry

    lax.fori_loop(0, HEADS * N_HEAD, fold, 0)


def near(queries, keys, values):
    return pl.pallas_call(
        near_kernel,
        out_shape=pltpu.VMEM((HEADS * GROUP, BLOCK, 2 * HEAD_SIZE), jnp.float32),
        compiler_params=pltpu.CompilerParams(vmem_limit_bytes=16 << 20),
        name="near",
    )(queries, keys, values)


PIECES = ((0, 0, LINE, 0), (1, 3, LINE, 0), (2, 1, LINE, 0), (3, 2, CUT, 0), (4, 2, LINE - CUT, CUT))


EARLY = 3, 1


def rows_of(steps, me):
    return [
        pl.ds(pl.multiple_of((me + step) % N_HEAD * QUARTER + strip * STRIP, STRIP), STRIP) for step, strip in steps
    ]


def queries(q_ref, rows, h, g):
    return [q_ref[x, columns(h * GROUP + g)] for x in rows]


def own_sums(near_ref, rows, i):
    return jnp.concatenate([near_ref[i, x] for x in rows], 0)


def seen_in(piece, host, other):
    _, step, size, start = piece
    chip = host // N_CORE
    before = chip + other * (host % N_CORE) - (chip // N_Z + step) % N_Y * N_Z
    return jnp.clip(before * PASSING - start, 0, size)


def passing(side, pieces, h, host, other):
    k = [side[piece[0]][: piece[2], columns(h)] for piece in pieces]
    v = []
    for piece in pieces:
        seen = lax.broadcasted_iota(jnp.int32, (piece[2], HEAD_SIZE), 0) < seen_in(piece, host, other)
        v.append(with_ones(side[piece[0]][: piece[2], columns(HEADS + h)], seen))
    return k, v


def start_heads(q_ref, rows, state, acc_ref):
    heads = []
    for h in range(HEADS):
        q = jnp.concatenate([x for g in range(GROUP) for x in queries(q_ref, rows, h, g)], 0)
        acc_ref[h] = jnp.concatenate([state(h * GROUP + g) for g in range(GROUP)], 0)
        heads.append((q, acc_ref[h, :, 2 * HEAD_SIZE - 1 :]))
    return heads


def early_kernel(steps, info, q_ref, near_ref, *refs):
    *sides, out_ref, acc_ref = refs
    side0, side1 = sides[: EARLY[0]], sides[EARLY[0] :]
    host, me = info[0], info[1]
    rows = rows_of(steps, me)
    heads = start_heads(q_ref, rows, lambda i: own_sums(near_ref, rows, i), acc_ref)

    @pl.when(host > 0)
    def _():
        for other, side in enumerate((side0, side1)):
            for h, (q, m) in enumerate(heads):
                k, v = passing(side, PIECES[: EARLY[other]], h, host, other)
                acc_ref[h] += weigh(scores_of(q, jnp.concatenate(k, 0)), m, jnp.concatenate(v, 0))

    for h, (q, m) in enumerate(heads):
        lane = lax.broadcasted_iota(jnp.int32, (ROWS, 2 * HEAD_SIZE), 1)
        x = jnp.where(lane < HEAD_SIZE + HEAD_SIZE // 2, acc_ref[h], m)
        for g in range(GROUP):
            out_ref[h * GROUP + g] = x[g * QUARTER : (g + 1) * QUARTER]


def attend_early(steps, info, queries, near_part, side0, side1):
    vmem = pl.BlockSpec(memory_space=pltpu.VMEM)
    sides = [*side0[: EARLY[0]], *side1[: EARLY[1]]]
    return pl.pallas_call(
        functools.partial(early_kernel, steps),
        out_shape=pltpu.VMEM((HEADS * GROUP, QUARTER, 2 * HEAD_SIZE), jnp.float32),
        in_specs=[pl.BlockSpec(memory_space=pltpu.SMEM)] + [vmem] * (2 + len(sides)),
        out_specs=vmem,
        scratch_shapes=[pltpu.VMEM((HEADS, ROWS, 2 * HEAD_SIZE), jnp.float32)],
        compiler_params=pltpu.CompilerParams(vmem_limit_bytes=24 << 20),
        name="early",
    )(info, *in_vmem(queries, near_part), *sides)


def attend_kernel(steps, early, info, q_ref, near_ref, weight_hbm, *refs):
    side0, side1, refs = refs[: len(PIECES)], refs[len(PIECES) : 2 * len(PIECES)], refs[2 * len(PIECES) :]
    *added, out_a, out_b, acc_ref, anchor_ref, attended_ref, weight, sem = refs
    host, me = info[0], info[1]
    last = pltpu.make_async_copy(weight_hbm, weight, sem)
    last.start()
    rows = rows_of(steps, me)
    state = functools.partial(own_sums, near_ref, rows)
    if early:
        state, *added = added
        state = state.__getitem__
    core = host % N_CORE
    for i, j in enumerate((0, 1, 2, 4)):
        start = LINE - CUT if j == 4 else LINE
        x, y = [side[j][start : start + SLICE] for side in (side0, side1)]
        anchor_ref[i * SLICE : (i + 1) * SLICE] = jnp.where(core == 0, x, y)
    def anchor(h):
        v = anchor_ref[:, columns(HEADS + h)]
        return anchor_ref[:, columns(h)], jnp.concatenate([v, jnp.ones_like(v)], 1)

    heads = start_heads(q_ref, rows, state, acc_ref)

    @pl.when(host > 0)
    def _():
        for other, side in enumerate((side0, side1)):
            for h, (q, m) in enumerate(heads):
                k, v = passing(side, PIECES[EARLY[other] if early else 0 :], h, host, other)
                if other == 0:
                    k, v = [x + [y] for x, y in zip((k, v), anchor(h))]
                acc_ref[h] += weigh(scores_of(q, jnp.concatenate(k, 0)), m, jnp.concatenate(v, 0))

    sums = slice(HEAD_SIZE, HEAD_SIZE + HEAD_SIZE // 2)
    worst = jnp.max(jnp.where(acc_ref[:, :, sums] < LIMIT, 0.0, 1.0))

    @pl.when(worst > 0)
    def _():
        def again(i, carry):
            h, g = i // GROUP, i % GROUP
            q = jnp.concatenate(queries(q_ref, rows, h, g), 0)
            acc = own_sums(near_ref, rows, i)
            old = acc[:, 2 * HEAD_SIZE - 1 :]
            k, v = anchor(h)
            chunks = [(k, v, ANCHOR_ROWS)] + [
                (*(x[0] for x in passing(side, [piece], h, host, other)), seen_in(piece, host, other))
                for other, side in enumerate((side0, side1))
                for piece in PIECES
            ]
            for k, v, count in chunks:
                s = scores_of(q, k)
                s = jnp.where(lax.broadcasted_iota(jnp.int32, s.shape, 1) < count, s, NEG)
                m = jnp.maximum(old, jnp.max(s, axis=1, keepdims=True))
                acc = acc * jnp.exp2(old - m) + weigh(s, m, v)
                old = m
            acc_ref[h, pl.ds(pl.multiple_of(g * QUARTER, QUARTER), QUARTER)] = acc
            return carry

        lax.fori_loop(0, HEADS * GROUP, again, 0)

    outs = [acc_ref[h, :, :HEAD_SIZE] / acc_ref[h, :, HEAD_SIZE : HEAD_SIZE + 1] for h in range(HEADS)]
    attended_ref[...] = jnp.concatenate(
        [o[g * QUARTER : (g + 1) * QUARTER].astype(jnp.bfloat16) for o in outs for g in range(GROUP)], 1
    )
    last.wait()
    piece = 1024

    def project(i, carry):
        cut = pl.ds(pl.multiple_of(i * piece, piece), piece)
        x = jnp.dot(attended_ref[...], weight[:, cut], preferred_element_type=jnp.float32)
        for j, out in enumerate((out_a, out_b)):
            strip = x[j * STRIP : (j + 1) * STRIP]
            for ref in added[j::2]:
                strip = strip + ref[:, cut].astype(jnp.float32)
            out[:, cut] = strip.astype(jnp.bfloat16)
        return carry

    lax.fori_loop(0, D // piece, project, 0)


def attend(steps, info, queries, near_part, weight, sides, added, early):
    width = HEADS * GROUP * HEAD_SIZE
    resident, anywhere = [pl.BlockSpec(memory_space=x) for x in (pltpu.VMEM, pl.ANY)]
    return pl.pallas_call(
        functools.partial(attend_kernel, steps, early),
        out_shape=[jax.ShapeDtypeStruct((STRIP, D), jnp.bfloat16)] * 2,
        in_specs=[pl.BlockSpec(memory_space=pltpu.SMEM), resident, resident, anywhere]
        + [resident] * (len(sides) + len(added)),
        out_specs=[resident] * 2,
        scratch_shapes=[
            pltpu.VMEM((HEADS, ROWS, 2 * HEAD_SIZE), jnp.float32),
            pltpu.VMEM((ANCHOR_ROWS, 2 * WIDTH), jnp.bfloat16),
            pltpu.VMEM((QUARTER, width), jnp.bfloat16),
            pltpu.VMEM((width, D), jnp.bfloat16),
            pltpu.SemaphoreType.DMA(()),
        ],
        compiler_params=pltpu.CompilerParams(vmem_limit_bytes=30 << 20),
        name="attend",
    )(info, *in_vmem(queries, near_part), *in_hbm(weight), *sides, *added)


def slices_kernel(k_hbm, v_hbm, *refs):
    *outs, sem = refs
    copies = [
        pltpu.make_async_copy(x.at[pl.ds(i * SLICE, SLICE)], out.at[:, pl.ds(j * WIDTH, WIDTH)], sem.at[i, j])
        for i, out in enumerate(outs)
        for j, x in enumerate((k_hbm, v_hbm))
    ]
    for copy in copies:
        copy.start()
    for copy in copies:
        copy.wait()


def slices_of(keys, values):
    return pl.pallas_call(
        slices_kernel,
        out_shape=[jax.ShapeDtypeStruct((SLICE, 2 * WIDTH), jnp.bfloat16)] * N_Y,
        in_specs=[pl.BlockSpec(memory_space=pl.ANY)] * 2,
        out_specs=[pl.BlockSpec(memory_space=pltpu.VMEM)] * N_Y,
        scratch_shapes=[pltpu.SemaphoreType.DMA((N_Y, 2))],
        name="slices",
    )(*in_hbm(keys, values))


def pick_kernel(rows_ref, k_hbm, v_hbm, out_ref, k_buf, v_buf, sem):
    pairs = ((k_hbm, k_buf), (v_hbm, v_buf))
    copies = [pltpu.make_async_copy(x, buf, sem.at[i]) for i, (x, buf) in enumerate(pairs)]
    for copy in copies:
        copy.start()
    one_hot = lax.broadcasted_iota(jnp.int32, (BLOCK, PASSING), 0) == rows_ref[...]
    one_hot = jnp.where(one_hot, 1.0, 0.0).astype(jnp.bfloat16)
    for i, (copy, (_, buf)) in enumerate(zip(copies, pairs)):
        copy.wait()
        out_ref[:, i * WIDTH : (i + 1) * WIDTH] = lax.dot_general(
            one_hot, buf[...], (((0,), (0,)), ((), ())), preferred_element_type=jnp.float32
        ).astype(jnp.bfloat16)


def pick(rows, keys, values):
    vmem, anywhere = pl.BlockSpec(memory_space=pltpu.VMEM), pl.BlockSpec(memory_space=pl.ANY)
    return pl.pallas_call(
        pick_kernel,
        out_shape=jax.ShapeDtypeStruct((PASSING, 2 * WIDTH), jnp.bfloat16),
        in_specs=[vmem, anywhere, anywhere],
        out_specs=vmem,
        scratch_shapes=[pltpu.VMEM((BLOCK, WIDTH), jnp.bfloat16)] * 2 + [pltpu.SemaphoreType.DMA((2,))],
        name="pick",
    )(rows, *in_hbm(keys, values))


def units_kernel(host, picked_ref, own_ref, *refs):
    *slices, out_ref = refs
    piece = jnp.where(host[0] == 0, own_ref[...], jnp.zeros(own_ref.shape, own_ref.dtype))
    for ref in slices:
        piece = piece + ref[...]
    for z in range(N_Z):
        out_ref[z, :PASSING] = picked_ref[...]
        out_ref[z, PASSING:] = piece


def plane_kernel(line_ref, out_ref):
    for z in range(N_Z):
        out_ref[z * PASSING : (z + 1) * PASSING] = line_ref[z, :PASSING]
    out_ref[LINE:] = line_ref[0, PASSING:]


def local(kernel, shapes, name):
    shapes = [jax.ShapeDtypeStruct(shape, jnp.bfloat16) for shape in shapes]
    return pl.pallas_call(kernel, out_shape=shapes, name=name)


def units_of(host, picked, own, slices):
    vmem = pl.BlockSpec(memory_space=pltpu.VMEM)
    return pl.pallas_call(
        units_kernel,
        out_shape=jax.ShapeDtypeStruct((N_Z, PASSING + SLICE, 2 * WIDTH), jnp.bfloat16),
        in_specs=[pl.BlockSpec(memory_space=pltpu.SMEM)] + [vmem] * (2 + len(slices)),
        out_specs=vmem,
        name="units",
    )(host.reshape(1), picked, own, *slices)


def place(y, z, core):
    return ((y % N_Y) * N_Z + z % N_Z) * N_CORE + core


def send(x, pairs):
    return lax.ppermute(x, "hst", pairs)


def on_device(queries, keys, values, pass_rows, out_weight):
    host = lax.axis_index("hst")
    me = lax.axis_index("head")
    along_z = [[place(y, z, c) for z in range(N_Z)] for y in range(N_Y) for c in range(N_CORE)]
    a2a = functools.partial(lax.all_to_all, axis_name="hst", split_axis=0, concat_axis=0, tiled=True)
    cores = [(h, h ^ 1) for h in range(N_Y * N_Z * N_CORE)]
    first, *slices = slices_of(keys, values)
    slices = [send(x, [(0, place(y + 1, 0, 0))]) for y, x in enumerate(slices)]
    units = units_of(host, pick(pass_rows, keys, values), first, slices)
    line = a2a(units, axis_index_groups=along_z)
    (plane,) = local(plane_kernel, [(PLANE, 2 * WIDTH)], "plane")(line)

    def along_y(x, step):
        places = [(y, z, c) for y in range(N_Y) for z in range(N_Z) for c in range(N_CORE)]
        return send(x, [(place(y, z, c), place(y + step, z, c)) for y, z, c in places])

    below, above = along_y(plane, 1), along_y(plane, -1)
    held, _ = lax.optimization_barrier((queries, plane))
    below, above, near_part = lax.optimization_barrier((below, above, near(held, keys, values)))
    side0 = [plane, below, above]
    side1 = [send(x, cores) for x in side0]
    halves = [along_y(below[:CUT], 1), along_y(above[CUT:], -1)]
    info = jnp.stack([host, me]).astype(jnp.int32)
    own, right, far, left = range(N_HEAD)
    first = ((far, 0), (far, 1))
    *halves, state = lax.optimization_barrier(
        (*halves, attend_early(first, info, queries, near_part, side0, side1))
    )
    sides = side0 + halves + side1 + [send(x, cores) for x in halves]

    def part(steps, *added, queries=queries, early=False):
        return attend(steps, info, queries, near_part, out_weight, sides, added, early)

    def shift(x, step):
        return lax.ppermute(x, "head", [(i, (i + step) % N_HEAD) for i in range(N_HEAD)])

    a, b = part(first, state, early=True)
    via_right, via_left = shift(a, 1), shift(b, -1)
    a, b = part(((right, 1), (left, 0)))
    held, a, b = lax.optimization_barrier((queries, a, b))
    left1, right0 = shift(a, 1), shift(b, -1)
    a, b = part(((right, 0), (left, 1)), via_right, via_left, queries=held)
    held, a, b = lax.optimization_barrier((queries, a, b))
    left0, right1 = shift(a, 1), shift(b, -1)
    a, b = part(((own, 0), (own, 1)), right0, left1, queries=held)
    own, received = [jnp.concatenate(x, 0).astype(jnp.float32) for x in ((a, b), (left0, right1))]
    return (own + received).astype(jnp.bfloat16)


def solution(mesh):
    placed = (P("hst", "head"), P("hst", "head"), P("hst", "head"), P("hst", None), P("head", None))
    return jax.shard_map(
        on_device, mesh=mesh, in_specs=placed, out_specs=P(("hst", "head"), None), check_vma=False
    )
```

```python
import functools

import jax
import jax.numpy as jnp
import numpy as np
from jax import lax
from jax.experimental import pallas as pl
from jax.experimental.pallas import tpu as pltpu
from jax.sharding import PartitionSpec as P

HEAD_SIZE = 128
GROUP = 4
HEADS = 2
ANCHOR_ROWS = 128
BLOCK = 512
QUARTER = 128
STRIP = 64
ROWS = GROUP * QUARTER
N_Y, N_Z, N_CORE, N_HEAD = 4, 8, 2, 4
PASSING = 64
WIDTH = HEADS * HEAD_SIZE
SLICE = ANCHOR_ROWS // N_Y
LINE = N_Z * PASSING
PLANE = LINE + SLICE
D = 4096
FACTOR = float(HEAD_SIZE**-0.5 * np.log2(np.e))
NEG = -1e30
LIMIT = float(2.0**110)


def in_hbm(*arrays):
    return [pltpu.with_memory_space_constraint(x, pltpu.HBM) for x in arrays]


def in_vmem(*arrays):
    return [pltpu.with_memory_space_constraint(x, pltpu.VMEM) for x in arrays]


def scores_of(q, k):
    return lax.dot_general(q, k, (((1,), (1,)), ((), ())), preferred_element_type=jnp.float32) * FACTOR


def with_ones(v, seen):
    return jnp.concatenate([jnp.where(seen, v, 0), jnp.where(seen, jnp.ones_like(v), 0)], 1)


def weigh(s, m, v):
    return jnp.dot(jnp.exp2(s - m).astype(jnp.bfloat16), v, preferred_element_type=jnp.float32)


def columns(i):
    return pl.ds(i * HEAD_SIZE if isinstance(i, int) else pl.multiple_of(i * HEAD_SIZE, HEAD_SIZE), HEAD_SIZE)


def near_kernel(q_ref, k_ref, v_ref, out_hbm, out_ref, sems):
    def store(i):
        h, quarter = i // N_HEAD, i % N_HEAD
        rows = pl.ds(pl.multiple_of(quarter * QUARTER, QUARTER), QUARTER)
        at = (pl.ds(h * GROUP, GROUP), rows)
        return h, quarter, rows, pltpu.make_async_copy(out_ref.at[at], out_hbm.at[at], sems.at[i])

    def fold(i, carry):
        h, quarter, rows, copy = store(i)
        q = jnp.concatenate([q_ref[rows, columns(h * GROUP + g)] for g in range(GROUP)], 0)
        v = v_ref[:, columns(h)]
        row = lax.broadcasted_iota(jnp.int32, (QUARTER, BLOCK), 0) + quarter * QUARTER
        col = lax.broadcasted_iota(jnp.int32, (QUARTER, BLOCK), 1)
        unseen = jnp.concatenate([jnp.where(col <= row, 0.0, NEG)] * GROUP, 0)
        s = scores_of(q, k_ref[:, columns(h)]) + unseen
        m = jnp.max(s, axis=1, keepdims=True)
        x = weigh(s, m, jnp.concatenate([v, jnp.ones_like(v)], 1))
        lane = lax.broadcasted_iota(jnp.int32, x.shape, 1)
        x = jnp.where(lane < HEAD_SIZE + HEAD_SIZE // 2, x, m)
        for g in range(GROUP):
            out_ref[h * GROUP + g, rows] = x[g * QUARTER : (g + 1) * QUARTER]
        copy.start()
        return carry

    def finish(i, carry):
        store(i)[-1].wait()
        return carry

    lax.fori_loop(0, HEADS * N_HEAD, fold, 0)
    lax.fori_loop(0, HEADS * N_HEAD, finish, 0)


def near(queries, keys, values):
    shape = pltpu.HBM((HEADS * GROUP, BLOCK, 2 * HEAD_SIZE), jnp.float32)
    vmem = pl.BlockSpec(memory_space=pltpu.VMEM)
    return pl.pallas_call(
        near_kernel,
        out_shape=shape,
        in_specs=[vmem] * 3,
        out_specs=pl.BlockSpec(memory_space=pltpu.HBM),
        scratch_shapes=[pltpu.VMEM(shape.shape, shape.dtype), pltpu.SemaphoreType.DMA((HEADS * N_HEAD,))],
        compiler_params=pltpu.CompilerParams(vmem_limit_bytes=16 << 20),
        name="near",
    )(queries, keys, values)


PIECES = (0, 3, 1, 2)
EARLY = 3, 1


def rows_of(steps, me):
    return [
        pl.ds(pl.multiple_of((me + step) % N_HEAD * QUARTER + strip * STRIP, STRIP), STRIP) for step, strip in steps
    ]


def queries(q_ref, rows, h, g):
    return [q_ref[x, columns(h * GROUP + g)] for x in rows]


def own_sums(near_ref, rows, i):
    return jnp.concatenate([near_ref[i, x] for x in rows], 0)


def seen_in(piece, host, other):
    chip = host // N_CORE
    before = chip + other * (host % N_CORE) - (chip // N_Z + PIECES[piece]) % N_Y * N_Z
    return jnp.clip(before * PASSING, 0, LINE)


def passing(side, pieces, h, host, other):
    k = [side[piece][:LINE, columns(h)] for piece in pieces]
    v = []
    for piece in pieces:
        seen = lax.broadcasted_iota(jnp.int32, (LINE, HEAD_SIZE), 0) < seen_in(piece, host, other)
        v.append(with_ones(side[piece][:LINE, columns(HEADS + h)], seen))
    return k, v


def start_heads(q_ref, rows, state, acc_ref):
    heads = []
    for h in range(HEADS):
        q = jnp.concatenate([x for g in range(GROUP) for x in queries(q_ref, rows, h, g)], 0)
        acc_ref[h] = jnp.concatenate([state(h * GROUP + g) for g in range(GROUP)], 0)
        heads.append((q, acc_ref[h, :, 2 * HEAD_SIZE - 1 :]))
    return heads


def early_kernel(steps, info, q_ref, near_hbm, *refs):
    *sides, out_ref, acc_ref, near_ref, sems = refs
    side0, side1 = sides[: EARLY[0]], sides[EARLY[0] :]
    host, me = info[0], info[1]
    rows = rows_of(steps, me)
    loads = [
        pltpu.make_async_copy(near_hbm.at[:, x], near_ref.at[:, pl.ds(i * STRIP, STRIP)], sems.at[i])
        for i, x in enumerate(rows)
    ]
    for load in loads:
        load.start()
    for load in loads:
        load.wait()
    heads = start_heads(q_ref, rows, near_ref.__getitem__, acc_ref)

    @pl.when(host > 0)
    def _():
        for other, side in enumerate((side0, side1)):
            for h, (q, m) in enumerate(heads):
                k, v = passing(side, range(EARLY[other]), h, host, other)
                acc_ref[h] += weigh(scores_of(q, jnp.concatenate(k, 0)), m, jnp.concatenate(v, 0))

    for h, (q, m) in enumerate(heads):
        lane = lax.broadcasted_iota(jnp.int32, (ROWS, 2 * HEAD_SIZE), 1)
        x = jnp.where(lane < HEAD_SIZE + HEAD_SIZE // 2, acc_ref[h], m)
        for g in range(GROUP):
            out_ref[h * GROUP + g] = x[g * QUARTER : (g + 1) * QUARTER]


def attend_early(steps, info, queries, near_part, side0, side1):
    vmem, anywhere = [pl.BlockSpec(memory_space=x) for x in (pltpu.VMEM, pl.ANY)]
    sides = [*side0[: EARLY[0]], *side1[: EARLY[1]]]
    return pl.pallas_call(
        functools.partial(early_kernel, steps),
        out_shape=pltpu.VMEM((HEADS * GROUP, QUARTER, 2 * HEAD_SIZE), jnp.float32),
        in_specs=[pl.BlockSpec(memory_space=pltpu.SMEM), vmem, anywhere] + [vmem] * len(sides),
        out_specs=vmem,
        scratch_shapes=[
            pltpu.VMEM((HEADS, ROWS, 2 * HEAD_SIZE), jnp.float32),
            pltpu.VMEM((HEADS * GROUP, QUARTER, 2 * HEAD_SIZE), jnp.float32),
            pltpu.SemaphoreType.DMA((2,)),
        ],
        compiler_params=pltpu.CompilerParams(vmem_limit_bytes=24 << 20),
        name="early",
    )(info, *in_vmem(queries), *in_hbm(near_part), *sides)


def attend_kernel(steps, early, info, q_ref, near_ref, weight_hbm, *refs):
    side0, side1, refs = refs[: len(PIECES)], refs[len(PIECES) : 2 * len(PIECES)], refs[2 * len(PIECES) :]
    *added, out_a, out_b, acc_ref, anchor_ref, attended_ref, weight, sem = refs
    host, me = info[0], info[1]
    last = pltpu.make_async_copy(weight_hbm, weight, sem)
    last.start()
    rows = rows_of(steps, me)
    state = functools.partial(own_sums, near_ref, rows)
    if early:
        state, *added = added
        state = state.__getitem__
    core = host % N_CORE
    for i in range(N_Y):
        x, y = [side[i][LINE:] for side in (side0, side1)]
        anchor_ref[i * SLICE : (i + 1) * SLICE] = jnp.where(core == 0, x, y)

    def anchor(h):
        v = anchor_ref[:, columns(HEADS + h)]
        return anchor_ref[:, columns(h)], jnp.concatenate([v, jnp.ones_like(v)], 1)

    heads = start_heads(q_ref, rows, state, acc_ref)

    @pl.when(host > 0)
    def _():
        for other, side in enumerate((side0, side1)):
            for h, (q, m) in enumerate(heads):
                k, v = passing(side, range(EARLY[other] if early else 0, len(PIECES)), h, host, other)
                if other == 0:
                    k, v = [x + [y] for x, y in zip((k, v), anchor(h))]
                acc_ref[h] += weigh(scores_of(q, jnp.concatenate(k, 0)), m, jnp.concatenate(v, 0))

    sums = slice(HEAD_SIZE, HEAD_SIZE + HEAD_SIZE // 2)
    worst = jnp.max(jnp.where(acc_ref[:, :, sums] < LIMIT, 0.0, 1.0))

    @pl.when(worst > 0)
    def _():
        def again(i, carry):
            h, g = i // GROUP, i % GROUP
            q = jnp.concatenate(queries(q_ref, rows, h, g), 0)
            acc = own_sums(near_ref, rows, i)
            old = acc[:, 2 * HEAD_SIZE - 1 :]
            k, v = anchor(h)
            chunks = [(k, v, ANCHOR_ROWS)] + [
                (*(x[0] for x in passing(side, [piece], h, host, other)), seen_in(piece, host, other))
                for other, side in enumerate((side0, side1))
                for piece in range(len(PIECES))
            ]
            for k, v, count in chunks:
                s = scores_of(q, k)
                s = jnp.where(lax.broadcasted_iota(jnp.int32, s.shape, 1) < count, s, NEG)
                m = jnp.maximum(old, jnp.max(s, axis=1, keepdims=True))
                acc = acc * jnp.exp2(old - m) + weigh(s, m, v)
                old = m
            acc_ref[h, pl.ds(pl.multiple_of(g * QUARTER, QUARTER), QUARTER)] = acc
            return carry

        lax.fori_loop(0, HEADS * GROUP, again, 0)

    outs = [acc_ref[h, :, :HEAD_SIZE] / acc_ref[h, :, HEAD_SIZE : HEAD_SIZE + 1] for h in range(HEADS)]
    attended_ref[...] = jnp.concatenate(
        [o[g * QUARTER : (g + 1) * QUARTER].astype(jnp.bfloat16) for o in outs for g in range(GROUP)], 1
    )
    last.wait()
    piece = 1024

    def project(i, carry):
        cut = pl.ds(pl.multiple_of(i * piece, piece), piece)
        x = jnp.dot(attended_ref[...], weight[:, cut], preferred_element_type=jnp.float32)
        for j, out in enumerate((out_a, out_b)):
            strip = x[j * STRIP : (j + 1) * STRIP]
            for ref in added[j::2]:
                strip = strip + ref[:, cut].astype(jnp.float32)
            out[:, cut] = strip.astype(jnp.bfloat16)
        return carry

    lax.fori_loop(0, D // piece, project, 0)


def attend(steps, info, queries, near_part, weight, sides, added, early):
    width = HEADS * GROUP * HEAD_SIZE
    resident, anywhere = [pl.BlockSpec(memory_space=x) for x in (pltpu.VMEM, pl.ANY)]
    return pl.pallas_call(
        functools.partial(attend_kernel, steps, early),
        out_shape=[jax.ShapeDtypeStruct((STRIP, D), jnp.bfloat16)] * 2,
        in_specs=[pl.BlockSpec(memory_space=pltpu.SMEM), resident, resident, anywhere]
        + [resident] * (len(sides) + len(added)),
        out_specs=[resident] * 2,
        scratch_shapes=[
            pltpu.VMEM((HEADS, ROWS, 2 * HEAD_SIZE), jnp.float32),
            pltpu.VMEM((ANCHOR_ROWS, 2 * WIDTH), jnp.bfloat16),
            pltpu.VMEM((QUARTER, width), jnp.bfloat16),
            pltpu.VMEM((width, D), jnp.bfloat16),
            pltpu.SemaphoreType.DMA(()),
        ],
        compiler_params=pltpu.CompilerParams(vmem_limit_bytes=30 << 20),
        name="attend",
    )(info, *in_vmem(queries, near_part), *in_hbm(weight), *sides, *added)


def slices_kernel(k_hbm, v_hbm, *refs):
    *outs, sem = refs
    copies = [
        pltpu.make_async_copy(x.at[pl.ds(i * SLICE, SLICE)], out.at[:, pl.ds(j * WIDTH, WIDTH)], sem.at[i, j])
        for i, out in enumerate(outs)
        for j, x in enumerate((k_hbm, v_hbm))
    ]
    for copy in copies:
        copy.start()
    for copy in copies:
        copy.wait()


def slices_of(keys, values):
    return pl.pallas_call(
        slices_kernel,
        out_shape=[jax.ShapeDtypeStruct((SLICE, 2 * WIDTH), jnp.bfloat16)] * N_Y,
        in_specs=[pl.BlockSpec(memory_space=pl.ANY)] * 2,
        out_specs=[pl.BlockSpec(memory_space=pltpu.VMEM)] * N_Y,
        scratch_shapes=[pltpu.SemaphoreType.DMA((N_Y, 2))],
        name="slices",
    )(*in_hbm(keys, values))


def pick_kernel(rows_ref, k_hbm, v_hbm, out_ref, k_buf, v_buf, sem):
    pairs = ((k_hbm, k_buf), (v_hbm, v_buf))
    copies = [pltpu.make_async_copy(x, buf, sem.at[i]) for i, (x, buf) in enumerate(pairs)]
    for copy in copies:
        copy.start()
    one_hot = lax.broadcasted_iota(jnp.int32, (BLOCK, PASSING), 0) == rows_ref[...]
    one_hot = jnp.where(one_hot, 1.0, 0.0).astype(jnp.bfloat16)
    for i, (copy, (_, buf)) in enumerate(zip(copies, pairs)):
        copy.wait()
        out_ref[:, i * WIDTH : (i + 1) * WIDTH] = lax.dot_general(
            one_hot, buf[...], (((0,), (0,)), ((), ())), preferred_element_type=jnp.float32
        ).astype(jnp.bfloat16)


def pick(rows, keys, values):
    vmem, anywhere = pl.BlockSpec(memory_space=pltpu.VMEM), pl.BlockSpec(memory_space=pl.ANY)
    return pl.pallas_call(
        pick_kernel,
        out_shape=jax.ShapeDtypeStruct((PASSING, 2 * WIDTH), jnp.bfloat16),
        in_specs=[vmem, anywhere, anywhere],
        out_specs=vmem,
        scratch_shapes=[pltpu.VMEM((BLOCK, WIDTH), jnp.bfloat16)] * 2 + [pltpu.SemaphoreType.DMA((2,))],
        name="pick",
    )(rows, *in_hbm(keys, values))


def units_kernel(host, picked_ref, own_ref, *refs):
    *slices, out_ref = refs
    piece = jnp.where(host[0] == 0, own_ref[...], jnp.zeros(own_ref.shape, own_ref.dtype))
    for ref in slices:
        piece = piece + ref[...]
    for z in range(N_Z):
        out_ref[z, :PASSING] = picked_ref[...]
        out_ref[z, PASSING:] = piece


def plane_kernel(line_ref, out_ref):
    for z in range(N_Z):
        out_ref[z * PASSING : (z + 1) * PASSING] = line_ref[z, :PASSING]
    out_ref[LINE:] = line_ref[0, PASSING:]


def local(kernel, shapes, name):
    shapes = [jax.ShapeDtypeStruct(shape, jnp.bfloat16) for shape in shapes]
    return pl.pallas_call(kernel, out_shape=shapes, name=name)


def units_of(host, picked, own, slices):
    vmem = pl.BlockSpec(memory_space=pltpu.VMEM)
    return pl.pallas_call(
        units_kernel,
        out_shape=jax.ShapeDtypeStruct((N_Z, PASSING + SLICE, 2 * WIDTH), jnp.bfloat16),
        in_specs=[pl.BlockSpec(memory_space=pltpu.SMEM)] + [vmem] * (2 + len(slices)),
        out_specs=vmem,
        name="units",
    )(host.reshape(1), picked, own, *slices)


def place(y, z, core):
    return ((y % N_Y) * N_Z + z % N_Z) * N_CORE + core


def send(x, pairs):
    return lax.ppermute(x, "hst", pairs)


def on_device(queries, keys, values, pass_rows, out_weight):
    host = lax.axis_index("hst")
    me = lax.axis_index("head")
    along_z = [[place(y, z, c) for z in range(N_Z)] for y in range(N_Y) for c in range(N_CORE)]
    a2a = functools.partial(lax.all_to_all, axis_name="hst", split_axis=0, concat_axis=0, tiled=True)
    cores = [(h, h ^ 1) for h in range(N_Y * N_Z * N_CORE)]
    first, *slices = slices_of(keys, values)
    slices = [send(x, [(0, place(y + 1, 0, 0))]) for y, x in enumerate(slices)]
    units = units_of(host, pick(pass_rows, keys, values), first, slices)
    line = a2a(units, axis_index_groups=along_z)
    (plane,) = local(plane_kernel, [(PLANE, 2 * WIDTH)], "plane")(line)

    def along_y(x, step):
        places = [(y, z, c) for y in range(N_Y) for z in range(N_Z) for c in range(N_CORE)]
        return send(x, [(place(y, z, c), place(y + step, z, c)) for y, z, c in places])

    below, above = along_y(plane, 1), along_y(plane, -1)
    held, _ = lax.optimization_barrier((queries, plane))
    below, above, near_part = lax.optimization_barrier((below, above, near(held, keys, values)))
    side0 = [plane, below, above]
    side1 = [send(x, cores) for x in side0]
    onward = [(place(y, z, c), place(y + 1 - 2 * c, z, c)) for y in range(N_Y) for z in range(N_Z) for c in range(N_CORE)]
    opposite = send(jnp.where(host % N_CORE == 0, below, above), onward)
    info = jnp.stack([host, me]).astype(jnp.int32)
    own, right, far, left = range(N_HEAD)
    first = ((far, 0), (far, 1))
    opposite, state = lax.optimization_barrier(
        (opposite, attend_early(first, info, queries, near_part, side0, side1))
    )
    sides = side0 + [opposite] + side1 + [send(opposite, cores)]

    def part(steps, *added, queries=queries, early=False):
        return attend(steps, info, queries, near_part, out_weight, sides, added, early)

    def shift(x, step):
        return lax.ppermute(x, "head", [(i, (i + step) % N_HEAD) for i in range(N_HEAD)])

    a, b = part(first, state, early=True)
    via_right, via_left = shift(a, 1), shift(b, -1)
    a, b = part(((right, 1), (left, 0)))
    held, a, b = lax.optimization_barrier((queries, a, b))
    left1, right0 = shift(a, 1), shift(b, -1)
    a, b = part(((right, 0), (left, 1)), via_right, via_left, queries=held)
    held, a, b = lax.optimization_barrier((queries, a, b))
    left0, right1 = shift(a, 1), shift(b, -1)
    a, b = part(((own, 0), (own, 1)), right0, left1, queries=held)
    own, received = [jnp.concatenate(x, 0).astype(jnp.float32) for x in ((a, b), (left0, right1))]
    return (own + received).astype(jnp.bfloat16)


def solution(mesh):
    placed = (P("hst", "head"), P("hst", "head"), P("hst", "head"), P("hst", None), P("head", None))
    return jax.shard_map(
        on_device, mesh=mesh, in_specs=placed, out_specs=P(("hst", "head"), None), check_vma=False
    )
```

```python
import functools

import jax
import jax.numpy as jnp
import numpy as np
from jax import lax
from jax.experimental import pallas as pl
from jax.experimental.pallas import tpu as pltpu
from jax.sharding import PartitionSpec as P

HEAD_SIZE = 128
GROUP = 4
HEADS = 2
ANCHOR_ROWS = 128
BLOCK = 512
QUARTER = 128
STRIP = 64
ROWS = GROUP * QUARTER
N_Y, N_Z, N_CORE, N_HEAD = 4, 8, 2, 4
PASSING = 64
WIDTH = HEADS * HEAD_SIZE
SLICE = ANCHOR_ROWS // N_Y
LINE = N_Z * PASSING
PLANE = LINE + SLICE
CUT = PLANE // 2
D = 4096
CHUNK = 1024
FACTOR = float(HEAD_SIZE**-0.5 * np.log2(np.e))
NEG = -1e30
LIMIT = float(2.0**110)


def in_hbm(*arrays):
    return [pltpu.with_memory_space_constraint(x, pltpu.HBM) for x in arrays]


def in_vmem(*arrays):
    return [pltpu.with_memory_space_constraint(x, pltpu.VMEM) for x in arrays]


def scores_of(q, k):
    return lax.dot_general(q, k, (((1,), (1,)), ((), ())), preferred_element_type=jnp.float32) * FACTOR


def with_ones(v, seen):
    return jnp.concatenate([jnp.where(seen, v, 0), jnp.where(seen, jnp.ones_like(v), 0)], 1)


def weigh(s, m, v):
    return jnp.dot(jnp.exp2(s - m).astype(jnp.bfloat16), v, preferred_element_type=jnp.float32)


def columns(i):
    return pl.ds(i * HEAD_SIZE if isinstance(i, int) else pl.multiple_of(i * HEAD_SIZE, HEAD_SIZE), HEAD_SIZE)


def near_kernel(q_ref, k_ref, v_ref, out_hbm, out_ref, sems):
    def store(i):
        h, quarter = i // N_HEAD, i % N_HEAD
        rows = pl.ds(pl.multiple_of(quarter * QUARTER, QUARTER), QUARTER)
        at = (pl.ds(h * GROUP, GROUP), rows)
        return h, quarter, rows, pltpu.make_async_copy(out_ref.at[at], out_hbm.at[at], sems.at[i])

    def fold(i, carry):
        h, quarter, rows, copy = store(i)
        q = jnp.concatenate([q_ref[rows, columns(h * GROUP + g)] for g in range(GROUP)], 0)
        v = v_ref[:, columns(h)]
        row = lax.broadcasted_iota(jnp.int32, (QUARTER, BLOCK), 0) + quarter * QUARTER
        col = lax.broadcasted_iota(jnp.int32, (QUARTER, BLOCK), 1)
        unseen = jnp.concatenate([jnp.where(col <= row, 0.0, NEG)] * GROUP, 0)
        s = scores_of(q, k_ref[:, columns(h)]) + unseen
        m = jnp.max(s, axis=1, keepdims=True)
        x = weigh(s, m, jnp.concatenate([v, jnp.ones_like(v)], 1))
        lane = lax.broadcasted_iota(jnp.int32, x.shape, 1)
        x = jnp.where(lane < HEAD_SIZE + HEAD_SIZE // 2, x, m)
        for g in range(GROUP):
            out_ref[h * GROUP + g, rows] = x[g * QUARTER : (g + 1) * QUARTER]
        copy.start()
        return carry

    def finish(i, carry):
        store(i)[-1].wait()
        return carry

    lax.fori_loop(0, HEADS * N_HEAD, fold, 0)
    lax.fori_loop(0, HEADS * N_HEAD, finish, 0)


def near(queries, keys, values):
    shape = pltpu.HBM((HEADS * GROUP, BLOCK, 2 * HEAD_SIZE), jnp.float32)
    vmem = pl.BlockSpec(memory_space=pltpu.VMEM)
    return pl.pallas_call(
        near_kernel,
        out_shape=shape,
        in_specs=[vmem] * 3,
        out_specs=pl.BlockSpec(memory_space=pltpu.HBM),
        scratch_shapes=[pltpu.VMEM(shape.shape, shape.dtype), pltpu.SemaphoreType.DMA((HEADS * N_HEAD,))],
        compiler_params=pltpu.CompilerParams(vmem_limit_bytes=16 << 20),
        name="near",
    )(queries, keys, values)


PIECES = ((0, 0, LINE, 0), (1, 3, LINE, 0), (2, 1, LINE, 0), (3, 2, CUT, 0), (4, 2, LINE - CUT, CUT))


EARLY = 3, 1


def rows_of(steps, me):
    return [
        pl.ds(pl.multiple_of((me + step) % N_HEAD * QUARTER + strip * STRIP, STRIP), STRIP) for step, strip in steps
    ]


def queries(q_ref, rows, h, g):
    return [q_ref[x, columns(h * GROUP + g)] for x in rows]


def own_sums(near_ref, rows, i):
    return jnp.concatenate([near_ref[i, x] for x in rows], 0)


def seen_in(piece, host, other):
    _, step, size, start = piece
    chip = host // N_CORE
    before = chip + other * (host % N_CORE) - (chip // N_Z + step) % N_Y * N_Z
    return jnp.clip(before * PASSING - start, 0, size)


def passing(side, pieces, h, host, other):
    k = [side[piece[0]][: piece[2], columns(h)] for piece in pieces]
    v = []
    for piece in pieces:
        seen = lax.broadcasted_iota(jnp.int32, (piece[2], HEAD_SIZE), 0) < seen_in(piece, host, other)
        v.append(with_ones(side[piece[0]][: piece[2], columns(HEADS + h)], seen))
    return k, v


def start_heads(q_ref, rows, state, acc_ref):
    heads = []
    for h in range(HEADS):
        q = jnp.concatenate([x for g in range(GROUP) for x in queries(q_ref, rows, h, g)], 0)
        acc_ref[h] = jnp.concatenate([state(h * GROUP + g) for g in range(GROUP)], 0)
        heads.append((q, acc_ref[h, :, 2 * HEAD_SIZE - 1 :]))
    return heads


def early_kernel(steps, info, q_ref, near_hbm, *refs):
    *sides, out_ref, acc_ref, near_ref, sems = refs
    side0, side1 = sides[: EARLY[0]], sides[EARLY[0] :]
    host, me = info[0], info[1]
    rows = rows_of(steps, me)
    loads = [
        pltpu.make_async_copy(near_hbm.at[:, x], near_ref.at[:, pl.ds(i * STRIP, STRIP)], sems.at[i])
        for i, x in enumerate(rows)
    ]
    for load in loads:
        load.start()
    for load in loads:
        load.wait()
    heads = start_heads(q_ref, rows, near_ref.__getitem__, acc_ref)

    @pl.when(host > 0)
    def _():
        for other, side in enumerate((side0, side1)):
            for h, (q, m) in enumerate(heads):
                k, v = passing(side, PIECES[: EARLY[other]], h, host, other)
                acc_ref[h] += weigh(scores_of(q, jnp.concatenate(k, 0)), m, jnp.concatenate(v, 0))

    for h, (q, m) in enumerate(heads):
        lane = lax.broadcasted_iota(jnp.int32, (ROWS, 2 * HEAD_SIZE), 1)
        x = jnp.where(lane < HEAD_SIZE + HEAD_SIZE // 2, acc_ref[h], m)
        for g in range(GROUP):
            out_ref[h * GROUP + g] = x[g * QUARTER : (g + 1) * QUARTER]


def attend_early(steps, info, queries, near_part, side0, side1):
    vmem, anywhere = [pl.BlockSpec(memory_space=x) for x in (pltpu.VMEM, pl.ANY)]
    sides = [*side0[: EARLY[0]], *side1[: EARLY[1]]]
    return pl.pallas_call(
        functools.partial(early_kernel, steps),
        out_shape=pltpu.VMEM((HEADS * GROUP, QUARTER, 2 * HEAD_SIZE), jnp.float32),
        in_specs=[pl.BlockSpec(memory_space=pltpu.SMEM), vmem, anywhere] + [vmem] * len(sides),
        out_specs=vmem,
        scratch_shapes=[
            pltpu.VMEM((HEADS, ROWS, 2 * HEAD_SIZE), jnp.float32),
            pltpu.VMEM((HEADS * GROUP, QUARTER, 2 * HEAD_SIZE), jnp.float32),
            pltpu.SemaphoreType.DMA((2,)),
        ],
        compiler_params=pltpu.CompilerParams(vmem_limit_bytes=24 << 20),
        name="early",
    )(info, *in_vmem(queries), *in_hbm(near_part), *sides)


def attend_kernel(steps, early, info, q_ref, near_ref, weight_hbm, *refs):
    side0, side1, refs = refs[: len(PIECES)], refs[len(PIECES) : 2 * len(PIECES)], refs[2 * len(PIECES) :]
    *added, out_a, out_b, acc_ref, anchor_ref, attended_ref, weight, sems = refs
    host, me = info[0], info[1]

    def load(i):
        cut = pl.ds(pl.multiple_of(i * CHUNK, CHUNK), CHUNK)
        return cut, pltpu.make_async_copy(weight_hbm.at[:, cut], weight.at[:, cut], sems.at[i])

    for i in range(D // CHUNK):
        load(i)[1].start()
    rows = rows_of(steps, me)
    state = functools.partial(own_sums, near_ref, rows)
    if early:
        state, *added = added
        state = state.__getitem__
    core = host % N_CORE
    for i, j in enumerate((0, 1, 2, 4)):
        start = LINE - CUT if j == 4 else LINE
        x, y = [side[j][start : start + SLICE] for side in (side0, side1)]
        anchor_ref[i * SLICE : (i + 1) * SLICE] = jnp.where(core == 0, x, y)
    def anchor(h):
        v = anchor_ref[:, columns(HEADS + h)]
        return anchor_ref[:, columns(h)], jnp.concatenate([v, jnp.ones_like(v)], 1)

    heads = start_heads(q_ref, rows, state, acc_ref)

    @pl.when(host > 0)
    def _():
        for other, side in enumerate((side0, side1)):
            for h, (q, m) in enumerate(heads):
                k, v = passing(side, PIECES[EARLY[other] if early else 0 :], h, host, other)
                if other == 0:
                    k, v = [x + [y] for x, y in zip((k, v), anchor(h))]
                acc_ref[h] += weigh(scores_of(q, jnp.concatenate(k, 0)), m, jnp.concatenate(v, 0))

    sums = slice(HEAD_SIZE, HEAD_SIZE + HEAD_SIZE // 2)
    worst = jnp.max(jnp.where(acc_ref[:, :, sums] < LIMIT, 0.0, 1.0))

    @pl.when(worst > 0)
    def _():
        def again(i, carry):
            h, g = i // GROUP, i % GROUP
            q = jnp.concatenate(queries(q_ref, rows, h, g), 0)
            acc = own_sums(near_ref, rows, i)
            old = acc[:, 2 * HEAD_SIZE - 1 :]
            k, v = anchor(h)
            chunks = [(k, v, ANCHOR_ROWS)] + [
                (*(x[0] for x in passing(side, [piece], h, host, other)), seen_in(piece, host, other))
                for other, side in enumerate((side0, side1))
                for piece in PIECES
            ]
            for k, v, count in chunks:
                s = scores_of(q, k)
                s = jnp.where(lax.broadcasted_iota(jnp.int32, s.shape, 1) < count, s, NEG)
                m = jnp.maximum(old, jnp.max(s, axis=1, keepdims=True))
                acc = acc * jnp.exp2(old - m) + weigh(s, m, v)
                old = m
            acc_ref[h, pl.ds(pl.multiple_of(g * QUARTER, QUARTER), QUARTER)] = acc
            return carry

        lax.fori_loop(0, HEADS * GROUP, again, 0)

    outs = [acc_ref[h, :, :HEAD_SIZE] / acc_ref[h, :, HEAD_SIZE : HEAD_SIZE + 1] for h in range(HEADS)]
    attended_ref[...] = jnp.concatenate(
        [o[g * QUARTER : (g + 1) * QUARTER].astype(jnp.bfloat16) for o in outs for g in range(GROUP)], 1
    )

    def project(i, carry):
        cut, copy = load(i)
        copy.wait()
        x = jnp.dot(attended_ref[...], weight[:, cut], preferred_element_type=jnp.float32)
        for j, out in enumerate((out_a, out_b)):
            strip = x[j * STRIP : (j + 1) * STRIP]
            for ref in added[j::2]:
                strip = strip + ref[:, cut].astype(jnp.float32)
            out[:, cut] = strip.astype(jnp.bfloat16)
        return carry

    lax.fori_loop(0, D // CHUNK, project, 0)


def attend(steps, info, queries, near_part, weight, sides, added, early):
    width = HEADS * GROUP * HEAD_SIZE
    resident, anywhere = [pl.BlockSpec(memory_space=x) for x in (pltpu.VMEM, pl.ANY)]
    return pl.pallas_call(
        functools.partial(attend_kernel, steps, early),
        out_shape=[jax.ShapeDtypeStruct((STRIP, D), jnp.bfloat16)] * 2,
        in_specs=[pl.BlockSpec(memory_space=pltpu.SMEM), resident, resident, anywhere]
        + [resident] * (len(sides) + len(added)),
        out_specs=[resident] * 2,
        scratch_shapes=[
            pltpu.VMEM((HEADS, ROWS, 2 * HEAD_SIZE), jnp.float32),
            pltpu.VMEM((ANCHOR_ROWS, 2 * WIDTH), jnp.bfloat16),
            pltpu.VMEM((QUARTER, width), jnp.bfloat16),
            pltpu.VMEM((width, D), jnp.bfloat16),
            pltpu.SemaphoreType.DMA((D // CHUNK,)),
        ],
        compiler_params=pltpu.CompilerParams(vmem_limit_bytes=30 << 20),
        name="attend",
    )(info, *in_vmem(queries, near_part), *in_hbm(weight), *sides, *added)


def slices_kernel(k_hbm, v_hbm, *refs):
    *outs, sem = refs
    copies = [
        pltpu.make_async_copy(x.at[pl.ds(i * SLICE, SLICE)], out.at[:, pl.ds(j * WIDTH, WIDTH)], sem.at[i, j])
        for i, out in enumerate(outs)
        for j, x in enumerate((k_hbm, v_hbm))
    ]
    for copy in copies:
        copy.start()
    for copy in copies:
        copy.wait()


def slices_of(keys, values):
    return pl.pallas_call(
        slices_kernel,
        out_shape=[jax.ShapeDtypeStruct((SLICE, 2 * WIDTH), jnp.bfloat16)] * N_Y,
        in_specs=[pl.BlockSpec(memory_space=pl.ANY)] * 2,
        out_specs=[pl.BlockSpec(memory_space=pltpu.VMEM)] * N_Y,
        scratch_shapes=[pltpu.SemaphoreType.DMA((N_Y, 2))],
        name="slices",
    )(*in_hbm(keys, values))


def pick_kernel(rows_ref, k_hbm, v_hbm, out_ref, k_buf, v_buf, sem):
    pairs = ((k_hbm, k_buf), (v_hbm, v_buf))
    copies = [pltpu.make_async_copy(x, buf, sem.at[i]) for i, (x, buf) in enumerate(pairs)]
    for copy in copies:
        copy.start()
    one_hot = lax.broadcasted_iota(jnp.int32, (BLOCK, PASSING), 0) == rows_ref[...]
    one_hot = jnp.where(one_hot, 1.0, 0.0).astype(jnp.bfloat16)
    for i, (copy, (_, buf)) in enumerate(zip(copies, pairs)):
        copy.wait()
        out_ref[:, i * WIDTH : (i + 1) * WIDTH] = lax.dot_general(
            one_hot, buf[...], (((0,), (0,)), ((), ())), preferred_element_type=jnp.float32
        ).astype(jnp.bfloat16)


def pick(rows, keys, values):
    vmem, anywhere = pl.BlockSpec(memory_space=pltpu.VMEM), pl.BlockSpec(memory_space=pl.ANY)
    return pl.pallas_call(
        pick_kernel,
        out_shape=jax.ShapeDtypeStruct((PASSING, 2 * WIDTH), jnp.bfloat16),
        in_specs=[vmem, anywhere, anywhere],
        out_specs=vmem,
        scratch_shapes=[pltpu.VMEM((BLOCK, WIDTH), jnp.bfloat16)] * 2 + [pltpu.SemaphoreType.DMA((2,))],
        name="pick",
    )(rows, *in_hbm(keys, values))


def units_kernel(host, picked_ref, own_ref, *refs):
    *slices, out_ref = refs
    piece = jnp.where(host[0] == 0, own_ref[...], jnp.zeros(own_ref.shape, own_ref.dtype))
    for ref in slices:
        piece = piece + ref[...]
    for z in range(N_Z):
        out_ref[z, :PASSING] = picked_ref[...]
        out_ref[z, PASSING:] = piece


def plane_kernel(line_ref, out_ref):
    for z in range(N_Z):
        out_ref[z * PASSING : (z + 1) * PASSING] = line_ref[z, :PASSING]
    out_ref[LINE:] = line_ref[0, PASSING:]


def local(kernel, shapes, name):
    shapes = [jax.ShapeDtypeStruct(shape, jnp.bfloat16) for shape in shapes]
    return pl.pallas_call(kernel, out_shape=shapes, name=name)


def units_of(host, picked, own, slices):
    vmem = pl.BlockSpec(memory_space=pltpu.VMEM)
    return pl.pallas_call(
        units_kernel,
        out_shape=jax.ShapeDtypeStruct((N_Z, PASSING + SLICE, 2 * WIDTH), jnp.bfloat16),
        in_specs=[pl.BlockSpec(memory_space=pltpu.SMEM)] + [vmem] * (2 + len(slices)),
        out_specs=vmem,
        name="units",
    )(host.reshape(1), *in_vmem(picked, own, *slices))


def place(y, z, core):
    return ((y % N_Y) * N_Z + z % N_Z) * N_CORE + core


def send(x, pairs):
    return lax.ppermute(x, "hst", pairs)


def on_device(queries, keys, values, pass_rows, out_weight):
    host = lax.axis_index("hst")
    me = lax.axis_index("head")
    along_z = [[place(y, z, c) for z in range(N_Z)] for y in range(N_Y) for c in range(N_CORE)]
    a2a = functools.partial(lax.all_to_all, axis_name="hst", split_axis=0, concat_axis=0, tiled=True)
    cores = [(h, h ^ 1) for h in range(N_Y * N_Z * N_CORE)]
    first, *slices = slices_of(keys, values)
    slices = [send(x, [(0, place(y + 1, 0, 0))]) for y, x in enumerate(slices)]
    units = units_of(host, pick(pass_rows, keys, values), first, slices)
    line = a2a(units, axis_index_groups=along_z)
    (plane,) = local(plane_kernel, [(PLANE, 2 * WIDTH)], "plane")(line)

    def along_y(x, step):
        places = [(y, z, c) for y in range(N_Y) for z in range(N_Z) for c in range(N_CORE)]
        return send(x, [(place(y, z, c), place(y + step, z, c)) for y, z, c in places])

    below, above = along_y(plane, 1), along_y(plane, -1)
    held, _ = lax.optimization_barrier((queries, plane))
    below, above, near_part = lax.optimization_barrier((below, above, near(held, keys, values)))
    side0 = [plane, below, above]
    side1 = [send(x, cores) for x in side0]
    halves = [along_y(below[:CUT], 1), along_y(above[CUT:], -1)]
    info = jnp.stack([host, me]).astype(jnp.int32)
    own, right, far, left = range(N_HEAD)
    first = ((far, 0), (far, 1))
    *halves, state = lax.optimization_barrier(
        (*halves, attend_early(first, info, queries, near_part, side0, side1))
    )
    sides = side0 + halves + side1 + [send(x, cores) for x in halves]

    def part(steps, *added, queries=queries, early=False):
        return attend(steps, info, queries, near_part, out_weight, sides, added, early)

    def shift(x, step):
        return lax.ppermute(x, "head", [(i, (i + step) % N_HEAD) for i in range(N_HEAD)])

    a, b = part(first, state, early=True)
    via_right, via_left = shift(a, 1), shift(b, -1)
    a, b = part(((right, 1), (left, 0)))
    held, a, b = lax.optimization_barrier((queries, a, b))
    left1, right0 = shift(a, 1), shift(b, -1)
    a, b = part(((right, 0), (left, 1)), via_right, via_left, queries=held)
    held, a, b = lax.optimization_barrier((queries, a, b))
    left0, right1 = shift(a, 1), shift(b, -1)
    a, b = part(((own, 0), (own, 1)), right0, left1, queries=held)
    own, received = [jnp.concatenate(x, 0).astype(jnp.float32) for x in ((a, b), (left0, right1))]
    return (own + received).astype(jnp.bfloat16)


def solution(mesh):
    placed = (P("hst", "head"), P("hst", "head"), P("hst", "head"), P("hst", None), P("head", None))
    return jax.shard_map(
        on_device, mesh=mesh, in_specs=placed, out_specs=P(("hst", "head"), None), check_vma=False
    )
```

```python
import functools

import jax
import jax.numpy as jnp
import numpy as np
from jax import lax
from jax.experimental import pallas as pl
from jax.experimental.pallas import tpu as pltpu
from jax.sharding import PartitionSpec as P

HEAD_SIZE = 128
GROUP = 4
HEADS = 2
ANCHOR_ROWS = 128
BLOCK = 512
QUARTER = 128
STRIP = 64
ROWS = GROUP * QUARTER
N_Y, N_Z, N_CORE, N_HEAD = 4, 8, 2, 4
PASSING = 64
WIDTH = HEADS * HEAD_SIZE
SLICE = ANCHOR_ROWS // N_Y
LINE = N_Z * PASSING
PLANE = LINE + SLICE
CUT = PLANE // 2
D = 4096
CHUNK = 1024
FACTOR = float(HEAD_SIZE**-0.5 * np.log2(np.e))
NEG = -1e30
LIMIT = float(2.0**110)


def in_hbm(*arrays):
    return [pltpu.with_memory_space_constraint(x, pltpu.HBM) for x in arrays]


def in_vmem(*arrays):
    return [pltpu.with_memory_space_constraint(x, pltpu.VMEM) for x in arrays]


def scores_of(q, k):
    return lax.dot_general(q, k, (((1,), (1,)), ((), ())), preferred_element_type=jnp.float32) * FACTOR


def with_ones(v, seen):
    return jnp.concatenate([jnp.where(seen, v, 0), jnp.where(seen, jnp.ones_like(v), 0)], 1)


def weigh(s, m, v):
    return jnp.dot(jnp.exp2(s - m).astype(jnp.bfloat16), v, preferred_element_type=jnp.float32)


def columns(i):
    return pl.ds(i * HEAD_SIZE if isinstance(i, int) else pl.multiple_of(i * HEAD_SIZE, HEAD_SIZE), HEAD_SIZE)


def near_kernel(q_ref, k_ref, v_ref, out_hbm, out_ref, sems):
    def store(i):
        h, quarter = i // N_HEAD, i % N_HEAD
        rows = pl.ds(pl.multiple_of(quarter * QUARTER, QUARTER), QUARTER)
        at = (pl.ds(h * GROUP, GROUP), rows)
        return h, quarter, rows, pltpu.make_async_copy(out_ref.at[at], out_hbm.at[at], sems.at[i])

    def fold(i, carry):
        h, quarter, rows, copy = store(i)
        q = jnp.concatenate([q_ref[rows, columns(h * GROUP + g)] for g in range(GROUP)], 0)
        v = v_ref[:, columns(h)]
        row = lax.broadcasted_iota(jnp.int32, (QUARTER, BLOCK), 0) + quarter * QUARTER
        col = lax.broadcasted_iota(jnp.int32, (QUARTER, BLOCK), 1)
        unseen = jnp.concatenate([jnp.where(col <= row, 0.0, NEG)] * GROUP, 0)
        s = scores_of(q, k_ref[:, columns(h)]) + unseen
        m = jnp.max(s, axis=1, keepdims=True)
        x = weigh(s, m, jnp.concatenate([v, jnp.ones_like(v)], 1))
        lane = lax.broadcasted_iota(jnp.int32, x.shape, 1)
        x = jnp.where(lane < HEAD_SIZE + HEAD_SIZE // 2, x, m)
        for g in range(GROUP):
            out_ref[h * GROUP + g, rows] = x[g * QUARTER : (g + 1) * QUARTER]
        copy.start()
        return carry

    def finish(i, carry):
        store(i)[-1].wait()
        return carry

    lax.fori_loop(0, HEADS * N_HEAD, fold, 0)
    lax.fori_loop(0, HEADS * N_HEAD, finish, 0)


def near(queries, keys, values):
    shape = pltpu.HBM((HEADS * GROUP, BLOCK, 2 * HEAD_SIZE), jnp.float32)
    vmem = pl.BlockSpec(memory_space=pltpu.VMEM)
    return pl.pallas_call(
        near_kernel,
        out_shape=shape,
        in_specs=[vmem] * 3,
        out_specs=pl.BlockSpec(memory_space=pltpu.HBM),
        scratch_shapes=[pltpu.VMEM(shape.shape, shape.dtype), pltpu.SemaphoreType.DMA((HEADS * N_HEAD,))],
        compiler_params=pltpu.CompilerParams(vmem_limit_bytes=16 << 20),
        name="near",
    )(queries, keys, values)


PIECES = ((0, 0, LINE, 0), (1, 3, LINE, 0), (2, 1, LINE, 0), (3, 2, CUT, 0), (4, 2, LINE - CUT, CUT))


EARLY = 3, 1


def rows_of(steps, me):
    return [
        pl.ds(pl.multiple_of((me + step) % N_HEAD * QUARTER + strip * STRIP, STRIP), STRIP) for step, strip in steps
    ]


def queries(q_ref, rows, h, g):
    return [q_ref[x, columns(h * GROUP + g)] for x in rows]


def own_sums(near_ref, rows, i):
    return jnp.concatenate([near_ref[i, x] for x in rows], 0)


def seen_in(piece, host, other):
    _, step, size, start = piece
    chip = host // N_CORE
    before = chip + other * (host % N_CORE) - (chip // N_Z + step) % N_Y * N_Z
    return jnp.clip(before * PASSING - start, 0, size)


def passing(side, pieces, h, host, other):
    k = [side[piece[0]][: piece[2], columns(h)] for piece in pieces]
    v = []
    for piece in pieces:
        seen = lax.broadcasted_iota(jnp.int32, (piece[2], HEAD_SIZE), 0) < seen_in(piece, host, other)
        v.append(with_ones(side[piece[0]][: piece[2], columns(HEADS + h)], seen))
    return k, v


def start_heads(q_ref, rows, state, acc_ref):
    heads = []
    for h in range(HEADS):
        q = jnp.concatenate([x for g in range(GROUP) for x in queries(q_ref, rows, h, g)], 0)
        acc_ref[h] = jnp.concatenate([state(h * GROUP + g) for g in range(GROUP)], 0)
        heads.append((q, acc_ref[h, :, 2 * HEAD_SIZE - 1 :]))
    return heads


def early_kernel(steps, info, q_ref, near_hbm, *refs):
    *sides, out_ref, acc_ref, near_ref, sems = refs
    side0, side1 = sides[: EARLY[0]], sides[EARLY[0] :]
    host, me = info[0], info[1]
    rows = rows_of(steps, me)
    loads = [
        pltpu.make_async_copy(near_hbm.at[:, x], near_ref.at[:, pl.ds(i * STRIP, STRIP)], sems.at[i])
        for i, x in enumerate(rows)
    ]
    for load in loads:
        load.start()
    for load in loads:
        load.wait()
    heads = start_heads(q_ref, rows, near_ref.__getitem__, acc_ref)

    @pl.when(host > 0)
    def _():
        for other, side in enumerate((side0, side1)):
            for h, (q, m) in enumerate(heads):
                k, v = passing(side, PIECES[: EARLY[other]], h, host, other)
                acc_ref[h] += weigh(scores_of(q, jnp.concatenate(k, 0)), m, jnp.concatenate(v, 0))

    for h, (q, m) in enumerate(heads):
        lane = lax.broadcasted_iota(jnp.int32, (ROWS, 2 * HEAD_SIZE), 1)
        x = jnp.where(lane < HEAD_SIZE + HEAD_SIZE // 2, acc_ref[h], m)
        for g in range(GROUP):
            out_ref[h * GROUP + g] = x[g * QUARTER : (g + 1) * QUARTER]


def attend_early(steps, info, queries, near_part, side0, side1):
    vmem, anywhere = [pl.BlockSpec(memory_space=x) for x in (pltpu.VMEM, pl.ANY)]
    sides = [*side0[: EARLY[0]], *side1[: EARLY[1]]]
    return pl.pallas_call(
        functools.partial(early_kernel, steps),
        out_shape=pltpu.VMEM((HEADS * GROUP, QUARTER, 2 * HEAD_SIZE), jnp.float32),
        in_specs=[pl.BlockSpec(memory_space=pltpu.SMEM), vmem, anywhere] + [vmem] * len(sides),
        out_specs=vmem,
        scratch_shapes=[
            pltpu.VMEM((HEADS, ROWS, 2 * HEAD_SIZE), jnp.float32),
            pltpu.VMEM((HEADS * GROUP, QUARTER, 2 * HEAD_SIZE), jnp.float32),
            pltpu.SemaphoreType.DMA((2,)),
        ],
        compiler_params=pltpu.CompilerParams(vmem_limit_bytes=24 << 20),
        name="early",
    )(info, *in_vmem(queries), *in_hbm(near_part), *sides)


def attend_kernel(steps, early, info, q_ref, near_ref, weight_hbm, *refs):
    side0, side1, refs = refs[: len(PIECES)], refs[len(PIECES) : 2 * len(PIECES)], refs[2 * len(PIECES) :]
    *added, out_a, out_b, acc_ref, anchor_ref, attended_ref, weight, sems = refs
    host, me = info[0], info[1]

    def load(i):
        cut = pl.ds(pl.multiple_of(i * CHUNK, CHUNK), CHUNK)
        return cut, pltpu.make_async_copy(weight_hbm.at[:, cut], weight.at[:, cut], sems.at[i])

    for i in range(D // CHUNK):
        load(i)[1].start()
    rows = rows_of(steps, me)
    state = functools.partial(own_sums, near_ref, rows)
    if early:
        state, *added = added
        state = state.__getitem__
    core = host % N_CORE
    for i, j in enumerate((0, 1, 2, 4)):
        start = LINE - CUT if j == 4 else LINE
        x, y = [side[j][start : start + SLICE] for side in (side0, side1)]
        anchor_ref[i * SLICE : (i + 1) * SLICE] = jnp.where(core == 0, x, y)
    def anchor(h):
        v = anchor_ref[:, columns(HEADS + h)]
        return anchor_ref[:, columns(h)], jnp.concatenate([v, jnp.ones_like(v)], 1)

    heads = start_heads(q_ref, rows, state, acc_ref)

    @pl.when(host > 0)
    def _():
        for other, side in enumerate((side0, side1)):
            for h, (q, m) in enumerate(heads):
                k, v = passing(side, PIECES[EARLY[other] if early else 0 :], h, host, other)
                if other == 0:
                    k, v = [x + [y] for x, y in zip((k, v), anchor(h))]
                acc_ref[h] += weigh(scores_of(q, jnp.concatenate(k, 0)), m, jnp.concatenate(v, 0))

    sums = slice(HEAD_SIZE, HEAD_SIZE + HEAD_SIZE // 2)
    worst = jnp.max(jnp.where(acc_ref[:, :, sums] < LIMIT, 0.0, 1.0))

    @pl.when(worst > 0)
    def _():
        def again(i, carry):
            h, g = i // GROUP, i % GROUP
            q = jnp.concatenate(queries(q_ref, rows, h, g), 0)
            acc = own_sums(near_ref, rows, i)
            old = acc[:, 2 * HEAD_SIZE - 1 :]
            k, v = anchor(h)
            chunks = [(k, v, ANCHOR_ROWS)] + [
                (*(x[0] for x in passing(side, [piece], h, host, other)), seen_in(piece, host, other))
                for other, side in enumerate((side0, side1))
                for piece in PIECES
            ]
            for k, v, count in chunks:
                s = scores_of(q, k)
                s = jnp.where(lax.broadcasted_iota(jnp.int32, s.shape, 1) < count, s, NEG)
                m = jnp.maximum(old, jnp.max(s, axis=1, keepdims=True))
                acc = acc * jnp.exp2(old - m) + weigh(s, m, v)
                old = m
            acc_ref[h, pl.ds(pl.multiple_of(g * QUARTER, QUARTER), QUARTER)] = acc
            return carry

        lax.fori_loop(0, HEADS * GROUP, again, 0)

    outs = [acc_ref[h, :, :HEAD_SIZE] / acc_ref[h, :, HEAD_SIZE : HEAD_SIZE + 1] for h in range(HEADS)]
    attended_ref[...] = jnp.concatenate(
        [o[g * QUARTER : (g + 1) * QUARTER].astype(jnp.bfloat16) for o in outs for g in range(GROUP)], 1
    )

    def project(i, carry):
        cut, copy = load(i)
        copy.wait()
        x = jnp.dot(attended_ref[...], weight[:, cut], preferred_element_type=jnp.float32)
        for j, out in enumerate((out_a, out_b)):
            strip = x[j * STRIP : (j + 1) * STRIP]
            for ref in added[j::2]:
                strip = strip + ref[:, cut].astype(jnp.float32)
            out[:, cut] = strip.astype(jnp.bfloat16)
        return carry

    lax.fori_loop(0, D // CHUNK, project, 0)


def attend(steps, info, queries, near_part, weight, sides, added, early):
    width = HEADS * GROUP * HEAD_SIZE
    resident, anywhere = [pl.BlockSpec(memory_space=x) for x in (pltpu.VMEM, pl.ANY)]
    return pl.pallas_call(
        functools.partial(attend_kernel, steps, early),
        out_shape=[jax.ShapeDtypeStruct((STRIP, D), jnp.bfloat16)] * 2,
        in_specs=[pl.BlockSpec(memory_space=pltpu.SMEM), resident, resident, anywhere]
        + [resident] * (len(sides) + len(added)),
        out_specs=[resident] * 2,
        scratch_shapes=[
            pltpu.VMEM((HEADS, ROWS, 2 * HEAD_SIZE), jnp.float32),
            pltpu.VMEM((ANCHOR_ROWS, 2 * WIDTH), jnp.bfloat16),
            pltpu.VMEM((QUARTER, width), jnp.bfloat16),
            pltpu.VMEM((width, D), jnp.bfloat16),
            pltpu.SemaphoreType.DMA((D // CHUNK,)),
        ],
        compiler_params=pltpu.CompilerParams(vmem_limit_bytes=30 << 20),
        name="attend",
    )(info, *in_vmem(queries, near_part), *in_hbm(weight), *sides, *added)


def slices_kernel(k_hbm, v_hbm, *refs):
    *outs, sem = refs
    copies = [
        pltpu.make_async_copy(x.at[pl.ds(i * SLICE, SLICE)], out.at[:, pl.ds(j * WIDTH, WIDTH)], sem.at[i, j])
        for i, out in enumerate(outs)
        for j, x in enumerate((k_hbm, v_hbm))
    ]
    for copy in copies:
        copy.start()
    for copy in copies:
        copy.wait()


def slices_of(keys, values):
    return pl.pallas_call(
        slices_kernel,
        out_shape=[jax.ShapeDtypeStruct((SLICE, 2 * WIDTH), jnp.bfloat16)] * N_Y,
        in_specs=[pl.BlockSpec(memory_space=pl.ANY)] * 2,
        out_specs=[pl.BlockSpec(memory_space=pltpu.VMEM)] * N_Y,
        scratch_shapes=[pltpu.SemaphoreType.DMA((N_Y, 2))],
        name="slices",
    )(*in_hbm(keys, values))


def pick_kernel(rows_ref, k_hbm, v_hbm, out_ref, k_buf, v_buf, sem):
    pairs = ((k_hbm, k_buf), (v_hbm, v_buf))
    copies = [pltpu.make_async_copy(x, buf, sem.at[i]) for i, (x, buf) in enumerate(pairs)]
    for copy in copies:
        copy.start()
    one_hot = lax.broadcasted_iota(jnp.int32, (BLOCK, PASSING), 0) == rows_ref[...]
    one_hot = jnp.where(one_hot, 1.0, 0.0).astype(jnp.bfloat16)
    for i, (copy, (_, buf)) in enumerate(zip(copies, pairs)):
        copy.wait()
        out_ref[:, i * WIDTH : (i + 1) * WIDTH] = lax.dot_general(
            one_hot, buf[...], (((0,), (0,)), ((), ())), preferred_element_type=jnp.float32
        ).astype(jnp.bfloat16)


def pick(rows, keys, values):
    vmem, anywhere = pl.BlockSpec(memory_space=pltpu.VMEM), pl.BlockSpec(memory_space=pl.ANY)
    return pl.pallas_call(
        pick_kernel,
        out_shape=jax.ShapeDtypeStruct((PASSING, 2 * WIDTH), jnp.bfloat16),
        in_specs=[vmem, anywhere, anywhere],
        out_specs=vmem,
        scratch_shapes=[pltpu.VMEM((BLOCK, WIDTH), jnp.bfloat16)] * 2 + [pltpu.SemaphoreType.DMA((2,))],
        name="pick",
    )(rows, *in_hbm(keys, values))


def units_kernel(host, picked_ref, own_ref, *refs):
    *slices, out_ref = refs
    piece = jnp.where(host[0] == 0, own_ref[...], jnp.zeros(own_ref.shape, own_ref.dtype))
    for ref in slices:
        piece = piece + ref[...]
    for z in range(N_Z):
        out_ref[z, :PASSING] = picked_ref[...]
        out_ref[z, PASSING:] = piece


def plane_kernel(line_ref, out_ref):
    for z in range(N_Z):
        out_ref[z * PASSING : (z + 1) * PASSING] = line_ref[z, :PASSING]
    out_ref[LINE:] = line_ref[0, PASSING:]


def local(kernel, shapes, name):
    shapes = [jax.ShapeDtypeStruct(shape, jnp.bfloat16) for shape in shapes]
    return pl.pallas_call(kernel, out_shape=shapes, name=name)


def units_of(host, picked, own, slices):
    vmem = pl.BlockSpec(memory_space=pltpu.VMEM)
    return pl.pallas_call(
        units_kernel,
        out_shape=jax.ShapeDtypeStruct((N_Z, PASSING + SLICE, 2 * WIDTH), jnp.bfloat16),
        in_specs=[pl.BlockSpec(memory_space=pltpu.SMEM)] + [vmem] * (2 + len(slices)),
        out_specs=vmem,
        name="units",
    )(host.reshape(1), *in_vmem(picked, own, *slices))


def place(y, z, core):
    return ((y % N_Y) * N_Z + z % N_Z) * N_CORE + core


def send(x, pairs):
    return lax.ppermute(x, "hst", pairs)


def on_device(queries, keys, values, pass_rows, out_weight):
    host = lax.axis_index("hst")
    me = lax.axis_index("head")
    along_z = [[place(y, z, c) for z in range(N_Z)] for y in range(N_Y) for c in range(N_CORE)]
    a2a = functools.partial(lax.all_to_all, axis_name="hst", split_axis=0, concat_axis=0, tiled=True)
    cores = [(h, h ^ 1) for h in range(N_Y * N_Z * N_CORE)]
    first, *slices = slices_of(keys, values)
    slices = [send(x, [(0, place(y + 1, 0, 0))]) for y, x in enumerate(slices)]
    units = units_of(host, pick(pass_rows, keys, values), first, slices)
    line = a2a(units, axis_index_groups=along_z)
    (plane,) = local(plane_kernel, [(PLANE, 2 * WIDTH)], "plane")(*in_vmem(line))

    def along_y(x, step):
        places = [(y, z, c) for y in range(N_Y) for z in range(N_Z) for c in range(N_CORE)]
        return send(x, [(place(y, z, c), place(y + step, z, c)) for y, z, c in places])

    below, above = along_y(plane, 1), along_y(plane, -1)
    held, _ = lax.optimization_barrier((queries, plane))
    below, above, near_part = lax.optimization_barrier((below, above, near(held, keys, values)))
    side0 = [plane, below, above]
    side1 = [send(x, cores) for x in side0]
    halves = [along_y(below[:CUT], 1), along_y(above[CUT:], -1)]
    info = jnp.stack([host, me]).astype(jnp.int32)
    own, right, far, left = range(N_HEAD)
    first = ((far, 0), (far, 1))
    *halves, state = lax.optimization_barrier(
        (*halves, attend_early(first, info, queries, near_part, side0, side1))
    )
    sides = side0 + halves + side1 + [send(x, cores) for x in halves]

    def part(steps, *added, queries=queries, early=False):
        return attend(steps, info, queries, near_part, out_weight, sides, added, early)

    def shift(x, step):
        return lax.ppermute(x, "head", [(i, (i + step) % N_HEAD) for i in range(N_HEAD)])

    a, b = part(first, state, early=True)
    via_right, via_left = shift(a, 1), shift(b, -1)
    a, b = part(((right, 1), (left, 0)))
    held, a, b = lax.optimization_barrier((queries, a, b))
    left1, right0 = shift(a, 1), shift(b, -1)
    a, b = part(((right, 0), (left, 1)), via_right, via_left, queries=held)
    held, a, b = lax.optimization_barrier((queries, a, b))
    left0, right1 = shift(a, 1), shift(b, -1)
    a, b = part(((own, 0), (own, 1)), right0, left1, queries=held)
    own, received = [jnp.concatenate(x, 0).astype(jnp.float32) for x in ((a, b), (left0, right1))]
    return (own + received).astype(jnp.bfloat16)


def solution(mesh):
    placed = (P("hst", "head"), P("hst", "head"), P("hst", "head"), P("hst", None), P("head", None))
    return jax.shard_map(
        on_device, mesh=mesh, in_specs=placed, out_specs=P(("hst", "head"), None), check_vma=False
    )
```
